32 devices in a mesh: grp: 2 (over y), img: 4 (over z), sub: 2 (over x), cls: 2 (over core).
Axes of the slice: x: 2, y: 2, z: 4, core: 2. Of those that a mesh axis runs over, the one named last changes fastest.
Arguments:
- images: bfloat16 [4096, 3072], P(('grp', 'img', 'sub', 'cls')), parts along dimension 0, may hold values from -10 to 10
- labels: int32 [4096], P(('grp', 'img', 'sub', 'cls')), parts along dimension 0, may hold values from 0 to 999
- seeds: int32 [128], replicated, may hold values from 0 to 46336
Outputs:
- rfactor: float32 [1024, 512], P('grp'), parts along dimension 0
- projections: float32 [1024, 1000], P('grp', 'cls'), parts along dimension 0
The draws below stay inside these ranges and needn't reach their ends.
There are 2 independent parts, one for each index of `grp`. The reference program is written for one: setup_inputs(seed, part) draws one part's arguments, and reference() takes and returns one part's arrays. A program takes and returns all parts, laid end to end along the dimension named above; an argument that names none is the same for every part. Nothing has to cross between parts.
All inputs are finite; a program needn't handle non-finite values.
Results may differ from the reference program's by a relative error of at most 0.0058.
Values sent between devices are 32-bit elements; how exact they have to be, the bound alone decides.
No kernel may reach another device: no remote copies, remote signals or barrier semaphores. Data moves between devices by JAX's collectives and lax.ppermute only.
A program may use at most 128 MiB of HBM per device.

```python
import math
import jax
import jax.numpy as jnp
from jax import lax

FILTERS = 128
FEAT = 512
CLASSES = 1000
PIXELS = 3072
IMAGES = 2048


def draw_images(key, part):
    key_noise, key_scale, key_pattern, key_phase = jax.random.split(key, 4)
    rows = jnp.arange(IMAGES, dtype=jnp.float32)[:, None] / IMAGES
    phase = jax.random.uniform(key_phase, (), jnp.float32, 0.0, 6.283185)
    noise = jnp.clip(jax.random.normal(key_noise, (IMAGES, PIXELS), jnp.float32), -4.0, 4.0)
    scale = jnp.exp(jax.random.uniform(key_scale, (IMAGES, 1), jnp.float32, math.log(0.5), math.log(2.0)))
    pattern = jax.random.uniform(key_pattern, (1, PIXELS), jnp.float32, -1.0, 1.0)
    amplitude = 1.2 * jnp.sin(6.283185 * 3.0 * rows + phase)
    return (noise * scale + amplitude * pattern).astype(jnp.bfloat16)


def touch_ends(drawn, stream_key, least, top_value):
    index_at = [jax.random.randint(jax.random.fold_in(stream_key, axis), (), 0, length) for axis, length in enumerate(drawn.shape)]
    widest = drawn.shape.index(max(drawn.shape))
    neighbour = index_at[:widest] + [(index_at[widest] + 1) % drawn.shape[widest]] + index_at[widest + 1:]
    return drawn.at[tuple(index_at)].set(least).at[tuple(neighbour)].set(top_value)


def setup_inputs(seed: int = 0, part: int = 0) -> dict:
    keys = jax.random.split(jax.random.key(seed), 4)
    part_splits = jax.random.split(jax.random.fold_in(keys[3], part), 4)
    return {
        "images": draw_images(jax.random.fold_in(jax.random.fold_in(keys[3], part), 71), part),
        "labels": touch_ends(jax.random.randint(part_splits[1], (IMAGES,), 0, CLASSES), jax.random.fold_in(part_splits[1], 1), 0, CLASSES - 1).astype(jnp.int32),
        "seeds": touch_ends(jax.random.randint(keys[2], (FILTERS,), 0, 46337), jax.random.fold_in(keys[2], 1), 0, 46336).astype(jnp.int32),
    }


def make_filters(seeds):
    count = seeds.shape[0]
    index = lax.broadcasted_iota(jnp.int32, (count, 108), 1)
    first = (seeds[:, None] * 7919 + index * 104729) % 46337
    second = (first * first + seeds[:, None]) % 46337
    values = (second.astype(jnp.float32) / 46337.0 - 0.5) * math.sqrt(12.0 / 108.0)
    return values.reshape(count, 3, 6, 6).astype(jnp.bfloat16)

def features_of(block, filters):
    pictures = block.reshape(block.shape[0], 3, 32, 32)
    response = lax.conv_general_dilated(pictures, filters, (2, 2), 'VALID', dimension_numbers=('NCHW', 'OIHW', 'NCHW'), preferred_element_type=jnp.float32)
    active = jnp.maximum(response, 0.0)
    active = active.reshape(block.shape[0], filters.shape[0], 2, 7, 2, 7)
    pooled = lax.optimization_barrier(jnp.mean(active, axis=(3, 5)))
    return pooled.reshape(block.shape[0], filters.shape[0] * 4)

def reference(images, labels, seeds):
    filters = make_filters(seeds)
    count = images.shape[0]
    width = min(1024, count)
    blocks = count // width
    image_blocks = images.reshape(blocks, width, images.shape[1])
    label_blocks = labels.reshape(blocks, width)
    classes_row = jnp.arange(CLASSES, dtype=jnp.int32)

    def accumulate(carry, pair):
        gram, sums = carry
        block, marks = pair
        feats = features_of(block, filters)
        onehot = (marks[:, None] == classes_row[None, :]).astype(jnp.float32)
        gram = gram + lax.dot_general(feats.astype(jnp.float32), feats.astype(jnp.float32), (((0,), (0,)), ((), ())), precision=lax.Precision.HIGHEST, preferred_element_type=jnp.float32)
        sums = sums + lax.dot_general(feats.astype(jnp.float32), onehot.astype(jnp.float32), (((0,), (0,)), ((), ())), precision=lax.Precision.HIGHEST, preferred_element_type=jnp.float32)
        return ((gram, sums), None)
    start = (jnp.zeros((FEAT, FEAT), jnp.float32), jnp.zeros((FEAT, CLASSES), jnp.float32))
    (gram, sums), _ = lax.scan(accumulate, start, (image_blocks, label_blocks))
    gram = gram + 0.001 * count * jnp.eye(FEAT, dtype=jnp.float32)
    lower = jnp.linalg.cholesky(gram)
    projections = lax.linalg.triangular_solve(lower, sums, left_side=True, lower=True)
    return (lower.T, projections)
```

```python
import math

import jax
import jax.numpy as jnp
from jax import lax
from jax.experimental import pallas as pl
from jax.experimental.pallas import tpu as pltpu
from jax.sharding import PartitionSpec as P

CLASSES = 1000
RIDGE = 0.001
BLOCK = 128
HIGHEST = lax.Precision.HIGHEST
ROWS = (((0,), (0,)), ((), ()))
LANES = (((1,), (1,)), ((), ()))
VMEM_BYTES = 48 * 2**20
MOST_BLOCKS = 16


def make_filters(seeds):
    count = seeds.shape[0]
    index = lax.broadcasted_iota(jnp.int32, (count, 108), 1)
    first = (seeds[:, None] * 7919 + index * 104729) % 46337
    second = (first * first + seeds[:, None]) % 46337
    values = (second.astype(jnp.float32) / 46337.0 - 0.5) * math.sqrt(12.0 / 108.0)
    return values.reshape(count, 3, 6, 6).astype(jnp.bfloat16)


def features_of(block, filters):
    pictures = block.reshape(block.shape[0], 3, 32, 32)
    response = lax.conv_general_dilated(
        pictures,
        filters,
        (2, 2),
        "VALID",
        dimension_numbers=("NCHW", "OIHW", "NCHW"),
        preferred_element_type=jnp.float32,
    )
    active = jnp.maximum(response, 0.0)
    active = active.reshape(block.shape[0], filters.shape[0], 2, 7, 2, 7)
    pooled = jnp.mean(active, axis=(3, 5))
    return pooled.reshape(block.shape[0], filters.shape[0] * 4)


def lane_copies(tile, lane):
    return jnp.broadcast_to(tile[:, lane : lane + 1], (8, BLOCK))


def row_copies(tile, row):
    return jnp.broadcast_to(tile[row : row + 1, :], (8, BLOCK))


def factor_block(tiles):
    lane = lax.broadcasted_iota(jnp.int32, (8, BLOCK), 1)
    row = lax.broadcasted_iota(jnp.int32, (8, BLOCK), 0)
    count = len(tiles)
    left = list(tiles)
    right = [jnp.where(lane == row + 8 * g, 1.0, 0.0) for g in range(count)]
    upper, inverse = [], []
    for p in range(count):
        a = [row_copies(left[p], i) for i in range(8)]
        b = [row_copies(right[p], i) for i in range(8)]
        s = {(i, j): lane_copies(a[i], 8 * p + j) for i in range(8) for j in range(i, 8)}
        cols = {g: [lane_copies(left[g], 8 * p + j) for j in range(8)] for g in range(p + 1, count)}
        for j in range(8):
            r = lax.rsqrt(s[j, j])
            r = r * (1.5 - 0.5 * s[j, j] * r * r)
            u = {c: s[j, c] * r for c in range(j + 1, 8)}
            a[j] = a[j] * r
            b[j] = b[j] * r
            for g in cols:
                cols[g][j] = cols[g][j] * r
            for i in range(j + 1, 8):
                for c in range(i, 8):
                    s[i, c] = s[i, c] - u[i] * u[c]
                a[i] = a[i] - u[i] * a[j]
                b[i] = b[i] - u[i] * b[j]
                for g in cols:
                    cols[g][i] = cols[g][i] - u[i] * cols[g][j]
        for g in cols:
            for j in range(8):
                left[g] = left[g] - cols[g][j] * a[j]
                right[g] = right[g] - cols[g][j] * b[j]
        top, bottom = a[0], b[0]
        for j in range(1, 8):
            top = jnp.where(row == j, a[j], top)
            bottom = jnp.where(row == j, b[j], bottom)
        upper.append(jnp.where(lane >= row + 8 * p, top, 0.0))
        inverse.append(bottom)
    return upper, inverse


def form_sums(start_ref, block_refs, gram, sums, high, low, marks):
    feat, width = gram.shape[0], block_refs[0].shape[1]
    classes = marks.shape[0]
    class_row = lax.broadcasted_iota(jnp.int32, (classes, width), 0) + start_ref[0]
    for n, ref in enumerate(block_refs):
        at = slice(n * width, (n + 1) * width)
        whole = ref[:feat, :]
        top = whole.astype(jnp.bfloat16)
        high[:, at] = top
        low[:, at] = (whole - top.astype(jnp.float32)).astype(jnp.bfloat16)
        label = ref[feat : feat + 1, :].astype(jnp.int32)
        marks[:, at] = jnp.where(class_row == label, 1.0, 0.0).astype(jnp.bfloat16)

    def product(one, two):
        return lax.dot_general(one, two, LANES, preferred_element_type=jnp.float32)

    for i in range(0, feat, BLOCK):
        at = slice(i, i + BLOCK)
        cross = product(high[at, :], low[i:, :]) + product(low[at, :], high[i:, :])
        gram[at, i:] = product(high[at, :], high[i:, :]) + (cross + product(low[at, :], low[i:, :]))
    sums[...] = product(high[...], marks[...]) + product(low[...], marks[...])


def factor_and_solve(ridge, gram, sums, inverse, factor_ref, rotated_ref):
    feat = gram.shape[0]
    blocks = feat // BLOCK
    factor_ref[...] = jnp.zeros_like(factor_ref)
    lane = lax.broadcasted_iota(jnp.int32, (8, BLOCK), 1)
    row = lax.broadcasted_iota(jnp.int32, (8, BLOCK), 0)

    def step(k, carry):
        start = pl.multiple_of(k * BLOCK, BLOCK)
        tiles = []
        for g in range(BLOCK // 8):
            tile = gram[pl.ds(pl.multiple_of(start + 8 * g, 8), 8), pl.ds(start, BLOCK)]
            tiles.append(tile + jnp.where(lane == row + 8 * g, ridge, 0.0))
        upper, inverted = factor_block(tiles)
        for g in range(BLOCK // 8):
            factor_ref[pl.ds(pl.multiple_of(start + 8 * g, 8), 8), pl.ds(start, BLOCK)] = upper[g]
            inverse[8 * g : 8 * g + 8, :] = inverted[g]
        for kk in range(blocks):

            @pl.when(k == kk)
            def _():
                at, rest = slice(BLOCK * kk, BLOCK * kk + BLOCK), BLOCK * kk + BLOCK
                turned = jnp.dot(inverse[...], sums[at, :], precision=HIGHEST, preferred_element_type=jnp.float32)
                rotated_ref[at, :] = turned[:, : rotated_ref.shape[1]]
                if rest < feat:
                    across = jnp.dot(inverse[...], gram[at, rest:], precision=HIGHEST, preferred_element_type=jnp.float32)
                    factor_ref[at, rest:] = across
                    for i in range(rest, feat, BLOCK):
                        part = across[:, i - rest : i - rest + BLOCK]
                        gram[i : i + BLOCK, i:] -= lax.dot_general(
                            part, across[:, i - rest :], ROWS, precision=HIGHEST, preferred_element_type=jnp.float32
                        )
                    sums[rest:, :] -= lax.dot_general(
                        across, turned, ROWS, precision=HIGHEST, preferred_element_type=jnp.float32
                    )

        return carry

    lax.fori_loop(0, blocks, step, 0)


def panel_kernel(ridge, count, start_ref, *refs):
    blocks, (factor_ref, rotated_ref, gram, sums, inverse, high, low, marks) = refs[:count], refs[count:]
    form_sums(start_ref, blocks, gram, sums, high, low, marks)
    factor_and_solve(ridge, gram, sums, inverse, factor_ref, rotated_ref)


def sums_kernel(count, start_ref, *refs):
    blocks, (gram, sums, high, low, marks) = refs[:count], refs[count:]
    gram[...] = jnp.zeros_like(gram)
    form_sums(start_ref, blocks, gram, sums, high, low, marks)


def solve_kernel(ridge, gram_ref, sums_ref, factor_ref, rotated_ref, gram, sums, inverse):
    gram[...] = gram_ref[...]
    sums[...] = sums_ref[...]
    factor_and_solve(ridge, gram, sums, inverse, factor_ref, rotated_ref)


def call(kernel, operands, outs, scratch, scalars):
    vmem = pl.BlockSpec(memory_space=pltpu.VMEM)
    smem = pl.BlockSpec(memory_space=pltpu.SMEM)
    return pl.pallas_call(
        kernel,
        out_shape=[jax.ShapeDtypeStruct(shape, jnp.float32) for shape in outs],
        in_specs=[smem] * scalars + [vmem] * (len(operands) - scalars),
        out_specs=[vmem] * len(outs),
        scratch_shapes=[pltpu.VMEM(shape, dtype) for shape, dtype in scratch],
        compiler_params=pltpu.CompilerParams(vmem_limit_bytes=VMEM_BYTES),
    )(*operands)


def ring(blocks, axis):
    size = lax.axis_size(axis)
    turn = [(i, (i + 1) % size) for i in range(size)]
    out = []
    for block in blocks:
        out.append(block)
        for _ in range(size - 1):
            block = lax.ppermute(block, axis, turn)
            out.append(block)
    return out


def shards(images, labels, seeds):
    filters = make_filters(seeds)
    count = images.shape[0]
    feats = features_of(images, filters)
    feat = feats.shape[1]
    shards_here = math.prod(lax.axis_size(axis) for axis in ("img", "sub", "cls"))
    ridge = RIDGE * count * shards_here
    classes = CLASSES // lax.axis_size("cls")
    padded = -(-classes // BLOCK) * BLOCK
    start = jnp.full((1,), classes, jnp.int32) * lax.axis_index("cls")
    extra = jnp.broadcast_to(labels.astype(jnp.float32)[None, :], (8, count))
    block = jnp.concatenate([feats.T, extra], axis=0)
    f32, bf16 = jnp.float32, jnp.bfloat16
    outs = [(feat, feat), (feat, classes)]
    solve_scratch = [((feat, feat), f32), ((feat, padded), f32), ((BLOCK, BLOCK), f32)]

    def panel_scratch(blocks):
        width = len(blocks) * count
        return [((feat, width), bf16), ((feat, width), bf16), ((padded, width), bf16)]

    if shards_here <= MOST_BLOCKS:
        blocks = ring(ring(ring([block], "img"), "sub"), "cls")
        kernel = lambda *refs: panel_kernel(ridge, len(blocks), *refs)
        return tuple(call(kernel, [start] + blocks, outs, solve_scratch + panel_scratch(blocks), 1))
    blocks = ring([block], "cls")
    kernel = lambda *refs: sums_kernel(len(blocks), *refs)
    parts = call(kernel, [start] + blocks, [(feat, feat), (feat, padded)], panel_scratch(blocks), 1)
    parts = lax.psum(tuple(parts), ("img", "sub"))
    kernel = lambda *refs: solve_kernel(ridge, *refs)
    return tuple(call(kernel, list(parts), outs, solve_scratch, 0))


def solution(mesh):
    placed = (P(("grp", "img", "sub", "cls"), None), P(("grp", "img", "sub", "cls")), P())
    return jax.shard_map(
        shards,
        mesh=mesh,
        in_specs=placed,
        out_specs=(P("grp", None), P("grp", "cls")),
        check_vma=False,
    )
```

```python
import math

import jax
import jax.numpy as jnp
from jax import lax
from jax.experimental import pallas as pl
from jax.experimental.pallas import tpu as pltpu
from jax.sharding import PartitionSpec as P

CLASSES = 1000
CHANNELS, SIDE, KERNEL, OUT, POOL = 3, 32, 6, 14, 7
MODULUS = 46337
RIDGE = 0.001
BLOCK = 128
HIGHEST = lax.Precision.HIGHEST
ROWS = (((0,), (0,)), ((), ()))
LANES = (((1,), (1,)), ((), ()))
VMEM_BYTES = 48 * 2**20
MOST_BLOCKS = 16
F32, BF16 = jnp.float32, jnp.bfloat16


def call(kernel, operands, outs, scratch=(), scalars=0, flops=0, aliases=None):
    vmem = pl.BlockSpec(memory_space=pltpu.VMEM)
    smem = pl.BlockSpec(memory_space=pltpu.SMEM)
    moved = 4 * sum(math.prod(shape) for shape in outs) + sum(o.size * o.dtype.itemsize for o in operands)
    return pl.pallas_call(
        kernel,
        out_shape=[jax.ShapeDtypeStruct(shape, F32) for shape in outs],
        in_specs=[smem] * scalars + [vmem] * (len(operands) - scalars),
        out_specs=[vmem] * len(outs),
        scratch_shapes=[pltpu.VMEM(shape, dtype) for shape, dtype in scratch],
        input_output_aliases=aliases or {},
        cost_estimate=pl.CostEstimate(flops=flops, bytes_accessed=moved, transcendentals=0),
        compiler_params=pltpu.CompilerParams(vmem_limit_bytes=VMEM_BYTES),
    )(*operands)


def residue(x):
    quotient = jnp.floor(x.astype(F32) * (1.0 / MODULUS)).astype(jnp.int32)
    rest = x - quotient * MODULUS
    rest = jnp.where(rest < 0, rest + MODULUS, rest)
    return jnp.where(rest >= MODULUS, rest - MODULUS, rest)


def filter_values(seeds, taps):
    index = lax.broadcasted_iota(jnp.int32, (BLOCK, seeds.shape[1]), 0)
    seed = jnp.broadcast_to(seeds, index.shape)
    first = residue(seed * 7919 + index * 104729)
    second = residue(first * first + seed)
    values = (second.astype(F32) / 46337.0 - 0.5) * math.sqrt(12.0 / 108.0)
    return jnp.where(index < taps, values, 0.0).astype(BF16)


def features_kernel(seeds_ref, labels_ref, image_ref, out_ref, shifted, bank, pools):
    filters, (images, pixels) = seeds_ref.shape[1], image_ref.shape
    plane, window, half = SIDE * SIDE, 2 * BLOCK, BLOCK // 2
    taps = CHANNELS * KERNEL * KERNEL
    values = filter_values(seeds_ref[...], taps)
    tap = lax.broadcasted_iota(jnp.int32, (BLOCK, CHANNELS * window), 0)
    at = lax.broadcasted_iota(jnp.int32, (BLOCK, CHANNELS * window), 1)
    channel, row, column = at // window, (at % window) // SIDE, at % SIDE
    chosen = (tap == (channel * KERNEL + row) * KERNEL + column) & (row < KERNEL) & (column < KERNEL)
    spread = lax.dot_general(values, jnp.where(chosen, 1.0, 0.0).astype(BF16), ROWS, preferred_element_type=F32)
    for j in range(OUT):
        for t in range(0, CHANNELS * window, BLOCK):
            tile = spread[:, t : t + BLOCK]
            if j:
                tile = pltpu.roll(tile, 2 * j, 1)
            bank[j * filters : (j + 1) * filters, t : t + BLOCK] = tile.astype(BF16)
    shifted[:, : pixels - BLOCK] = image_ref[:, half : pixels - half]
    shifted[:, pixels - BLOCK :] = jnp.concatenate(
        [image_ref[:, pixels - half :], jnp.zeros((images, half), BF16)], axis=1
    )
    pools[...] = jnp.zeros_like(pools)

    def windows(ref, m):
        starts = [plane * c + BLOCK * m for c in range(CHANNELS)]
        return jnp.concatenate([ref[:, s : s + window] for s in starts], axis=1)

    for m in range(OUT // 2):
        both = jnp.concatenate([windows(image_ref, m), windows(shifted, m)], axis=0)
        for q in range(2):
            part = bank[POOL * q * filters : POOL * (q + 1) * filters, :]
            active = jnp.maximum(lax.dot_general(part, both, LANES, preferred_element_type=F32), 0.0)
            total = active[:filters]
            for j in range(1, POOL):
                total = total + active[j * filters : (j + 1) * filters]
            pools[2 * (2 * m // POOL) + q] += total[:, :images]
            pools[2 * ((2 * m + 1) // POOL) + q] += total[:, images:]
    for w in range(4):
        out_ref[pl.ds(w, filters, stride=4), :] = pools[w] * (1.0 / (POOL * POOL))
    out_ref[4 * filters :, :] = jnp.broadcast_to(labels_ref[...].astype(F32), (8, images))


def panel_block(images, labels, seeds):
    count, pixels = images.shape
    filters = seeds.shape[0]
    width = CHANNELS * 2 * BLOCK
    return call(
        features_kernel,
        [seeds[None], labels[None], images],
        [(4 * filters + 8, count)],
        [((count, pixels), BF16), ((OUT * filters, width), BF16), ((4, filters, count), F32)],
        flops=2 * OUT * OUT * filters * width * count,
    )[0]


def lane_copies(tile, lane):
    return jnp.broadcast_to(tile[:, lane : lane + 1], (8, BLOCK))


def row_copies(tile, row):
    return jnp.broadcast_to(tile[row : row + 1, :], (8, BLOCK))


def factor_block(tiles):
    lane = lax.broadcasted_iota(jnp.int32, (8, BLOCK), 1)
    row = lax.broadcasted_iota(jnp.int32, (8, BLOCK), 0)
    count = len(tiles)
    left = list(tiles)
    right = [jnp.where(lane == row + 8 * g, 1.0, 0.0) for g in range(count)]
    upper, inverse = [], []
    for p in range(count):
        a = [row_copies(left[p], i) for i in range(8)]
        b = [row_copies(right[p], i) for i in range(8)]
        s = {(i, j): lane_copies(a[i], 8 * p + j) for i in range(8) for j in range(i, 8)}
        cols = {g: [lane_copies(left[g], 8 * p + j) for j in range(8)] for g in range(p + 1, count)}
        for j in range(8):
            r = lax.rsqrt(s[j, j])
            r = r * (1.5 - 0.5 * s[j, j] * r * r)
            u = {c: s[j, c] * r for c in range(j + 1, 8)}
            a[j] = a[j] * r
            b[j] = b[j] * r
            for g in cols:
                cols[g][j] = cols[g][j] * r
            for i in range(j + 1, 8):
                for c in range(i, 8):
                    s[i, c] = s[i, c] - u[i] * u[c]
                a[i] = a[i] - u[i] * a[j]
                b[i] = b[i] - u[i] * b[j]
                for g in cols:
                    cols[g][i] = cols[g][i] - u[i] * cols[g][j]
        for g in cols:
            for j in range(8):
                left[g] = left[g] - cols[g][j] * a[j]
                right[g] = right[g] - cols[g][j] * b[j]
        top, bottom = a[0], b[0]
        for j in range(1, 8):
            top = jnp.where(row == j, a[j], top)
            bottom = jnp.where(row == j, b[j], bottom)
        upper.append(jnp.where(lane >= row + 8 * p, top, 0.0))
        inverse.append(bottom)
    return upper, inverse


def slots(feat):
    blocks = feat // BLOCK
    pairs = [(i, j) for i in range(blocks) for j in range(i, blocks)]
    return {pair: slice(n * BLOCK, (n + 1) * BLOCK) for n, pair in enumerate(pairs)}


def product(one, two):
    return lax.dot_general(one, two, LANES, preferred_element_type=F32)


def split(block_refs, high, low):
    feat, width = high.shape[0], block_refs[0].shape[1]
    for n, ref in enumerate(block_refs):
        at = slice(n * width, (n + 1) * width)
        whole = ref[:feat, :]
        top = whole.astype(BF16)
        high[:, at] = top
        low[:, at] = (whole - top.astype(F32)).astype(BF16)


def add_gram(so_far, gram_ref, high, low):
    feat = high.shape[0]
    place = slots(feat)
    for i in range(feat // BLOCK):
        at = slice(i * BLOCK, (i + 1) * BLOCK)
        one, two = high[at, :], low[at, :]
        cross = product(one, low[i * BLOCK :, :]) + product(two, high[i * BLOCK :, :])
        total = product(one, high[i * BLOCK :, :]) + (cross + product(two, low[i * BLOCK :, :]))
        for j in range(i, feat // BLOCK):
            tile = total[:, (j - i) * BLOCK : (j - i + 1) * BLOCK]
            gram_ref[place[i, j], :] = tile if so_far is None else so_far[place[i, j], :] + tile


def add_label_sums(starts_ref, block_refs, so_far, sums_refs, high, low, marks):
    feat, width = high.shape[0], block_refs[0].shape[1]
    class_row = lax.broadcasted_iota(jnp.int32, (marks.shape[0], width), 0)
    for d, sums_ref in enumerate(sums_refs):
        for n, ref in enumerate(block_refs):
            label = ref[feat : feat + 1, :].astype(jnp.int32) - starts_ref[d]
            marks[:, n * width : (n + 1) * width] = jnp.where(class_row == label, 1.0, 0.0).astype(BF16)
        total = product(marks[...], high[...]) + product(marks[...], low[...])
        sums_ref[...] = total if so_far is None else so_far[d][...] + total


def sums_kernel(blocks, carried, grams, starts_ref, *refs):
    so_far, block_refs, refs = refs[:carried], refs[carried : carried + blocks], refs[carried + blocks :]
    outs, (high, low, marks) = refs[:-3], refs[-3:]
    split(block_refs, high, low)
    if grams:
        add_gram(so_far[0] if carried else None, outs[0], high, low)
    if outs[grams:]:
        add_label_sums(starts_ref, block_refs, so_far[grams:] or None, outs[grams:], high, low, marks)


def panel_sums(gram, sums, blocks, starts, feat, classes, parts):
    width = sum(block.shape[1] for block in blocks)
    packed = (len(slots(feat)) * BLOCK, BLOCK)
    outs = [packed] * (gram is not False) + [(classes, feat)] * (parts if sums is not False else 0)
    carried = ([] if gram is None or gram is False else [gram]) + list(sums or [])
    kernel = lambda *refs: sums_kernel(len(blocks), len(carried), int(gram is not False), *refs)
    scratch = [((feat, width), BF16), ((feat, width), BF16), ((classes, width), BF16)]
    aliases = {1 + d: d for d in range(len(carried))}
    flops = 8 * width * math.prod(packed) + 4 * parts * width * classes * feat
    return call(kernel, [starts] + carried + blocks, outs, scratch, 1, flops, aliases)


def factor_kernel(ridge, parts, *refs):
    gram_refs, (factor_ref, inverse_ref, gram) = refs[:parts], refs[parts:]
    feat = gram.shape[0]
    blocks = feat // BLOCK
    for (i, j), at in slots(feat).items():
        total = gram_refs[0][at, :]
        for ref in gram_refs[1:]:
            total = total + ref[at, :]
        gram[i * BLOCK : (i + 1) * BLOCK, j * BLOCK : (j + 1) * BLOCK] = total
    factor_ref[...] = jnp.zeros_like(factor_ref)
    lane = lax.broadcasted_iota(jnp.int32, (8, BLOCK), 1)
    row = lax.broadcasted_iota(jnp.int32, (8, BLOCK), 0)

    def step(k, carry):
        start = pl.multiple_of(k * BLOCK, BLOCK)
        tiles = []
        for g in range(BLOCK // 8):
            tile = gram[pl.ds(pl.multiple_of(start + 8 * g, 8), 8), pl.ds(start, BLOCK)]
            tiles.append(tile + jnp.where(lane == row + 8 * g, ridge, 0.0))
        upper, inverted = factor_block(tiles)
        for g in range(BLOCK // 8):
            at = pl.ds(pl.multiple_of(start + 8 * g, 8), 8)
            factor_ref[at, pl.ds(start, BLOCK)] = upper[g]
            inverse_ref[at, :] = inverted[g]
        for kk in range(blocks - 1):

            @pl.when(k == kk)
            def _():
                at, rest = slice(BLOCK * kk, BLOCK * kk + BLOCK), BLOCK * kk + BLOCK
                across = jnp.dot(inverse_ref[at, :], gram[at, rest:], precision=HIGHEST, preferred_element_type=F32)
                factor_ref[at, rest:] = across
                for i in range(rest, feat, BLOCK):
                    part = across[:, i - rest : i - rest + BLOCK]
                    gram[i : i + BLOCK, i:] -= lax.dot_general(
                        part, across[:, i - rest :], ROWS, precision=HIGHEST, preferred_element_type=F32
                    )

        return carry

    lax.fori_loop(0, blocks, step, 0)


def solve_kernel(parts, factor_ref, inverse_ref, *refs):
    sums_refs, (turned_ref, sums) = refs[:parts], refs[parts:]
    feat = factor_ref.shape[0]
    total = sums_refs[0][...]
    for ref in sums_refs[1:]:
        total = total + ref[...]
    sums[...] = total
    for start in range(0, feat, BLOCK):
        at, rest = slice(start, start + BLOCK), start + BLOCK
        turned = lax.dot_general(
            sums[:, at], inverse_ref[at, :], LANES, precision=HIGHEST, preferred_element_type=F32
        )
        turned_ref[:, at] = turned[: turned_ref.shape[0], :]
        if rest < feat:
            sums[:, rest:] -= jnp.dot(turned, factor_ref[at, rest:], precision=HIGHEST, preferred_element_type=F32)


def factor_and_solve(grams, sums, ridge, feat, classes):
    kernel = lambda *refs: factor_kernel(ridge, len(grams), *refs)
    outs = [(feat, feat), (feat, BLOCK)]
    factor, inverse = call(kernel, grams, outs, [((feat, feat), F32)], flops=2 * feat**3)
    kernel = lambda *refs: solve_kernel(len(sums), *refs)
    turned = call(kernel, [factor, inverse] + sums, [(classes, feat)], [(sums[0].shape, F32)], flops=6 * classes * feat**2)[0]
    return factor, turned.T


def turns(size, step):
    return [(i, (i + step) % size) for i in range(size)]


def gather(block):
    size, across = lax.axis_size("img"), lax.axis_size("sub")
    near, far = [block], []
    for step in range(size):
        swapped = [lax.ppermute(near[-1], "sub", turns(across, d)) for d in range(1, across)]
        if step < size - 1:
            passed = lax.ppermute(near[-1], "img", turns(size, 1))
            passed, swapped = lax.optimization_barrier((passed, swapped))
            near.append(passed)
        far.append(swapped)
    early = near + [one for some in far[:-1] for one in some]
    return early, far[-1]


def shards(images, labels, seeds):
    count = images.shape[0]
    feat = 4 * seeds.shape[0]
    parts = lax.axis_size("cls")
    members = math.prod(lax.axis_size(axis) for axis in ("img", "sub", "cls"))
    ridge = RIDGE * count * members
    classes = CLASSES // parts
    padded = -(-classes // BLOCK) * BLOCK
    mine = lax.axis_index("cls")
    starts = classes * ((mine + jnp.arange(parts, dtype=jnp.int32)) % parts)
    block = panel_block(images, labels, seeds)
    if members <= MOST_BLOCKS:
        early, late = gather(block)
        gram, *sums = panel_sums(None, None, early, starts, feat, padded, parts)
        gram, *late = lax.optimization_barrier((gram, *late))
        gram = panel_sums(gram, False, late, starts, feat, padded, parts)[0]
        gram, *late = lax.optimization_barrier((gram, *late))
        sums = panel_sums(False, sums, late, starts, feat, padded, parts)
    else:
        gram, *sums = panel_sums(None, None, [block], starts, feat, padded, parts)
        gram, sums = lax.psum((gram, sums), ("img", "sub"))
    grams = [gram] + [lax.ppermute(gram, "cls", turns(parts, d)) for d in range(1, parts)]
    sums = [sums[0]] + [lax.ppermute(sums[d], "cls", turns(parts, d)) for d in range(1, parts)]
    return factor_and_solve(grams, sums, ridge, feat, classes)


def solution(mesh):
    placed = (P(("grp", "img", "sub", "cls"), None), P(("grp", "img", "sub", "cls")), P())
    return jax.shard_map(
        shards,
        mesh=mesh,
        in_specs=placed,
        out_specs=(P("grp", None), P("grp", "cls")),
        check_vma=False,
    )
```

```python
import math

import jax
import jax.numpy as jnp
from jax import lax
from jax.experimental import pallas as pl
from jax.experimental.pallas import tpu as pltpu
from jax.sharding import PartitionSpec as P

CLASSES = 1000
CHANNELS, SIDE, KERNEL, OUT, POOL = 3, 32, 6, 14, 7
MODULUS = 46337
RIDGE = 0.001
BLOCK = 128
HIGHEST = lax.Precision.HIGHEST
ROWS = (((0,), (0,)), ((), ()))
LANES = (((1,), (1,)), ((), ()))
VMEM_BYTES = 48 * 2**20
MOST_BLOCKS = 16
STRIDE = 8
F32, BF16 = jnp.float32, jnp.bfloat16


def call(kernel, operands, outs, scratch=(), scalars=0, flops=0, aliases=None):
    vmem = pl.BlockSpec(memory_space=pltpu.VMEM)
    smem = pl.BlockSpec(memory_space=pltpu.SMEM)
    moved = 4 * sum(math.prod(shape) for shape in outs) + sum(o.size * o.dtype.itemsize for o in operands)
    return pl.pallas_call(
        kernel,
        out_shape=[jax.ShapeDtypeStruct(shape, F32) for shape in outs],
        in_specs=[smem] * scalars + [vmem] * (len(operands) - scalars),
        out_specs=[vmem] * len(outs),
        scratch_shapes=[pltpu.VMEM(shape, dtype) for shape, dtype in scratch],
        input_output_aliases=aliases or {},
        cost_estimate=pl.CostEstimate(flops=flops, bytes_accessed=moved, transcendentals=0),
        compiler_params=pltpu.CompilerParams(vmem_limit_bytes=VMEM_BYTES),
    )(*operands)


def residue(x):
    quotient = jnp.floor(x.astype(F32) * (1.0 / MODULUS)).astype(jnp.int32)
    rest = x - quotient * MODULUS
    rest = jnp.where(rest < 0, rest + MODULUS, rest)
    return jnp.where(rest >= MODULUS, rest - MODULUS, rest)


def filter_values(seeds, taps):
    index = lax.broadcasted_iota(jnp.int32, (BLOCK, seeds.shape[1]), 0)
    seed = jnp.broadcast_to(seeds, index.shape)
    first = residue(seed * 7919 + index * 104729)
    second = residue(first * first + seed)
    values = (second.astype(F32) / 46337.0 - 0.5) * math.sqrt(12.0 / 108.0)
    return jnp.where(index < taps, values, 0.0).astype(BF16)


def features_kernel(seeds_ref, labels_ref, image_ref, out_ref, shifted, bank, pools):
    filters, (images, pixels) = seeds_ref.shape[1], image_ref.shape
    plane, window, half = SIDE * SIDE, 2 * BLOCK, BLOCK // 2
    taps = CHANNELS * KERNEL * KERNEL
    values = filter_values(seeds_ref[...], taps)
    tap = lax.broadcasted_iota(jnp.int32, (BLOCK, CHANNELS * window), 0)
    at = lax.broadcasted_iota(jnp.int32, (BLOCK, CHANNELS * window), 1)
    channel, row, column = at // window, (at % window) // SIDE, at % SIDE
    chosen = (tap == (channel * KERNEL + row) * KERNEL + column) & (row < KERNEL) & (column < KERNEL)
    spread = lax.dot_general(values, jnp.where(chosen, 1.0, 0.0).astype(BF16), ROWS, preferred_element_type=F32)
    for j in range(OUT):
        for t in range(0, CHANNELS * window, BLOCK):
            tile = spread[:, t : t + BLOCK]
            if j:
                tile = pltpu.roll(tile, 2 * j, 1)
            bank[j * filters : (j + 1) * filters, t : t + BLOCK] = tile.astype(BF16)
    shifted[:, : pixels - BLOCK] = image_ref[:, half : pixels - half]
    shifted[:, pixels - BLOCK :] = jnp.concatenate(
        [image_ref[:, pixels - half :], jnp.zeros((images, half), BF16)], axis=1
    )
    pools[...] = jnp.zeros_like(pools)

    def windows(ref, m):
        starts = [plane * c + BLOCK * m for c in range(CHANNELS)]
        return jnp.concatenate([ref[:, s : s + window] for s in starts], axis=1)

    for m in range(OUT // 2):
        both = jnp.concatenate([windows(image_ref, m), windows(shifted, m)], axis=0)
        for q in range(2):
            part = bank[POOL * q * filters : POOL * (q + 1) * filters, :]
            active = jnp.maximum(lax.dot_general(part, both, LANES, preferred_element_type=F32), 0.0)
            total = active[:filters]
            for j in range(1, POOL):
                total = total + active[j * filters : (j + 1) * filters]
            pools[2 * (2 * m // POOL) + q] += total[:, :images]
            pools[2 * ((2 * m + 1) // POOL) + q] += total[:, images:]
    for w in range(4):
        out_ref[pl.ds(w, filters, stride=4), :] = pools[w] * (1.0 / (POOL * POOL))
    out_ref[4 * filters :, :] = jnp.broadcast_to(labels_ref[...].astype(F32), (8, images))


def panel_block(images, labels, seeds):
    count, pixels = images.shape
    filters = seeds.shape[0]
    width = CHANNELS * 2 * BLOCK
    return call(
        features_kernel,
        [seeds[None], labels[None], images],
        [(4 * filters + 8, count)],
        [((count, pixels), BF16), ((OUT * filters, width), BF16), ((4, filters, count), F32)],
        flops=2 * OUT * OUT * filters * width * count,
    )[0]


def lane_copies(tile, lane):
    return jnp.broadcast_to(tile[:, lane : lane + 1], (8, BLOCK))


def row_copies(tile, row):
    return jnp.broadcast_to(tile[row : row + 1, :], (8, BLOCK))


def factor_block(tiles):
    lane = lax.broadcasted_iota(jnp.int32, (8, BLOCK), 1)
    row = lax.broadcasted_iota(jnp.int32, (8, BLOCK), 0)
    count = len(tiles)
    left = list(tiles)
    right = [jnp.where(lane == row + 8 * g, 1.0, 0.0) for g in range(count)]
    upper, inverse, raw = [], [], []
    own = [lane_copies(left[0], j) for j in range(8)]
    for p in range(count):
        top, bottom, scale = left[p], right[p], None
        stop = min(count, (p // STRIDE + 1) * STRIDE)
        cols = {g: [lane_copies(left[g], 8 * p + j) for j in range(8)] for g in range(p + 1, stop)}
        coming = [lane_copies(left[p + 1], 8 * p + 8 + j) for j in range(8)] if p + 1 < stop else []
        for j in range(8):
            pivot = row_copies(own[j], j)
            r = 1.0 / pivot
            for i in range(j + 1, 8):
                across = row_copies(own[i], j)
                t = across * r
                own[i] = own[i] - (own[j] * across) * r
                for g in cols:
                    cols[g][i] = cols[g][i] - cols[g][j] * t
            below = jnp.where(row > j, own[j], 0.0)
            top_row = row_copies(top, j) * r
            bottom_row = row_copies(bottom, j) * r
            top = top - below * top_row
            bottom = bottom - below * bottom_row
            for g in cols:
                left[g] = left[g] - cols[g][j] * top_row
                right[g] = right[g] - cols[g][j] * bottom_row
            if coming:
                edge = cols[p + 1][j]
                scaled = edge * r
                for c in range(8):
                    coming[c] = coming[c] - edge * row_copies(scaled, c)
            root = lax.rsqrt(pivot)
            scale = root if j == 0 else jnp.where(row == j, root, scale)
        raw.append(top * scale)
        upper.append(jnp.where(lane >= row + 8 * p, raw[p], 0.0))
        inverse.append(bottom * scale)
        if p + 1 == stop < count:
            done = slice(stop - STRIDE, stop)
            one = jnp.concatenate(raw[done], axis=0)
            both = jnp.concatenate([one, jnp.concatenate(inverse[done], axis=0)], axis=1)
            change = lax.dot_general(one, both, ROWS, precision=HIGHEST, preferred_element_type=F32)
            for g in range(stop, count):
                left[g] = left[g] - change[8 * g : 8 * g + 8, :BLOCK]
                right[g] = right[g] - change[8 * g : 8 * g + 8, BLOCK:]
            coming = [lane_copies(left[stop], 8 * stop + j) for j in range(8)]
        own = coming
    return upper, inverse


def slots(feat):
    blocks = feat // BLOCK
    pairs = [(i, j) for i in range(blocks) for j in range(i, blocks)]
    return {pair: slice(n * BLOCK, (n + 1) * BLOCK) for n, pair in enumerate(pairs)}


def product(one, two):
    return lax.dot_general(one, two, LANES, preferred_element_type=F32)


def split(block_refs, high, low):
    feat, width = high.shape[0], block_refs[0].shape[1]
    for n, ref in enumerate(block_refs):
        at = slice(n * width, (n + 1) * width)
        whole = ref[:feat, :]
        top = whole.astype(BF16)
        high[:, at] = top
        low[:, at] = (whole - top.astype(F32)).astype(BF16)


def add_gram(so_far, gram_ref, high, low):
    feat = high.shape[0]
    place = slots(feat)
    for i in range(feat // BLOCK):
        at = slice(i * BLOCK, (i + 1) * BLOCK)
        one, two = high[at, :], low[at, :]
        cross = product(one, low[i * BLOCK :, :]) + product(two, high[i * BLOCK :, :])
        total = product(one, high[i * BLOCK :, :]) + (cross + product(two, low[i * BLOCK :, :]))
        for j in range(i, feat // BLOCK):
            tile = total[:, (j - i) * BLOCK : (j - i + 1) * BLOCK]
            gram_ref[place[i, j], :] = tile if so_far is None else so_far[place[i, j], :] + tile


def add_label_sums(start_ref, block_refs, so_far, sums_ref, high, low, marks):
    feat, width = high.shape[0], block_refs[0].shape[1]
    class_row = lax.broadcasted_iota(jnp.int32, (marks.shape[0], width), 0) + start_ref[0]
    for n, ref in enumerate(block_refs):
        label = ref[feat : feat + 1, :].astype(jnp.int32)
        marks[:, n * width : (n + 1) * width] = jnp.where(class_row == label, 1.0, 0.0).astype(BF16)
    total = product(marks[...], high[...]) + product(marks[...], low[...])
    sums_ref[...] = total if so_far is None else so_far[...] + total


def sums_kernel(blocks, carried, start_ref, *refs):
    so_far, block_refs, refs = refs[:carried], refs[carried : carried + blocks], refs[carried + blocks :]
    gram_ref, sums_ref, high, low, marks = refs
    so_far = so_far or (None, None)
    split(block_refs, high, low)
    add_gram(so_far[0], gram_ref, high, low)
    add_label_sums(start_ref, block_refs, so_far[1], sums_ref, high, low, marks)


def panel_scratch(blocks, feat, classes):
    width = sum(block.shape[1] for block in blocks)
    return [((feat, width), BF16), ((feat, width), BF16), ((classes, width), BF16)]


def panel_sums(so_far, blocks, start, feat, classes):
    width = sum(block.shape[1] for block in blocks)
    packed = (len(slots(feat)) * BLOCK, BLOCK)
    carried = list(so_far or [])
    kernel = lambda *refs: sums_kernel(len(blocks), len(carried), *refs)
    aliases = {1 + d: d for d in range(len(carried))}
    flops = 8 * width * math.prod(packed) + 4 * width * classes * feat
    outs = [packed, (classes, feat)]
    return call(kernel, [start] + carried + blocks, outs, panel_scratch(blocks, feat, classes), 1, flops, aliases)


def solve_kernel(ridge, late, start_ref, *refs):
    gram_ref, sums_ref, block_refs, refs = refs[0], refs[1], refs[2 : 2 + late], refs[2 + late :]
    factor_ref, turned_ref, packed, gram, sums, inverse = refs[:6]
    if late:
        high, low, marks = refs[6:]
        split(block_refs, high, low)
        add_gram(gram_ref, packed, high, low)
        add_label_sums(start_ref, block_refs, sums_ref, sums, high, low, marks)
    else:
        packed[...] = gram_ref[...]
        sums[...] = sums_ref[...]
    feat = gram.shape[0]
    blocks = feat // BLOCK
    for (i, j), at in slots(feat).items():
        gram[i * BLOCK : (i + 1) * BLOCK, j * BLOCK : (j + 1) * BLOCK] = packed[at, :]
    factor_ref[...] = jnp.zeros_like(factor_ref)
    inverse[...] = jnp.zeros_like(inverse)
    lane = lax.broadcasted_iota(jnp.int32, (8, BLOCK), 1)
    row = lax.broadcasted_iota(jnp.int32, (8, BLOCK), 0)

    def turn(at):
        turned = lax.dot_general(sums[:, at], inverse[...], LANES, precision=HIGHEST, preferred_element_type=F32)
        turned_ref[:, at] = turned[: turned_ref.shape[0], :]
        return turned

    def step(k, carry):
        before = pl.ds(pl.multiple_of(jnp.maximum(k - 1, 0) * BLOCK, BLOCK), BLOCK)
        turned = turn(before)
        sums[...] -= jnp.dot(turned, factor_ref[before, :], precision=HIGHEST, preferred_element_type=F32)
        start = pl.multiple_of(k * BLOCK, BLOCK)
        tiles = []
        for g in range(BLOCK // 8):
            tile = gram[pl.ds(pl.multiple_of(start + 8 * g, 8), 8), pl.ds(start, BLOCK)]
            tiles.append(tile + jnp.where(lane == row + 8 * g, ridge, 0.0))
        upper, inverted = factor_block(tiles)
        for g in range(BLOCK // 8):
            factor_ref[pl.ds(pl.multiple_of(start + 8 * g, 8), 8), pl.ds(start, BLOCK)] = upper[g]
            inverse[8 * g : 8 * g + 8, :] = inverted[g]
        for kk in range(blocks - 1):

            @pl.when(k == kk)
            def _():
                at, rest = slice(BLOCK * kk, BLOCK * kk + BLOCK), BLOCK * kk + BLOCK
                across = jnp.dot(inverse[...], gram[at, rest:], precision=HIGHEST, preferred_element_type=F32)
                factor_ref[at, rest:] = across
                for i in range(rest, feat, BLOCK):
                    part = across[:, i - rest : i - rest + BLOCK]
                    gram[i : i + BLOCK, i:] -= lax.dot_general(
                        part, across[:, i - rest :], ROWS, precision=HIGHEST, preferred_element_type=F32
                    )

        return carry

    lax.fori_loop(0, blocks, step, 0)
    turn(slice(feat - BLOCK, feat))


def factor_and_solve(sums, late, start, ridge, feat, classes):
    padded = sums[1].shape[0]
    kernel = lambda *refs: solve_kernel(ridge, len(late), *refs)
    scratch = [(sums[0].shape, F32), ((feat, feat), F32), ((padded, feat), F32), ((BLOCK, BLOCK), F32)]
    if late:
        scratch += panel_scratch(late, feat, padded)
    outs = [(feat, feat), (classes, feat)]
    factor, turned = call(kernel, [start] + list(sums) + late, outs, scratch, 1, 6 * classes * feat**2)
    return factor, turned.T


def turns(size, step):
    return [(i, (i + step) % size) for i in range(size)]


def passed_on(blocks, axis):
    size = lax.axis_size(axis)
    return [lax.ppermute(block, axis, turns(size, d)) for block in blocks for d in range(1, size)]


def gathered_sums(block, sums_of):
    size = lax.axis_size("img")
    ring, came, ready, so_far = block, [block], [], None
    for step in range(size):
        swapped = passed_on([ring], "sub")
        crossed = passed_on(came, "cls") if step else []
        if step < size - 1:
            ring = lax.ppermute(ring, "img", turns(size, 1))
        if step == size - 1:
            so_far, pending = sums_of(so_far, ready + came + crossed), []
        elif step == size - 2:
            so_far, ready, pending = sums_of(so_far, ready + came), [], crossed
        else:
            pending = came + crossed if step else []
        ring, swapped, pending, so_far = lax.optimization_barrier((ring, swapped, pending, so_far))
        ready = ready + pending
        came = ([] if step else came) + swapped + ([ring] if step < size - 1 else [])
    return so_far, came + passed_on(came, "cls")


def shards(images, labels, seeds):
    count = images.shape[0]
    feat = 4 * seeds.shape[0]
    members = math.prod(lax.axis_size(axis) for axis in ("img", "sub", "cls"))
    ridge = RIDGE * count * members
    classes = CLASSES // lax.axis_size("cls")
    padded = -(-classes // BLOCK) * BLOCK
    start = jnp.full((1,), classes, jnp.int32) * lax.axis_index("cls")
    block = panel_block(images, labels, seeds)
    sums_of = lambda so_far, blocks: panel_sums(so_far, blocks, start, feat, padded)
    if members <= MOST_BLOCKS:
        sums, late = gathered_sums(block, sums_of)
    else:
        sums, late = lax.psum(tuple(sums_of(None, [block] + passed_on([block], "cls"))), ("img", "sub")), []
    return factor_and_solve(sums, late, start, ridge, feat, classes)


def solution(mesh):
    placed = (P(("grp", "img", "sub", "cls"), None), P(("grp", "img", "sub", "cls")), P())
    return jax.shard_map(
        shards,
        mesh=mesh,
        in_specs=placed,
        out_specs=(P("grp", None), P("grp", "cls")),
        check_vma=False,
    )
```

```python
import math

import jax
import jax.numpy as jnp
from jax import lax
from jax.experimental import pallas as pl
from jax.experimental.pallas import tpu as pltpu
from jax.sharding import PartitionSpec as P

CLASSES = 1000
CHANNELS, SIDE, KERNEL, OUT, POOL = 3, 32, 6, 14, 7
MODULUS = 46337
RIDGE = 0.001
BLOCK = 128
HIGHEST = lax.Precision.HIGHEST
ROWS = (((0,), (0,)), ((), ()))
LANES = (((1,), (1,)), ((), ()))
VMEM_BYTES = 48 * 2**20
VMEM_ALL = 62 * 2**20
MOST_BLOCKS = 16
STRIDE = 8
F32, BF16 = jnp.float32, jnp.bfloat16


def call(kernel, operands, outs, scratch=(), scalars=0, flops=0, aliases=None, in_hbm=0, vmem=VMEM_BYTES):
    spaces = [pltpu.SMEM] * scalars + [pltpu.VMEM] * (len(operands) - scalars - in_hbm) + [pltpu.HBM] * in_hbm
    moved = 4 * sum(math.prod(shape) for shape in outs) + sum(o.size * o.dtype.itemsize for o in operands)
    return pl.pallas_call(
        kernel,
        out_shape=[jax.ShapeDtypeStruct(shape, F32) for shape in outs],
        in_specs=[pl.BlockSpec(memory_space=space) for space in spaces],
        out_specs=[pl.BlockSpec(memory_space=pltpu.VMEM)] * len(outs),
        scratch_shapes=[pltpu.VMEM(*some) if isinstance(some, tuple) else some for some in scratch],
        input_output_aliases=aliases or {},
        cost_estimate=pl.CostEstimate(flops=flops, bytes_accessed=moved, transcendentals=0),
        compiler_params=pltpu.CompilerParams(vmem_limit_bytes=vmem),
    )(*operands)


def residue(x):
    quotient = jnp.floor(x.astype(F32) * (1.0 / MODULUS)).astype(jnp.int32)
    rest = x - quotient * MODULUS
    rest = jnp.where(rest < 0, rest + MODULUS, rest)
    return jnp.where(rest >= MODULUS, rest - MODULUS, rest)


def filter_values(seeds, taps):
    index = lax.broadcasted_iota(jnp.int32, (BLOCK, seeds.shape[1]), 0)
    seed = jnp.broadcast_to(seeds, index.shape)
    first = residue(seed * 7919 + index * 104729)
    second = residue(first * first + seed)
    values = (second.astype(F32) / 46337.0 - 0.5) * math.sqrt(12.0 / 108.0)
    return jnp.where(index < taps, values, 0.0).astype(BF16)


def features_kernel(seeds_at, labels_at, images_at, out_ref, seeds_ref, labels_ref, image_ref, shifted, bank, pools, arrived):
    filters, (images, pixels) = seeds_ref.shape[1], image_ref.shape
    pairs = [(seeds_at, seeds_ref), (images_at, image_ref), (labels_at, labels_ref)]
    copies = [pltpu.make_async_copy(one, two, arrived.at[n]) for n, (one, two) in enumerate(pairs)]
    for copy in copies:
        copy.start()
    copies[0].wait()
    plane, window, half = SIDE * SIDE, 2 * BLOCK, BLOCK // 2
    taps = CHANNELS * KERNEL * KERNEL
    values = filter_values(seeds_ref[...], taps)
    tap = lax.broadcasted_iota(jnp.int32, (BLOCK, CHANNELS * window), 0)
    at = lax.broadcasted_iota(jnp.int32, (BLOCK, CHANNELS * window), 1)
    channel, row, column = at // window, (at % window) // SIDE, at % SIDE
    chosen = (tap == (channel * KERNEL + row) * KERNEL + column) & (row < KERNEL) & (column < KERNEL)
    spread = lax.dot_general(values, jnp.where(chosen, 1.0, 0.0).astype(BF16), ROWS, preferred_element_type=F32)
    for j in range(OUT):
        for t in range(0, CHANNELS * window, BLOCK):
            tile = spread[:, t : t + BLOCK]
            if j:
                tile = pltpu.roll(tile, 2 * j, 1)
            bank[j * filters : (j + 1) * filters, t : t + BLOCK] = tile.astype(BF16)
    copies[1].wait()
    shifted[:, : pixels - BLOCK] = image_ref[:, half : pixels - half]
    shifted[:, pixels - BLOCK :] = jnp.concatenate(
        [image_ref[:, pixels - half :], jnp.zeros((images, half), BF16)], axis=1
    )
    pools[...] = jnp.zeros_like(pools)

    def windows(ref, m):
        starts = [plane * c + BLOCK * m for c in range(CHANNELS)]
        return jnp.concatenate([ref[:, s : s + window] for s in starts], axis=1)

    for m in range(OUT // 2):
        both = jnp.concatenate([windows(image_ref, m), windows(shifted, m)], axis=0)
        for q in range(2):
            part = bank[POOL * q * filters : POOL * (q + 1) * filters, :]
            active = jnp.maximum(lax.dot_general(part, both, LANES, preferred_element_type=F32), 0.0)
            total = active[:filters]
            for j in range(1, POOL):
                total = total + active[j * filters : (j + 1) * filters]
            pools[2 * (2 * m // POOL) + q] += total[:, :images]
            pools[2 * ((2 * m + 1) // POOL) + q] += total[:, images:]
    for w in range(4):
        out_ref[pl.ds(w, filters, stride=4), :] = pools[w] * (1.0 / (POOL * POOL))
    copies[2].wait()
    out_ref[4 * filters :, :] = jnp.broadcast_to(labels_ref[...].astype(F32), (8, images))


def panel_block(images, labels, seeds):
    count, pixels = images.shape
    filters = seeds.shape[0]
    width = CHANNELS * 2 * BLOCK
    return call(
        features_kernel,
        [seeds[None], labels[None], images],
        [(4 * filters + 8, count)],
        [((1, filters), jnp.int32), ((1, count), jnp.int32), ((count, pixels), BF16)]
        + [((count, pixels), BF16), ((OUT * filters, width), BF16), ((4, filters, count), F32)]
        + [pltpu.SemaphoreType.DMA((3,))],
        flops=2 * OUT * OUT * filters * width * count,
        in_hbm=3,
        vmem=VMEM_ALL,
    )[0]


def lane_copies(tile, lane):
    return jnp.broadcast_to(tile[:, lane : lane + 1], (8, BLOCK))


def row_copies(tile, row):
    return jnp.broadcast_to(tile[row : row + 1, :], (8, BLOCK))


def factor_block(tiles):
    lane = lax.broadcasted_iota(jnp.int32, (8, BLOCK), 1)
    row = lax.broadcasted_iota(jnp.int32, (8, BLOCK), 0)
    count = len(tiles)
    left = list(tiles)
    right = [jnp.where(lane == row + 8 * g, 1.0, 0.0) for g in range(count)]
    upper, inverse, raw = [], [], []
    own = [lane_copies(left[0], j) for j in range(8)]
    for p in range(count):
        top, bottom, scale = left[p], right[p], None
        stop = min(count, (p // STRIDE + 1) * STRIDE)
        cols = {g: [lane_copies(left[g], 8 * p + j) for j in range(8)] for g in range(p + 1, stop)}
        coming = [lane_copies(left[p + 1], 8 * p + 8 + j) for j in range(8)] if p + 1 < stop else []
        for j in range(8):
            pivot = row_copies(own[j], j)
            r = 1.0 / pivot
            for i in range(j + 1, 8):
                across = row_copies(own[i], j)
                t = across * r
                own[i] = own[i] - (own[j] * across) * r
                for g in cols:
                    cols[g][i] = cols[g][i] - cols[g][j] * t
            below = jnp.where(row > j, own[j], 0.0)
            top_row = row_copies(top, j) * r
            bottom_row = row_copies(bottom, j) * r
            top = top - below * top_row
            bottom = bottom - below * bottom_row
            for g in cols:
                left[g] = left[g] - cols[g][j] * top_row
                right[g] = right[g] - cols[g][j] * bottom_row
            if coming:
                edge = cols[p + 1][j]
                scaled = edge * r
                for c in range(8):
                    coming[c] = coming[c] - edge * row_copies(scaled, c)
            root = lax.rsqrt(pivot)
            scale = root if j == 0 else jnp.where(row == j, root, scale)
        raw.append(top * scale)
        upper.append(jnp.where(lane >= row + 8 * p, raw[p], 0.0))
        inverse.append(bottom * scale)
        if p + 1 == stop < count:
            done = slice(stop - STRIDE, stop)
            one = jnp.concatenate(raw[done], axis=0)
            both = jnp.concatenate([one, jnp.concatenate(inverse[done], axis=0)], axis=1)
            change = lax.dot_general(one, both, ROWS, precision=HIGHEST, preferred_element_type=F32)
            for g in range(stop, count):
                left[g] = left[g] - change[8 * g : 8 * g + 8, :BLOCK]
                right[g] = right[g] - change[8 * g : 8 * g + 8, BLOCK:]
            coming = [lane_copies(left[stop], 8 * stop + j) for j in range(8)]
        own = coming
    return upper, inverse


def slots(feat):
    blocks = feat // BLOCK
    pairs = [(i, j) for i in range(blocks) for j in range(i, blocks)]
    return {pair: slice(n * BLOCK, (n + 1) * BLOCK) for n, pair in enumerate(pairs)}


def product(one, two):
    return lax.dot_general(one, two, LANES, preferred_element_type=F32)


def split(block_refs, high, low):
    feat, width = high.shape[0], block_refs[0].shape[1]
    for n, ref in enumerate(block_refs):
        at = slice(n * width, (n + 1) * width)
        whole = ref[:feat, :]
        top = whole.astype(BF16)
        high[:, at] = top
        low[:, at] = (whole - top.astype(F32)).astype(BF16)


def add_gram(so_far, gram_ref, high, low):
    feat = high.shape[0]
    place = slots(feat)
    for i in range(feat // BLOCK):
        at = slice(i * BLOCK, (i + 1) * BLOCK)
        one, two = high[at, :], low[at, :]
        cross = product(one, low[i * BLOCK :, :]) + product(two, high[i * BLOCK :, :])
        total = product(one, high[i * BLOCK :, :]) + (cross + product(two, low[i * BLOCK :, :]))
        for j in range(i, feat // BLOCK):
            tile = total[:, (j - i) * BLOCK : (j - i + 1) * BLOCK]
            gram_ref[place[i, j], :] = tile if so_far is None else so_far[place[i, j], :] + tile


def add_label_sums(starts_ref, block_refs, so_far, sums_refs, high, low, marks):
    feat, width = high.shape[0], block_refs[0].shape[1]
    class_row = lax.broadcasted_iota(jnp.int32, (marks.shape[0], width), 0)
    for d, sums_ref in enumerate(sums_refs):
        for n, ref in enumerate(block_refs):
            label = ref[feat : feat + 1, :].astype(jnp.int32) - starts_ref[d]
            marks[:, n * width : (n + 1) * width] = jnp.where(class_row == label, 1.0, 0.0).astype(BF16)
        total = product(marks[...], high[...]) + product(marks[...], low[...])
        sums_ref[...] = total if so_far is None else so_far[d][...] + total


def sums_kernel(blocks, carried, starts_ref, *refs):
    so_far, block_refs, refs = refs[:carried], refs[carried : carried + blocks], refs[carried + blocks :]
    gram_ref, sums_refs, (high, low, marks) = refs[0], refs[1:-3], refs[-3:]
    split(block_refs, high, low)
    add_gram(so_far[0] if carried else None, gram_ref, high, low)
    add_label_sums(starts_ref, block_refs, so_far[1:] or None, sums_refs, high, low, marks)


def panel_scratch(blocks, feat, classes):
    width = sum(block.shape[1] for block in blocks)
    return [((feat, width), BF16), ((feat, width), BF16), ((classes, width), BF16)]


def panel_sums(so_far, blocks, starts, feat, classes, parts):
    width = sum(block.shape[1] for block in blocks)
    packed = (len(slots(feat)) * BLOCK, BLOCK)
    carried = list(so_far or [])
    kernel = lambda *refs: sums_kernel(len(blocks), len(carried), *refs)
    aliases = {1 + d: d for d in range(len(carried))}
    flops = 8 * width * math.prod(packed) + 4 * parts * width * classes * feat
    outs = [packed] + [(classes, feat)] * parts
    return call(kernel, [starts] + carried + blocks, outs, panel_scratch(blocks, feat, classes), 1, flops, aliases)


def solve_kernel(ridge, given, late, starts_ref, *refs):
    gram_refs, sums_refs, block_refs = refs[:given], refs[given : 2 * given], refs[2 * given : 2 * given + late]
    factor_ref, turned_ref, gram, sums, inverse = refs[2 * given + late :][:5]
    sources = list(gram_refs)
    if late:
        packed, high, low, marks = refs[-4:]
        split(block_refs, high, low)
        add_gram(None, packed, high, low)
        add_label_sums(starts_ref, block_refs, None, [sums], high, low, marks)
        sources.append(packed)
    else:
        sums[...] = jnp.zeros_like(sums)
    for ref in sums_refs:
        sums[...] += ref[...]
    feat = gram.shape[0]
    blocks = feat // BLOCK
    for (i, j), at in slots(feat).items():
        gram[i * BLOCK : (i + 1) * BLOCK, j * BLOCK : (j + 1) * BLOCK] = sum(ref[at, :] for ref in sources)
    factor_ref[...] = jnp.zeros_like(factor_ref)
    inverse[...] = jnp.zeros_like(inverse)
    lane = lax.broadcasted_iota(jnp.int32, (8, BLOCK), 1)
    row = lax.broadcasted_iota(jnp.int32, (8, BLOCK), 0)

    def turn(at):
        turned = lax.dot_general(sums[:, at], inverse[...], LANES, precision=HIGHEST, preferred_element_type=F32)
        turned_ref[:, at] = turned[: turned_ref.shape[0], :]
        return turned

    def step(k, carry):
        before = pl.ds(pl.multiple_of(jnp.maximum(k - 1, 0) * BLOCK, BLOCK), BLOCK)
        turned = turn(before)
        sums[...] -= jnp.dot(turned, factor_ref[before, :], precision=HIGHEST, preferred_element_type=F32)
        start = pl.multiple_of(k * BLOCK, BLOCK)
        tiles = []
        for g in range(BLOCK // 8):
            tile = gram[pl.ds(pl.multiple_of(start + 8 * g, 8), 8), pl.ds(start, BLOCK)]
            tiles.append(tile + jnp.where(lane == row + 8 * g, ridge, 0.0))
        upper, inverted = factor_block(tiles)
        for g in range(BLOCK // 8):
            factor_ref[pl.ds(pl.multiple_of(start + 8 * g, 8), 8), pl.ds(start, BLOCK)] = upper[g]
            inverse[8 * g : 8 * g + 8, :] = inverted[g]
        for kk in range(blocks - 1):

            @pl.when(k == kk)
            def _():
                at, rest = slice(BLOCK * kk, BLOCK * kk + BLOCK), BLOCK * kk + BLOCK
                across = jnp.dot(inverse[...], gram[at, rest:], precision=HIGHEST, preferred_element_type=F32)
                factor_ref[at, rest:] = across
                for i in range(rest, feat, BLOCK):
                    part = across[:, i - rest : i - rest + BLOCK]
                    gram[i : i + BLOCK, i:] -= lax.dot_general(
                        part, across[:, i - rest :], ROWS, precision=HIGHEST, preferred_element_type=F32
                    )

        return carry

    lax.fori_loop(0, blocks, step, 0)
    turn(slice(feat - BLOCK, feat))


def factor_and_solve(grams, sums, late, starts, ridge, feat, classes):
    padded = sums[0].shape[0]
    kernel = lambda *refs: solve_kernel(ridge, len(grams), len(late), *refs)
    scratch = [((feat, feat), F32), ((padded, feat), F32), ((BLOCK, BLOCK), F32)]
    if late:
        scratch += [(grams[0].shape, F32)] + panel_scratch(late, feat, padded)
    outs = [(feat, feat), (classes, feat)]
    factor, turned = call(kernel, [starts] + grams + sums + late, outs, scratch, 1, 6 * classes * feat**2)
    return factor, turned.T


def turns(size, step):
    return [(i, (i + step) % size) for i in range(size)]


def passed_on(blocks, axis):
    size = lax.axis_size(axis)
    return [lax.ppermute(block, axis, turns(size, d)) for block in blocks for d in range(1, size)]


def sums_passed_on(gram, sums):
    size = lax.axis_size("cls")
    return passed_on([gram], "cls"), [lax.ppermute(sums[d], "cls", turns(size, d)) for d in range(1, size)]


def gathered_sums(block, sums_of):
    size = lax.axis_size("img")
    ring, came, sums = block, [block], None
    for step in range(size):
        swapped = passed_on([ring], "sub")
        if step < size - 1:
            ring = lax.ppermute(ring, "img", turns(size, 1))
        if step >= size - 2:
            sums = sums_of(sums, came)
            came = []
        ring, swapped, sums = lax.optimization_barrier((ring, swapped, sums))
        came = came + swapped + ([ring] if step < size - 1 else [])
    gram, *sums = sums
    grams, others = sums_passed_on(gram, sums)
    return [gram] + grams, [sums[0]] + others, came + passed_on(came, "cls")


def shards(images, labels, seeds):
    count = images.shape[0]
    feat = 4 * seeds.shape[0]
    parts = lax.axis_size("cls")
    members = math.prod(lax.axis_size(axis) for axis in ("img", "sub", "cls"))
    ridge = RIDGE * count * members
    classes = CLASSES // parts
    padded = -(-classes // BLOCK) * BLOCK
    starts = classes * ((lax.axis_index("cls") + jnp.arange(parts, dtype=jnp.int32)) % parts)
    block = panel_block(images, labels, seeds)

    def sums_of(so_far, blocks):
        return panel_sums(so_far, blocks, starts, feat, padded, parts)

    if members <= MOST_BLOCKS:
        grams, sums, late = gathered_sums(block, sums_of)
    else:
        gram, *sums = lax.psum(tuple(sums_of(None, [block])), ("img", "sub"))
        grams, others = sums_passed_on(gram, sums)
        grams, sums, late = [gram] + grams, [sums[0]] + others, []
    return factor_and_solve(grams, sums, late, starts, ridge, feat, classes)


def solution(mesh):
    placed = (P(("grp", "img", "sub", "cls"), None), P(("grp", "img", "sub", "cls")), P())
    return jax.shard_map(
        shards,
        mesh=mesh,
        in_specs=placed,
        out_specs=(P("grp", None), P("grp", "cls")),
        check_vma=False,
    )
```

```python
import math

import jax
import jax.numpy as jnp
from jax import lax
from jax.experimental import pallas as pl
from jax.experimental.pallas import tpu as pltpu
from jax.sharding import PartitionSpec as P

CLASSES = 1000
CHANNELS, SIDE, KERNEL, OUT, POOL = 3, 32, 6, 14, 7
MODULUS = 46337
RIDGE = 0.001
BLOCK = 128
HIGHEST = lax.Precision.HIGHEST
ROWS = (((0,), (0,)), ((), ()))
LANES = (((1,), (1,)), ((), ()))
VMEM_BYTES = 48 * 2**20
VMEM_ALL = 62 * 2**20
MOST_BLOCKS = 16
STRIDE = 8
F32, BF16 = jnp.float32, jnp.bfloat16


def call(kernel, operands, outs, scratch=(), scalars=0, flops=0, aliases=None, in_hbm=0, vmem=VMEM_BYTES):
    spaces = [pltpu.SMEM] * scalars + [pltpu.VMEM] * (len(operands) - scalars - in_hbm) + [pltpu.HBM] * in_hbm
    moved = 4 * sum(math.prod(shape) for shape in outs) + sum(o.size * o.dtype.itemsize for o in operands)
    return pl.pallas_call(
        kernel,
        out_shape=[jax.ShapeDtypeStruct(shape, F32) for shape in outs],
        in_specs=[pl.BlockSpec(memory_space=space) for space in spaces],
        out_specs=[pl.BlockSpec(memory_space=pltpu.VMEM)] * len(outs),
        scratch_shapes=[pltpu.VMEM(*some) if isinstance(some, tuple) else some for some in scratch],
        input_output_aliases=aliases or {},
        cost_estimate=pl.CostEstimate(flops=flops, bytes_accessed=moved, transcendentals=0),
        compiler_params=pltpu.CompilerParams(vmem_limit_bytes=vmem),
    )(*operands)


def residue(x):
    quotient = jnp.floor(x.astype(F32) * (1.0 / MODULUS)).astype(jnp.int32)
    rest = x - quotient * MODULUS
    rest = jnp.where(rest < 0, rest + MODULUS, rest)
    return jnp.where(rest >= MODULUS, rest - MODULUS, rest)


def filter_values(seeds, taps):
    index = lax.broadcasted_iota(jnp.int32, (BLOCK, seeds.shape[1]), 0)
    seed = jnp.broadcast_to(seeds, index.shape)
    first = residue(seed * 7919 + index * 104729)
    second = residue(first * first + seed)
    values = (second.astype(F32) / 46337.0 - 0.5) * math.sqrt(12.0 / 108.0)
    return jnp.where(index < taps, values, 0.0).astype(BF16)


def features_kernel(seeds_at, labels_at, images_at, out_ref, seeds_ref, labels_ref, image_ref, shifted, bank, pools, arrived):
    filters, (images, pixels) = seeds_ref.shape[1], image_ref.shape
    pairs = [(seeds_at, seeds_ref), (images_at, image_ref), (labels_at, labels_ref)]
    copies = [pltpu.make_async_copy(one, two, arrived.at[n]) for n, (one, two) in enumerate(pairs)]
    for copy in copies:
        copy.start()
    copies[0].wait()
    plane, window, half = SIDE * SIDE, 2 * BLOCK, BLOCK // 2
    taps = CHANNELS * KERNEL * KERNEL
    values = filter_values(seeds_ref[...], taps)
    tap = lax.broadcasted_iota(jnp.int32, (BLOCK, CHANNELS * window), 0)
    at = lax.broadcasted_iota(jnp.int32, (BLOCK, CHANNELS * window), 1)
    channel, row, column = at // window, (at % window) // SIDE, at % SIDE
    chosen = (tap == (channel * KERNEL + row) * KERNEL + column) & (row < KERNEL) & (column < KERNEL)
    spread = lax.dot_general(values, jnp.where(chosen, 1.0, 0.0).astype(BF16), ROWS, preferred_element_type=F32)
    for j in range(OUT):
        for t in range(0, CHANNELS * window, BLOCK):
            tile = spread[:, t : t + BLOCK]
            if j:
                tile = pltpu.roll(tile, 2 * j, 1)
            bank[j * filters : (j + 1) * filters, t : t + BLOCK] = tile.astype(BF16)
    copies[1].wait()
    shifted[:, : pixels - BLOCK] = image_ref[:, half : pixels - half]
    shifted[:, pixels - BLOCK :] = jnp.concatenate(
        [image_ref[:, pixels - half :], jnp.zeros((images, half), BF16)], axis=1
    )
    pools[...] = jnp.zeros_like(pools)

    def windows(ref, m):
        starts = [plane * c + BLOCK * m for c in range(CHANNELS)]
        return jnp.concatenate([ref[:, s : s + window] for s in starts], axis=1)

    for m in range(OUT // 2):
        both = jnp.concatenate([windows(image_ref, m), windows(shifted, m)], axis=0)
        for q in range(2):
            part = bank[POOL * q * filters : POOL * (q + 1) * filters, :]
            active = jnp.maximum(lax.dot_general(part, both, LANES, preferred_element_type=F32), 0.0)
            total = active[:filters]
            for j in range(1, POOL):
                total = total + active[j * filters : (j + 1) * filters]
            pools[2 * (2 * m // POOL) + q] += total[:, :images]
            pools[2 * ((2 * m + 1) // POOL) + q] += total[:, images:]
    for w in range(4):
        out_ref[pl.ds(w, filters, stride=4), :] = pools[w] * (1.0 / (POOL * POOL))
    copies[2].wait()
    out_ref[4 * filters :, :] = jnp.broadcast_to(labels_ref[...].astype(F32), (8, images))


def panel_block(images, labels, seeds):
    count, pixels = images.shape
    filters = seeds.shape[0]
    width = CHANNELS * 2 * BLOCK
    return call(
        features_kernel,
        [seeds[None], labels[None], images],
        [(4 * filters + 8, count)],
        [((1, filters), jnp.int32), ((1, count), jnp.int32), ((count, pixels), BF16)]
        + [((count, pixels), BF16), ((OUT * filters, width), BF16), ((4, filters, count), F32)]
        + [pltpu.SemaphoreType.DMA((3,))],
        flops=2 * OUT * OUT * filters * width * count,
        in_hbm=3,
        vmem=VMEM_ALL,
    )[0]


def pieces(x):
    top = x.astype(BF16)
    rest = x - top.astype(F32)
    middle = rest.astype(BF16)
    return top, middle, (rest - middle.astype(F32)).astype(BF16)


def long_dot(one, two, dims):
    (left,), (right,) = dims
    a, b, c = one
    d, e, f = two
    return lax.dot_general(
        jnp.concatenate([a, a, b, a, b, c], axis=left),
        jnp.concatenate([d, e, d, f, e, d], axis=right),
        (dims, ((), ())),
        preferred_element_type=F32,
    )


def lane_copies(tile, lane):
    return jnp.broadcast_to(tile[:, lane : lane + 1], (8, BLOCK))


def row_copies(tile, row):
    return jnp.broadcast_to(tile[row : row + 1, :], (8, BLOCK))


def factor_block(tiles):
    lane = lax.broadcasted_iota(jnp.int32, (8, BLOCK), 1)
    row = lax.broadcasted_iota(jnp.int32, (8, BLOCK), 0)
    count = len(tiles)
    left = list(tiles)
    right = [jnp.where(lane == row + 8 * g, 1.0, 0.0) for g in range(count)]
    upper, inverse, raw = [], [], []
    own = [lane_copies(left[0], j) for j in range(8)]
    for p in range(count):
        top, bottom, scale = left[p], right[p], None
        stop = min(count, (p // STRIDE + 1) * STRIDE)
        cols = {g: [lane_copies(left[g], 8 * p + j) for j in range(8)] for g in range(p + 1, stop)}
        coming = [lane_copies(left[p + 1], 8 * p + 8 + j) for j in range(8)] if p + 1 < stop else []
        for j in range(8):
            pivot = row_copies(own[j], j)
            r = 1.0 / pivot
            for i in range(j + 1, 8):
                across = row_copies(own[i], j)
                t = across * r
                own[i] = own[i] - (own[j] * across) * r
                for g in cols:
                    cols[g][i] = cols[g][i] - cols[g][j] * t
            below = jnp.where(row > j, own[j], 0.0)
            top_row = row_copies(top, j) * r
            bottom_row = row_copies(bottom, j) * r
            top = top - below * top_row
            bottom = bottom - below * bottom_row
            for g in cols:
                left[g] = left[g] - cols[g][j] * top_row
                right[g] = right[g] - cols[g][j] * bottom_row
            if coming:
                edge = cols[p + 1][j]
                scaled = edge * r
                for c in range(8):
                    coming[c] = coming[c] - edge * row_copies(scaled, c)
            root = lax.rsqrt(pivot)
            scale = root if j == 0 else jnp.where(row == j, root, scale)
        raw.append(top * scale)
        upper.append(jnp.where(lane >= row + 8 * p, raw[p], 0.0))
        inverse.append(bottom * scale)
        if p + 1 == stop < count:
            done = slice(stop - STRIDE, stop)
            one = jnp.concatenate(raw[done], axis=0)
            both = jnp.concatenate([one, jnp.concatenate(inverse[done], axis=0)], axis=1)
            change = long_dot(pieces(one), pieces(both), ((0,), (0,)))
            for g in range(stop, count):
                left[g] = left[g] - change[8 * g : 8 * g + 8, :BLOCK]
                right[g] = right[g] - change[8 * g : 8 * g + 8, BLOCK:]
            coming = [lane_copies(left[stop], 8 * stop + j) for j in range(8)]
        own = coming
    return upper, inverse


def slots(feat):
    blocks = feat // BLOCK
    pairs = [(i, j) for i in range(blocks) for j in range(i, blocks)]
    return {pair: slice(n * BLOCK, (n + 1) * BLOCK) for n, pair in enumerate(pairs)}


def product(one, two):
    return lax.dot_general(one, two, LANES, preferred_element_type=F32)


def split(block_refs, high, low):
    feat, width = high.shape[0], block_refs[0].shape[1]
    for n, ref in enumerate(block_refs):
        at = slice(n * width, (n + 1) * width)
        whole = ref[:feat, :]
        top = whole.astype(BF16)
        high[:, at] = top
        low[:, at] = (whole - top.astype(F32)).astype(BF16)


def add_gram(so_far, gram_ref, high, low):
    feat = high.shape[0]
    place = slots(feat)
    for i in range(feat // BLOCK):
        at = slice(i * BLOCK, (i + 1) * BLOCK)
        one, two = high[at, :], low[at, :]
        cross = product(one, low[i * BLOCK :, :]) + product(two, high[i * BLOCK :, :])
        total = product(one, high[i * BLOCK :, :]) + (cross + product(two, low[i * BLOCK :, :]))
        for j in range(i, feat // BLOCK):
            tile = total[:, (j - i) * BLOCK : (j - i + 1) * BLOCK]
            gram_ref[place[i, j], :] = tile if so_far is None else so_far[place[i, j], :] + tile


def add_label_sums(starts_ref, block_refs, so_far, sums_refs, high, low, marks):
    feat, width = high.shape[0], block_refs[0].shape[1]
    class_row = lax.broadcasted_iota(jnp.int32, (marks.shape[0], width), 0)
    for d, sums_ref in enumerate(sums_refs):
        for n, ref in enumerate(block_refs):
            label = ref[feat : feat + 1, :].astype(jnp.int32) - starts_ref[d]
            marks[:, n * width : (n + 1) * width] = jnp.where(class_row == label, 1.0, 0.0).astype(BF16)
        total = product(marks[...], high[...]) + product(marks[...], low[...])
        sums_ref[...] = total if so_far is None else so_far[d][...] + total


def sums_kernel(blocks, carried, starts_ref, *refs):
    so_far, block_refs, refs = refs[:carried], refs[carried : carried + blocks], refs[carried + blocks :]
    gram_ref, sums_refs, (high, low, marks) = refs[0], refs[1:-3], refs[-3:]
    split(block_refs, high, low)
    add_gram(so_far[0] if carried else None, gram_ref, high, low)
    add_label_sums(starts_ref, block_refs, so_far[1:] or None, sums_refs, high, low, marks)


def panel_scratch(blocks, feat, classes):
    width = sum(block.shape[1] for block in blocks)
    return [((feat, width), BF16), ((feat, width), BF16), ((classes, width), BF16)]


def panel_sums(so_far, blocks, starts, feat, classes, parts):
    width = sum(block.shape[1] for block in blocks)
    packed = (len(slots(feat)) * BLOCK, BLOCK)
    carried = list(so_far or [])
    kernel = lambda *refs: sums_kernel(len(blocks), len(carried), *refs)
    aliases = {1 + d: d for d in range(len(carried))}
    flops = 8 * width * math.prod(packed) + 4 * parts * width * classes * feat
    outs = [packed] + [(classes, feat)] * parts
    return call(kernel, [starts] + carried + blocks, outs, panel_scratch(blocks, feat, classes), 1, flops, aliases)


def solve_kernel(ridge, given, late, starts_ref, *refs):
    gram_refs, sums_refs, block_refs = refs[:given], refs[given : 2 * given], refs[2 * given : 2 * given + late]
    factor_ref, turned_ref, gram, sums, inverse = refs[2 * given + late :][:5]
    sources = list(gram_refs)
    if late:
        packed, high, low, marks = refs[-4:]
        split(block_refs, high, low)
        add_gram(None, packed, high, low)
        add_label_sums(starts_ref, block_refs, None, [sums], high, low, marks)
        sources.append(packed)
    else:
        sums[...] = jnp.zeros_like(sums)
    for ref in sums_refs:
        sums[...] += ref[...]
    feat = gram.shape[0]
    for (i, j), at in slots(feat).items():
        gram[i * BLOCK : (i + 1) * BLOCK, j * BLOCK : (j + 1) * BLOCK] = sum(ref[at, :] for ref in sources)
    factor_ref[...] = jnp.zeros_like(factor_ref)
    lane = lax.broadcasted_iota(jnp.int32, (8, BLOCK), 1)
    row = lax.broadcasted_iota(jnp.int32, (8, BLOCK), 0)

    def turn(at):
        turned = lax.dot_general(sums[:, at], inverse[...], LANES, precision=HIGHEST, preferred_element_type=F32)
        turned_ref[:, at] = turned[: turned_ref.shape[0], :]
        return turned

    for start in range(0, feat, BLOCK):
        at, rest = slice(start, start + BLOCK), start + BLOCK
        if start:
            before = slice(start - BLOCK, start)
            taken = jnp.dot(turn(before), factor_ref[before, start:], precision=HIGHEST, preferred_element_type=F32)
            sums[:, start:] -= taken
        tiles = []
        for g in range(BLOCK // 8):
            tile = gram[start + 8 * g : start + 8 * g + 8, at]
            tiles.append(tile + jnp.where(lane == row + 8 * g, ridge, 0.0))
        upper, inverted = factor_block(tiles)
        for g in range(BLOCK // 8):
            factor_ref[start + 8 * g : start + 8 * g + 8, at] = upper[g]
            inverse[8 * g : 8 * g + 8, :] = inverted[g]
        parts, turner = [], pieces(inverse[...])
        for i in range(rest, feat, BLOCK):
            here = slice(i, i + BLOCK)
            across = long_dot(turner, pieces(gram[at, here]), ((1,), (0,)))
            factor_ref[at, here] = across
            parts.append(pieces(across))
            for n, part in enumerate(parts):
                there = slice(rest + n * BLOCK, rest + (n + 1) * BLOCK)
                gram[there, here] -= long_dot(part, parts[-1], ((0,), (0,)))
    turn(slice(feat - BLOCK, feat))


def factor_and_solve(grams, sums, late, starts, ridge, feat, classes):
    padded = sums[0].shape[0]
    kernel = lambda *refs: solve_kernel(ridge, len(grams), len(late), *refs)
    scratch = [((feat, feat), F32), ((padded, feat), F32), ((BLOCK, BLOCK), F32)]
    if late:
        scratch += [(grams[0].shape, F32)] + panel_scratch(late, feat, padded)
    outs = [(feat, feat), (classes, feat)]
    factor, turned = call(kernel, [starts] + grams + sums + late, outs, scratch, 1, 6 * classes * feat**2)
    return factor, turned.T


def turns(size, step):
    return [(i, (i + step) % size) for i in range(size)]


def passed_on(blocks, axis):
    size = lax.axis_size(axis)
    return [lax.ppermute(block, axis, turns(size, d)) for block in blocks for d in range(1, size)]


def sums_passed_on(gram, sums):
    size = lax.axis_size("cls")
    return passed_on([gram], "cls"), [lax.ppermute(sums[d], "cls", turns(size, d)) for d in range(1, size)]


def gathered_sums(block, sums_of):
    size = lax.axis_size("img")
    ring, came, sums = block, [block], None
    for step in range(size):
        swapped = passed_on([ring], "sub")
        if step < size - 1:
            ring = lax.ppermute(ring, "img", turns(size, 1))
        if step:
            sums = sums_of(sums, came)
            came = []
        ring, swapped, sums = lax.optimization_barrier((ring, swapped, sums))
        came = came + swapped + ([ring] if step < size - 1 else [])
    gram, *sums = sums
    grams, others = sums_passed_on(gram, sums)
    return [gram] + grams, [sums[0]] + others, came + passed_on(came, "cls")


def shards(images, labels, seeds):
    count = images.shape[0]
    feat = 4 * seeds.shape[0]
    parts = lax.axis_size("cls")
    members = math.prod(lax.axis_size(axis) for axis in ("img", "sub", "cls"))
    ridge = RIDGE * count * members
    classes = CLASSES // parts
    padded = -(-classes // BLOCK) * BLOCK
    starts = classes * ((lax.axis_index("cls") + jnp.arange(parts, dtype=jnp.int32)) % parts)
    block = panel_block(images, labels, seeds)

    def sums_of(so_far, blocks):
        return panel_sums(so_far, blocks, starts, feat, padded, parts)

    if members <= MOST_BLOCKS:
        grams, sums, late = gathered_sums(block, sums_of)
    else:
        gram, *sums = lax.psum(tuple(sums_of(None, [block])), ("img", "sub"))
        grams, others = sums_passed_on(gram, sums)
        grams, sums, late = [gram] + grams, [sums[0]] + others, []
    return factor_and_solve(grams, sums, late, starts, ridge, feat, classes)


def solution(mesh):
    placed = (P(("grp", "img", "sub", "cls"), None), P(("grp", "img", "sub", "cls")), P())
    return jax.shard_map(
        shards,
        mesh=mesh,
        in_specs=placed,
        out_specs=(P("grp", None), P("grp", "cls")),
        check_vma=False,
    )
```

```python
import math

import jax
import jax.numpy as jnp
from jax import lax
from jax.experimental import pallas as pl
from jax.experimental.pallas import tpu as pltpu
from jax.sharding import PartitionSpec as P

CLASSES = 1000
CHANNELS, SIDE, KERNEL, OUT, POOL = 3, 32, 6, 14, 7
MODULUS = 46337
RIDGE = 0.001
BLOCK = 128
HIGHEST = lax.Precision.HIGHEST
ROWS = (((0,), (0,)), ((), ()))
LANES = (((1,), (1,)), ((), ()))
VMEM_BYTES = 48 * 2**20
VMEM_ALL = 62 * 2**20
MOST_BLOCKS = 16
STRIDE = 8
F32, BF16 = jnp.float32, jnp.bfloat16


def call(kernel, operands, outs, scratch=(), scalars=0, flops=0, aliases=None, in_hbm=0, vmem=VMEM_BYTES):
    spaces = [pltpu.SMEM] * scalars + [pltpu.VMEM] * (len(operands) - scalars - in_hbm) + [pltpu.HBM] * in_hbm
    moved = 4 * sum(math.prod(shape) for shape in outs) + sum(o.size * o.dtype.itemsize for o in operands)
    return pl.pallas_call(
        kernel,
        out_shape=[jax.ShapeDtypeStruct(shape, F32) for shape in outs],
        in_specs=[pl.BlockSpec(memory_space=space) for space in spaces],
        out_specs=[pl.BlockSpec(memory_space=pltpu.VMEM)] * len(outs),
        scratch_shapes=[pltpu.VMEM(*some) if isinstance(some, tuple) else some for some in scratch],
        input_output_aliases=aliases or {},
        cost_estimate=pl.CostEstimate(flops=flops, bytes_accessed=moved, transcendentals=0),
        compiler_params=pltpu.CompilerParams(vmem_limit_bytes=vmem),
    )(*operands)


def residue(x):
    quotient = jnp.floor(x.astype(F32) * (1.0 / MODULUS)).astype(jnp.int32)
    rest = x - quotient * MODULUS
    rest = jnp.where(rest < 0, rest + MODULUS, rest)
    return jnp.where(rest >= MODULUS, rest - MODULUS, rest)


def filter_values(seeds, taps):
    index = lax.broadcasted_iota(jnp.int32, (BLOCK, seeds.shape[1]), 0)
    seed = jnp.broadcast_to(seeds, index.shape)
    first = residue(seed * 7919 + index * 104729)
    second = residue(first * first + seed)
    values = (second.astype(F32) / 46337.0 - 0.5) * math.sqrt(12.0 / 108.0)
    return jnp.where(index < taps, values, 0.0).astype(BF16)


def features_kernel(seeds_at, labels_at, images_at, top_ref, bottom_ref, seeds_ref, labels_ref, image_ref, shifted, bank, pools, arrived):
    filters, (images, pixels) = seeds_ref.shape[1], image_ref.shape
    pairs = [(seeds_at, seeds_ref), (images_at, image_ref), (labels_at, labels_ref)]
    copies = [pltpu.make_async_copy(one, two, arrived.at[n]) for n, (one, two) in enumerate(pairs)]
    for copy in copies:
        copy.start()
    copies[0].wait()
    plane, window, half = SIDE * SIDE, 2 * BLOCK, BLOCK // 2
    taps = CHANNELS * KERNEL * KERNEL
    values = filter_values(seeds_ref[...], taps)
    tap = lax.broadcasted_iota(jnp.int32, (BLOCK, CHANNELS * window), 0)
    at = lax.broadcasted_iota(jnp.int32, (BLOCK, CHANNELS * window), 1)
    channel, row, column = at // window, (at % window) // SIDE, at % SIDE
    chosen = (tap == (channel * KERNEL + row) * KERNEL + column) & (row < KERNEL) & (column < KERNEL)
    spread = lax.dot_general(values, jnp.where(chosen, 1.0, 0.0).astype(BF16), ROWS, preferred_element_type=F32)
    for j in range(OUT):
        for t in range(0, CHANNELS * window, BLOCK):
            tile = spread[:, t : t + BLOCK]
            if j:
                tile = pltpu.roll(tile, 2 * j, 1)
            bank[j * filters : (j + 1) * filters, t : t + BLOCK] = tile.astype(BF16)
    copies[1].wait()
    shifted[:, : pixels - BLOCK] = image_ref[:, half : pixels - half]
    shifted[:, pixels - BLOCK :] = jnp.concatenate(
        [image_ref[:, pixels - half :], jnp.zeros((images, half), BF16)], axis=1
    )
    pools[...] = jnp.zeros_like(pools)

    def windows(ref, m):
        starts = [plane * c + BLOCK * m for c in range(CHANNELS)]
        return jnp.concatenate([ref[:, s : s + window] for s in starts], axis=1)

    for m in range(OUT // 2):
        both = jnp.concatenate([windows(image_ref, m), windows(shifted, m)], axis=0)
        for q in range(2):
            part = bank[POOL * q * filters : POOL * (q + 1) * filters, :]
            active = jnp.maximum(lax.dot_general(part, both, LANES, preferred_element_type=F32), 0.0)
            total = active[:filters]
            for j in range(1, POOL):
                total = total + active[j * filters : (j + 1) * filters]
            pools[2 * (2 * m // POOL) + q] += total[:, :images]
            pools[2 * ((2 * m + 1) // POOL) + q] += total[:, images:]
    for n, ref in enumerate((top_ref, bottom_ref)):
        some = slice(n * filters // 2, (n + 1) * filters // 2)
        for w in range(4):
            ref[pl.ds(w, filters // 2, stride=4), :] = pools[w, some] * (1.0 / (POOL * POOL))
    copies[2].wait()
    bottom_ref[2 * filters :, :] = jnp.broadcast_to(labels_ref[...].astype(F32), (8, images))


def panel_block(images, labels, seeds):
    count, pixels = images.shape
    filters = seeds.shape[0]
    width = CHANNELS * 2 * BLOCK
    return call(
        features_kernel,
        [seeds[None], labels[None], images],
        [(2 * filters, count), (2 * filters + 8, count)],
        [((1, filters), jnp.int32), ((1, count), jnp.int32), ((count, pixels), BF16)]
        + [((count, pixels), BF16), ((OUT * filters, width), BF16), ((4, filters, count), F32)]
        + [pltpu.SemaphoreType.DMA((3,))],
        flops=2 * OUT * OUT * filters * width * count,
        in_hbm=3,
        vmem=VMEM_ALL,
    )


def pieces(x):
    top = x.astype(BF16)
    rest = x - top.astype(F32)
    middle = rest.astype(BF16)
    return top, middle, (rest - middle.astype(F32)).astype(BF16)


def long_dot(one, two, dims):
    (left,), (right,) = dims
    a, b, c = one
    d, e, f = two
    return lax.dot_general(
        jnp.concatenate([a, a, b, a, b, c], axis=left),
        jnp.concatenate([d, e, d, f, e, d], axis=right),
        (dims, ((), ())),
        preferred_element_type=F32,
    )


def lane_copies(tile, lane):
    return jnp.broadcast_to(tile[:, lane : lane + 1], (8, BLOCK))


def row_copies(tile, row):
    return jnp.broadcast_to(tile[row : row + 1, :], (8, BLOCK))


def factor_block(tiles):
    lane = lax.broadcasted_iota(jnp.int32, (8, BLOCK), 1)
    row = lax.broadcasted_iota(jnp.int32, (8, BLOCK), 0)
    count = len(tiles)
    left = list(tiles)
    right = [jnp.where(lane == row + 8 * g, 1.0, 0.0) for g in range(count)]
    upper, inverse, raw = [], [], []
    own = [lane_copies(left[0], j) for j in range(8)]
    for p in range(count):
        top, bottom, scale = left[p], right[p], None
        stop = min(count, (p // STRIDE + 1) * STRIDE)
        cols = {g: [lane_copies(left[g], 8 * p + j) for j in range(8)] for g in range(p + 1, stop)}
        coming = [lane_copies(left[p + 1], 8 * p + 8 + j) for j in range(8)] if p + 1 < stop else []
        for j in range(8):
            pivot = row_copies(own[j], j)
            r = 1.0 / pivot
            for i in range(j + 1, 8):
                across = row_copies(own[i], j)
                t = across * r
                own[i] = own[i] - (own[j] * across) * r
                for g in cols:
                    cols[g][i] = cols[g][i] - cols[g][j] * t
            below = jnp.where(row > j, own[j], 0.0)
            top_row = row_copies(top, j) * r
            bottom_row = row_copies(bottom, j) * r
            top = top - below * top_row
            bottom = bottom - below * bottom_row
            for g in cols:
                left[g] = left[g] - cols[g][j] * top_row
                right[g] = right[g] - cols[g][j] * bottom_row
            if coming:
                edge = cols[p + 1][j]
                scaled = edge * r
                for c in range(8):
                    coming[c] = coming[c] - edge * row_copies(scaled, c)
            root = lax.rsqrt(pivot)
            scale = root if j == 0 else jnp.where(row == j, root, scale)
        raw.append(top * scale)
        upper.append(jnp.where(lane >= row + 8 * p, raw[p], 0.0))
        inverse.append(bottom * scale)
        if p + 1 == stop < count:
            done = slice(stop - STRIDE, stop)
            one = jnp.concatenate(raw[done], axis=0)
            both = jnp.concatenate([one, jnp.concatenate(inverse[done], axis=0)], axis=1)
            change = long_dot(pieces(one), pieces(both), ((0,), (0,)))
            for g in range(stop, count):
                left[g] = left[g] - change[8 * g : 8 * g + 8, :BLOCK]
                right[g] = right[g] - change[8 * g : 8 * g + 8, BLOCK:]
            coming = [lane_copies(left[stop], 8 * stop + j) for j in range(8)]
        own = coming
    return upper, inverse


def slots(feat):
    blocks = feat // BLOCK
    pairs = [(i, j) for i in range(blocks) for j in range(i, blocks)]
    return {pair: slice(n * BLOCK, (n + 1) * BLOCK) for n, pair in enumerate(pairs)}


def product(one, two):
    return lax.dot_general(one, two, LANES, preferred_element_type=F32)


def in_pairs(refs):
    return list(zip(refs[::2], refs[1::2]))


def split(block_refs, high, low):
    half, width = high.shape[0] // 2, block_refs[0][0].shape[1]
    for n, refs in enumerate(block_refs):
        at = slice(n * width, (n + 1) * width)
        for h, ref in enumerate(refs):
            rows = slice(h * half, (h + 1) * half)
            whole = ref[:half, :]
            top = whole.astype(BF16)
            high[rows, at] = top
            low[rows, at] = (whole - top.astype(F32)).astype(BF16)


def add_gram(so_far, gram_ref, high, low):
    feat = high.shape[0]
    place = slots(feat)
    for i in range(feat // BLOCK):
        at = slice(i * BLOCK, (i + 1) * BLOCK)
        one, two = high[at, :], low[at, :]
        cross = product(one, low[i * BLOCK :, :]) + product(two, high[i * BLOCK :, :])
        total = product(one, high[i * BLOCK :, :]) + (cross + product(two, low[i * BLOCK :, :]))
        for j in range(i, feat // BLOCK):
            tile = total[:, (j - i) * BLOCK : (j - i + 1) * BLOCK]
            gram_ref[place[i, j], :] = tile if so_far is None else so_far[place[i, j], :] + tile


def add_label_sums(starts_ref, block_refs, so_far, sums_refs, high, low, marks):
    half, width = high.shape[0] // 2, block_refs[0][0].shape[1]
    class_row = lax.broadcasted_iota(jnp.int32, (marks.shape[0], width), 0)
    for d, sums_ref in enumerate(sums_refs):
        for n, (_, ref) in enumerate(block_refs):
            label = ref[half : half + 1, :].astype(jnp.int32) - starts_ref[d]
            marks[:, n * width : (n + 1) * width] = jnp.where(class_row == label, 1.0, 0.0).astype(BF16)
        total = product(marks[...], high[...]) + product(marks[...], low[...])
        sums_ref[...] = total if so_far is None else so_far[d][...] + total


def sums_kernel(blocks, carried, starts_ref, *refs):
    so_far, block_refs, refs = refs[:carried], in_pairs(refs[carried : carried + 2 * blocks]), refs[carried + 2 * blocks :]
    gram_ref, sums_refs, (high, low, marks) = refs[0], refs[1:-3], refs[-3:]
    split(block_refs, high, low)
    add_gram(so_far[0] if carried else None, gram_ref, high, low)
    add_label_sums(starts_ref, block_refs, so_far[1:] or None, sums_refs, high, low, marks)


def panel_scratch(blocks, feat, classes):
    width = sum(block[0].shape[1] for block in blocks)
    return [((feat, width), BF16), ((feat, width), BF16), ((classes, width), BF16)]


def panel_sums(so_far, blocks, starts, feat, classes, parts):
    width = sum(block[0].shape[1] for block in blocks)
    packed = (len(slots(feat)) * BLOCK, BLOCK)
    carried = list(so_far or [])
    kernel = lambda *refs: sums_kernel(len(blocks), len(carried), *refs)
    aliases = {1 + d: d for d in range(len(carried))}
    flops = 8 * width * math.prod(packed) + 4 * parts * width * classes * feat
    outs = [packed] + [(classes, feat)] * parts
    operands = [starts] + carried + [half for block in blocks for half in block]
    return call(kernel, operands, outs, panel_scratch(blocks, feat, classes), 1, flops, aliases)


def solve_kernel(ridge, given, late, starts_ref, *refs):
    gram_refs, sums_refs, refs = refs[:given], refs[given : 2 * given], refs[2 * given :]
    block_refs, (factor_ref, turned_ref, gram, sums, inverse) = in_pairs(refs[: 2 * late]), refs[2 * late :][:5]
    sources = list(gram_refs)
    if late:
        packed, high, low, marks = refs[-4:]
        split(block_refs, high, low)
        add_gram(None, packed, high, low)
        add_label_sums(starts_ref, block_refs, None, [sums], high, low, marks)
        sources.append(packed)
    else:
        sums[...] = jnp.zeros_like(sums)
    for ref in sums_refs:
        sums[...] += ref[...]
    feat = gram.shape[0]
    for (i, j), at in slots(feat).items():
        gram[i * BLOCK : (i + 1) * BLOCK, j * BLOCK : (j + 1) * BLOCK] = sum(ref[at, :] for ref in sources)
    factor_ref[...] = jnp.zeros_like(factor_ref)
    lane = lax.broadcasted_iota(jnp.int32, (8, BLOCK), 1)
    row = lax.broadcasted_iota(jnp.int32, (8, BLOCK), 0)

    def turn(at):
        turned = lax.dot_general(sums[:, at], inverse[...], LANES, precision=HIGHEST, preferred_element_type=F32)
        turned_ref[:, at] = turned[: turned_ref.shape[0], :]
        return turned

    for start in range(0, feat, BLOCK):
        at, rest = slice(start, start + BLOCK), start + BLOCK
        if start:
            before = slice(start - BLOCK, start)
            taken = jnp.dot(turn(before), factor_ref[before, start:], precision=HIGHEST, preferred_element_type=F32)
            sums[:, start:] -= taken
        tiles = []
        for g in range(BLOCK // 8):
            tile = gram[start + 8 * g : start + 8 * g + 8, at]
            tiles.append(tile + jnp.where(lane == row + 8 * g, ridge, 0.0))
        upper, inverted = factor_block(tiles)
        for g in range(BLOCK // 8):
            factor_ref[start + 8 * g : start + 8 * g + 8, at] = upper[g]
            inverse[8 * g : 8 * g + 8, :] = inverted[g]
        parts, turner = [], pieces(inverse[...])
        for i in range(rest, feat, BLOCK):
            here = slice(i, i + BLOCK)
            across = long_dot(turner, pieces(gram[at, here]), ((1,), (0,)))
            factor_ref[at, here] = across
            parts.append(pieces(across))
            for n, part in enumerate(parts):
                there = slice(rest + n * BLOCK, rest + (n + 1) * BLOCK)
                gram[there, here] -= long_dot(part, parts[-1], ((0,), (0,)))
    turn(slice(feat - BLOCK, feat))


def factor_and_solve(grams, sums, late, starts, ridge, feat, classes):
    padded = sums[0].shape[0]
    kernel = lambda *refs: solve_kernel(ridge, len(grams), len(late), *refs)
    scratch = [((feat, feat), F32), ((padded, feat), F32), ((BLOCK, BLOCK), F32)]
    if late:
        scratch += [(grams[0].shape, F32)] + panel_scratch(late, feat, padded)
    outs = [(feat, feat), (classes, feat)]
    factor, turned = call(kernel, [starts] + grams + sums + [half for block in late for half in block], outs, scratch, 1, 6 * classes * feat**2)
    return factor, turned.T


def turns(size, step):
    return [(i, (i + step) % size) for i in range(size)]


def passed_on(blocks, axis):
    size = lax.axis_size(axis)
    return [lax.ppermute(block, axis, turns(size, d)) for block in blocks for d in range(1, size)]


def crossed(blocks):
    return list(zip(*[passed_on(halves, "cls") for halves in zip(*blocks)]))


def sums_passed_on(gram, sums):
    size = lax.axis_size("cls")
    return passed_on([gram], "cls"), [lax.ppermute(sums[d], "cls", turns(size, d)) for d in range(1, size)]


def gathered_sums(block, sums_of):
    size = lax.axis_size("img")
    ring, far, sums = list(block), [passed_on([half], "sub") for half in block], None
    first = far[1]
    next_ring = [lax.ppermute(half, "img", turns(size, 1)) for half in ring]
    came = [tuple(block)]
    for step in range(1, size):
        last, swapped, passed = step == size - 1, [None, None], [None, None]
        for h in range(2):
            tied = (next_ring[h], far[h], sums if h else None)
            next_ring[h], far[h], kept = lax.optimization_barrier(tied)
            if step == 1 and h:
                first = far[h]
            sums = kept if h else sums
            if not last:
                passed[h] = lax.ppermute(next_ring[h], "img", turns(size, 1))
            if last and h:
                swapped[h] = [lax.ppermute(half, "img", turns(size, -1)) for half in first]
            else:
                swapped[h] = passed_on([next_ring[h]], "sub")
        came += [tuple(next_ring)] + list(zip(*far))
        sums = sums_of(sums, came)
        came, next_ring, far = [], passed, swapped
    far, sums = lax.optimization_barrier((far, sums))
    late = list(zip(*far))
    gram, *sums = sums
    grams, others = sums_passed_on(gram, sums)
    return [gram] + grams, [sums[0]] + others, late + crossed(late)


def shards(images, labels, seeds):
    count = images.shape[0]
    feat = 4 * seeds.shape[0]
    parts = lax.axis_size("cls")
    members = math.prod(lax.axis_size(axis) for axis in ("img", "sub", "cls"))
    ridge = RIDGE * count * members
    classes = CLASSES // parts
    padded = -(-classes // BLOCK) * BLOCK
    starts = classes * ((lax.axis_index("cls") + jnp.arange(parts, dtype=jnp.int32)) % parts)
    block = panel_block(images, labels, seeds)

    def sums_of(so_far, blocks):
        return panel_sums(so_far, blocks, starts, feat, padded, parts)

    if members <= MOST_BLOCKS:
        grams, sums, late = gathered_sums(block, sums_of)
    else:
        gram, *sums = lax.psum(tuple(sums_of(None, [block])), ("img", "sub"))
        grams, others = sums_passed_on(gram, sums)
        grams, sums, late = [gram] + grams, [sums[0]] + others, []
    return factor_and_solve(grams, sums, late, starts, ridge, feat, classes)


def solution(mesh):
    placed = (P(("grp", "img", "sub", "cls"), None), P(("grp", "img", "sub", "cls")), P())
    return jax.shard_map(
        shards,
        mesh=mesh,
        in_specs=placed,
        out_specs=(P("grp", None), P("grp", "cls")),
        check_vma=False,
    )
```

```python
import math

import jax
import jax.numpy as jnp
from jax import lax
from jax.experimental import pallas as pl
from jax.experimental.pallas import tpu as pltpu
from jax.sharding import PartitionSpec as P

CLASSES = 1000
CHANNELS, SIDE, KERNEL, OUT, POOL = 3, 32, 6, 14, 7
MODULUS = 46337
RIDGE = 0.001
BLOCK = 128
HIGHEST = lax.Precision.HIGHEST
ROWS = (((0,), (0,)), ((), ()))
LANES = (((1,), (1,)), ((), ()))
VMEM_BYTES = 48 * 2**20
MOST_BLOCKS = 16
STRIDE = 8
F32, BF16 = jnp.float32, jnp.bfloat16


def call(kernel, operands, outs, scratch=(), scalars=0, flops=0, aliases=None):
    spaces = [pltpu.SMEM] * scalars + [pltpu.VMEM] * (len(operands) - scalars)
    moved = 4 * sum(math.prod(shape) for shape in outs) + sum(o.size * o.dtype.itemsize for o in operands)
    return pl.pallas_call(
        kernel,
        out_shape=[jax.ShapeDtypeStruct(shape, F32) for shape in outs],
        in_specs=[pl.BlockSpec(memory_space=space) for space in spaces],
        out_specs=[pl.BlockSpec(memory_space=pltpu.VMEM)] * len(outs),
        scratch_shapes=[pltpu.VMEM(shape, dtype) for shape, dtype in scratch],
        input_output_aliases=aliases or {},
        cost_estimate=pl.CostEstimate(flops=flops, bytes_accessed=moved, transcendentals=0),
        compiler_params=pltpu.CompilerParams(vmem_limit_bytes=VMEM_BYTES),
    )(*operands)


def residue(x):
    quotient = jnp.floor(x.astype(F32) * (1.0 / MODULUS)).astype(jnp.int32)
    rest = x - quotient * MODULUS
    rest = jnp.where(rest < 0, rest + MODULUS, rest)
    return jnp.where(rest >= MODULUS, rest - MODULUS, rest)


def filter_values(seeds, taps):
    index = lax.broadcasted_iota(jnp.int32, (BLOCK, seeds.shape[1]), 0)
    seed = jnp.broadcast_to(seeds, index.shape)
    first = residue(seed * 7919 + index * 104729)
    second = residue(first * first + seed)
    values = (second.astype(F32) / 46337.0 - 0.5) * math.sqrt(12.0 / 108.0)
    return jnp.where(index < taps, values, 0.0).astype(BF16)


def features_kernel(seeds_ref, labels_ref, image_ref, top_ref, bottom_ref, shifted, bank, pools):
    filters, (images, pixels) = seeds_ref.shape[1], image_ref.shape
    plane, window, half = SIDE * SIDE, 2 * BLOCK, BLOCK // 2
    taps = CHANNELS * KERNEL * KERNEL
    values = filter_values(seeds_ref[...], taps)
    tap = lax.broadcasted_iota(jnp.int32, (BLOCK, CHANNELS * window), 0)
    at = lax.broadcasted_iota(jnp.int32, (BLOCK, CHANNELS * window), 1)
    channel, row, column = at // window, (at % window) // SIDE, at % SIDE
    chosen = (tap == (channel * KERNEL + row) * KERNEL + column) & (row < KERNEL) & (column < KERNEL)
    spread = lax.dot_general(values, jnp.where(chosen, 1.0, 0.0).astype(BF16), ROWS, preferred_element_type=F32)
    for j in range(OUT):
        for t in range(0, CHANNELS * window, BLOCK):
            tile = spread[:, t : t + BLOCK]
            if j:
                tile = pltpu.roll(tile, 2 * j, 1)
            bank[j * filters : (j + 1) * filters, t : t + BLOCK] = tile.astype(BF16)
    shifted[:, : pixels - BLOCK] = image_ref[:, half : pixels - half]
    shifted[:, pixels - BLOCK :] = jnp.concatenate(
        [image_ref[:, pixels - half :], jnp.zeros((images, half), BF16)], axis=1
    )
    pools[...] = jnp.zeros_like(pools)

    def windows(ref, m):
        starts = [plane * c + BLOCK * m for c in range(CHANNELS)]
        return jnp.concatenate([ref[:, s : s + window] for s in starts], axis=1)

    for m in range(OUT // 2):
        both = jnp.concatenate([windows(image_ref, m), windows(shifted, m)], axis=0)
        for q in range(2):
            part = bank[POOL * q * filters : POOL * (q + 1) * filters, :]
            active = jnp.maximum(lax.dot_general(part, both, LANES, preferred_element_type=F32), 0.0)
            total = active[:filters]
            for j in range(1, POOL):
                total = total + active[j * filters : (j + 1) * filters]
            pools[2 * (2 * m // POOL) + q] += total[:, :images]
            pools[2 * ((2 * m + 1) // POOL) + q] += total[:, images:]
    for n, ref in enumerate((top_ref, bottom_ref)):
        some = slice(n * filters // 2, (n + 1) * filters // 2)
        for w in range(4):
            ref[pl.ds(w, filters // 2, stride=4), :] = pools[w, some] * (1.0 / (POOL * POOL))
    bottom_ref[2 * filters :, :] = jnp.broadcast_to(labels_ref[...].astype(F32), (8, images))


def panel_block(images, labels, seeds):
    count, pixels = images.shape
    filters = seeds.shape[0]
    width = CHANNELS * 2 * BLOCK
    return call(
        features_kernel,
        [seeds[None], labels[None], images],
        [(2 * filters, count), (2 * filters + 8, count)],
        [((count, pixels), BF16), ((OUT * filters, width), BF16), ((4, filters, count), F32)],
        flops=2 * OUT * OUT * filters * width * count,
    )


def pieces(x):
    top = x.astype(BF16)
    rest = x - top.astype(F32)
    middle = rest.astype(BF16)
    return top, middle, (rest - middle.astype(F32)).astype(BF16)


def long_dot(one, two, dims):
    (left,), (right,) = dims
    a, b, c = one
    d, e, f = two
    return lax.dot_general(
        jnp.concatenate([a, a, b, a, b, c], axis=left),
        jnp.concatenate([d, e, d, f, e, d], axis=right),
        (dims, ((), ())),
        preferred_element_type=F32,
    )


def lane_copies(tile, lane):
    return jnp.broadcast_to(tile[:, lane : lane + 1], (8, BLOCK))


def row_copies(tile, row):
    return jnp.broadcast_to(tile[row : row + 1, :], (8, BLOCK))


def factor_block(tiles):
    lane = lax.broadcasted_iota(jnp.int32, (8, BLOCK), 1)
    row = lax.broadcasted_iota(jnp.int32, (8, BLOCK), 0)
    count = len(tiles)
    left = list(tiles)
    right = [jnp.where(lane == row + 8 * g, 1.0, 0.0) for g in range(count)]
    upper, inverse, raw = [], [], []
    own = [lane_copies(left[0], j) for j in range(8)]
    for p in range(count):
        top, bottom, scale = left[p], right[p], None
        stop = min(count, (p // STRIDE + 1) * STRIDE)
        cols = {g: [lane_copies(left[g], 8 * p + j) for j in range(8)] for g in range(p + 1, stop)}
        coming = [lane_copies(left[p + 1], 8 * p + 8 + j) for j in range(8)] if p + 1 < stop else []
        for j in range(8):
            pivot = row_copies(own[j], j)
            r = 1.0 / pivot
            for i in range(j + 1, 8):
                across = row_copies(own[i], j)
                t = across * r
                own[i] = own[i] - (own[j] * across) * r
                for g in cols:
                    cols[g][i] = cols[g][i] - cols[g][j] * t
            below = jnp.where(row > j, own[j], 0.0)
            top_row = row_copies(top, j) * r
            bottom_row = row_copies(bottom, j) * r
            top = top - below * top_row
            bottom = bottom - below * bottom_row
            for g in cols:
                left[g] = left[g] - cols[g][j] * top_row
                right[g] = right[g] - cols[g][j] * bottom_row
            if coming:
                edge = cols[p + 1][j]
                scaled = edge * r
                for c in range(8):
                    coming[c] = coming[c] - edge * row_copies(scaled, c)
            root = lax.rsqrt(pivot)
            scale = root if j == 0 else jnp.where(row == j, root, scale)
        raw.append(top * scale)
        upper.append(jnp.where(lane >= row + 8 * p, raw[p], 0.0))
        inverse.append(bottom * scale)
        if p + 1 == stop < count:
            done = slice(stop - STRIDE, stop)
            one = jnp.concatenate(raw[done], axis=0)
            both = jnp.concatenate([one, jnp.concatenate(inverse[done], axis=0)], axis=1)
            change = long_dot(pieces(one), pieces(both), ((0,), (0,)))
            for g in range(stop, count):
                left[g] = left[g] - change[8 * g : 8 * g + 8, :BLOCK]
                right[g] = right[g] - change[8 * g : 8 * g + 8, BLOCK:]
            coming = [lane_copies(left[stop], 8 * stop + j) for j in range(8)]
        own = coming
    return upper, inverse


def slots(feat):
    blocks = feat // BLOCK
    pairs = [(i, j) for i in range(blocks) for j in range(i, blocks)]
    return {pair: slice(n * BLOCK, (n + 1) * BLOCK) for n, pair in enumerate(pairs)}


def product(ones, twos):
    one, two = jnp.concatenate(ones, axis=1), jnp.concatenate(twos, axis=1)
    return lax.dot_general(one, two, LANES, preferred_element_type=F32)


def in_pairs(refs):
    return list(zip(refs[::2], refs[1::2]))


def split(block_refs, high, low):
    half, width = high.shape[0] // 2, block_refs[0][0].shape[1]
    for n, refs in enumerate(block_refs):
        at = slice(n * width, (n + 1) * width)
        for h, ref in enumerate(refs):
            rows = slice(h * half, (h + 1) * half)
            whole = ref[:half, :]
            top = whole.astype(BF16)
            high[rows, at] = top
            low[rows, at] = (whole - top.astype(F32)).astype(BF16)


def add_gram(so_far, gram_ref, high, low):
    feat = high.shape[0]
    place = slots(feat)
    for i in range(feat // BLOCK):
        at = slice(i * BLOCK, (i + 1) * BLOCK)
        one, two, rest = high[at, :], low[at, :], slice(i * BLOCK, feat)
        total = product([one, one, two, two], [high[rest, :], low[rest, :], high[rest, :], low[rest, :]])
        for j in range(i, feat // BLOCK):
            tile = total[:, (j - i) * BLOCK : (j - i + 1) * BLOCK]
            gram_ref[place[i, j], :] = tile if so_far is None else so_far[place[i, j], :] + tile


def add_label_sums(starts_ref, block_refs, so_far, sums_refs, high, low, marks):
    half, width = high.shape[0] // 2, block_refs[0][0].shape[1]
    class_row = lax.broadcasted_iota(jnp.int32, (marks.shape[0], width), 0)
    for d, sums_ref in enumerate(sums_refs):
        for n, (_, ref) in enumerate(block_refs):
            label = ref[half : half + 1, :].astype(jnp.int32) - starts_ref[d]
            marks[:, n * width : (n + 1) * width] = jnp.where(class_row == label, 1.0, 0.0).astype(BF16)
        total = product([marks[...], marks[...]], [high[...], low[...]])
        sums_ref[...] = total if so_far is None else so_far[d][...] + total


def sums_kernel(blocks, carried, starts_ref, *refs):
    so_far, block_refs, refs = refs[:carried], in_pairs(refs[carried : carried + 2 * blocks]), refs[carried + 2 * blocks :]
    gram_ref, sums_refs, (high, low, marks) = refs[0], refs[1:-3], refs[-3:]
    split(block_refs, high, low)
    add_gram(so_far[0] if carried else None, gram_ref, high, low)
    add_label_sums(starts_ref, block_refs, so_far[1:] or None, sums_refs, high, low, marks)


def panel_scratch(blocks, feat, classes):
    width = sum(block[0].shape[1] for block in blocks)
    return [((feat, width), BF16), ((feat, width), BF16), ((classes, width), BF16)]


def panel_sums(so_far, blocks, starts, feat, classes, parts):
    width = sum(block[0].shape[1] for block in blocks)
    packed = (len(slots(feat)) * BLOCK, BLOCK)
    carried = list(so_far or [])
    kernel = lambda *refs: sums_kernel(len(blocks), len(carried), *refs)
    aliases = {1 + d: d for d in range(len(carried))}
    flops = 8 * width * math.prod(packed) + 4 * parts * width * classes * feat
    outs = [packed] + [(classes, feat)] * parts
    operands = [starts] + carried + [half for block in blocks for half in block]
    return call(kernel, operands, outs, panel_scratch(blocks, feat, classes), 1, flops, aliases)


def solve_kernel(ridge, given, late, starts_ref, *refs):
    gram_refs, sums_refs, refs = refs[:given], refs[given : 2 * given], refs[2 * given :]
    block_refs, (factor_ref, turned_ref, gram, sums, inverse) = in_pairs(refs[: 2 * late]), refs[2 * late :][:5]
    sources = list(gram_refs)
    if late:
        packed, high, low, marks = refs[-4:]
        split(block_refs, high, low)
        add_gram(None, packed, high, low)
        add_label_sums(starts_ref, block_refs, None, [sums], high, low, marks)
        sources.append(packed)
    else:
        sums[...] = jnp.zeros_like(sums)
    for ref in sums_refs:
        sums[...] += ref[...]
    feat = gram.shape[0]
    for (i, j), at in slots(feat).items():
        gram[i * BLOCK : (i + 1) * BLOCK, j * BLOCK : (j + 1) * BLOCK] = sum(ref[at, :] for ref in sources)
    factor_ref[...] = jnp.zeros_like(factor_ref)
    lane = lax.broadcasted_iota(jnp.int32, (8, BLOCK), 1)
    row = lax.broadcasted_iota(jnp.int32, (8, BLOCK), 0)

    def turn(at):
        turned = lax.dot_general(sums[:, at], inverse[...], LANES, precision=HIGHEST, preferred_element_type=F32)
        turned_ref[:, at] = turned[: turned_ref.shape[0], :]
        return turned

    for start in range(0, feat, BLOCK):
        at, rest = slice(start, start + BLOCK), start + BLOCK
        if start:
            before = slice(start - BLOCK, start)
            taken = jnp.dot(turn(before), factor_ref[before, start:], precision=HIGHEST, preferred_element_type=F32)
            sums[:, start:] -= taken
        tiles = []
        for g in range(BLOCK // 8):
            tile = gram[start + 8 * g : start + 8 * g + 8, at]
            tiles.append(tile + jnp.where(lane == row + 8 * g, ridge, 0.0))
        upper, inverted = factor_block(tiles)
        for g in range(BLOCK // 8):
            factor_ref[start + 8 * g : start + 8 * g + 8, at] = upper[g]
            inverse[8 * g : 8 * g + 8, :] = inverted[g]
        parts, turner = [], pieces(inverse[...])
        for i in range(rest, feat, BLOCK):
            here = slice(i, i + BLOCK)
            across = long_dot(turner, pieces(gram[at, here]), ((1,), (0,)))
            factor_ref[at, here] = across
            parts.append(pieces(across))
            for n, part in enumerate(parts):
                there = slice(rest + n * BLOCK, rest + (n + 1) * BLOCK)
                gram[there, here] -= long_dot(part, parts[-1], ((0,), (0,)))
    turn(slice(feat - BLOCK, feat))


def factor_and_solve(grams, sums, late, starts, ridge, feat, classes):
    padded = sums[0].shape[0]
    kernel = lambda *refs: solve_kernel(ridge, len(grams), len(late), *refs)
    scratch = [((feat, feat), F32), ((padded, feat), F32), ((BLOCK, BLOCK), F32)]
    if late:
        scratch += [(grams[0].shape, F32)] + panel_scratch(late, feat, padded)
    outs = [(feat, feat), (classes, feat)]
    factor, turned = call(kernel, [starts] + grams + sums + [half for block in late for half in block], outs, scratch, 1, 6 * classes * feat**2)
    return factor, turned.T


def turns(size, step):
    return [(i, (i + step) % size) for i in range(size)]


def passed_on(blocks, axis):
    size = lax.axis_size(axis)
    return [lax.ppermute(block, axis, turns(size, d)) for block in blocks for d in range(1, size)]


def crossed(blocks):
    return list(zip(*[passed_on(halves, "cls") for halves in zip(*blocks)]))


def sums_passed_on(gram, sums):
    size = lax.axis_size("cls")
    return passed_on([gram], "cls"), [lax.ppermute(sums[d], "cls", turns(size, d)) for d in range(1, size)]


def gathered_sums(block, sums_of):
    size = lax.axis_size("img")
    ring, far, sums = list(block), [passed_on([half], "sub") for half in block], None
    first = far[1]
    next_ring = [lax.ppermute(half, "img", turns(size, 1)) for half in ring]
    came = [tuple(block)]
    for step in range(1, size):
        last, swapped, passed = step == size - 1, [None, None], [None, None]
        for h in range(2):
            tied = (next_ring[h], far[h], sums if h else None)
            next_ring[h], far[h], kept = lax.optimization_barrier(tied)
            if step == 1 and h:
                first = far[h]
            sums = kept if h else sums
            if not last:
                passed[h] = lax.ppermute(next_ring[h], "img", turns(size, 1))
            if last and h:
                swapped[h] = [lax.ppermute(half, "img", turns(size, -1)) for half in first]
            else:
                swapped[h] = passed_on([next_ring[h]], "sub")
        came += [tuple(next_ring)] + list(zip(*far))
        if step == 1 or last:
            sums, came = sums_of(sums, came), []
        next_ring, far = passed, swapped
    far, sums = lax.optimization_barrier((far, sums))
    late = list(zip(*far))
    gram, *sums = sums
    grams, others = sums_passed_on(gram, sums)
    return [gram] + grams, [sums[0]] + others, late + crossed(late)


def shards(images, labels, seeds):
    count = images.shape[0]
    feat = 4 * seeds.shape[0]
    parts = lax.axis_size("cls")
    members = math.prod(lax.axis_size(axis) for axis in ("img", "sub", "cls"))
    ridge = RIDGE * count * members
    classes = CLASSES // parts
    padded = -(-classes // BLOCK) * BLOCK
    starts = classes * ((lax.axis_index("cls") + jnp.arange(parts, dtype=jnp.int32)) % parts)
    block = panel_block(images, labels, seeds)

    def sums_of(so_far, blocks):
        return panel_sums(so_far, blocks, starts, feat, padded, parts)

    if members <= MOST_BLOCKS:
        grams, sums, late = gathered_sums(block, sums_of)
    else:
        gram, *sums = lax.psum(tuple(sums_of(None, [block])), ("img", "sub"))
        grams, others = sums_passed_on(gram, sums)
        grams, sums, late = [gram] + grams, [sums[0]] + others, []
    return factor_and_solve(grams, sums, late, starts, ridge, feat, classes)


def solution(mesh):
    placed = (P(("grp", "img", "sub", "cls"), None), P(("grp", "img", "sub", "cls")), P())
    return jax.shard_map(
        shards,
        mesh=mesh,
        in_specs=placed,
        out_specs=(P("grp", None), P("grp", "cls")),
        check_vma=False,
    )
```

```python
import math

import jax
import jax.numpy as jnp
from jax import lax
from jax.experimental import pallas as pl
from jax.experimental.pallas import tpu as pltpu
from jax.sharding import PartitionSpec as P

CLASSES = 1000
CHANNELS, SIDE, KERNEL, OUT, POOL = 3, 32, 6, 14, 7
MODULUS = 46337
RIDGE = 0.001
BLOCK = 128
HIGHEST = lax.Precision.HIGHEST
ROWS = (((0,), (0,)), ((), ()))
LANES = (((1,), (1,)), ((), ()))
VMEM_BYTES = 48 * 2**20
MOST_BLOCKS = 16
STRIDE = 8
F32, BF16 = jnp.float32, jnp.bfloat16


def call(kernel, operands, outs, scratch=(), scalars=0, flops=0, aliases=None):
    spaces = [pltpu.SMEM] * scalars + [pltpu.VMEM] * (len(operands) - scalars)
    moved = 4 * sum(math.prod(shape) for shape in outs) + sum(o.size * o.dtype.itemsize for o in operands)
    return pl.pallas_call(
        kernel,
        out_shape=[jax.ShapeDtypeStruct(shape, F32) for shape in outs],
        in_specs=[pl.BlockSpec(memory_space=space) for space in spaces],
        out_specs=[pl.BlockSpec(memory_space=pltpu.VMEM)] * len(outs),
        scratch_shapes=[pltpu.VMEM(shape, dtype) for shape, dtype in scratch],
        input_output_aliases=aliases or {},
        cost_estimate=pl.CostEstimate(flops=flops, bytes_accessed=moved, transcendentals=0),
        compiler_params=pltpu.CompilerParams(vmem_limit_bytes=VMEM_BYTES),
    )(*operands)


def residue(x):
    quotient = jnp.floor(x.astype(F32) * (1.0 / MODULUS)).astype(jnp.int32)
    rest = x - quotient * MODULUS
    rest = jnp.where(rest < 0, rest + MODULUS, rest)
    return jnp.where(rest >= MODULUS, rest - MODULUS, rest)


def filter_values(seeds, taps):
    index = lax.broadcasted_iota(jnp.int32, (BLOCK, seeds.shape[1]), 0)
    seed = jnp.broadcast_to(seeds, index.shape)
    first = residue(seed * 7919 + index * 104729)
    second = residue(first * first + seed)
    values = (second.astype(F32) / 46337.0 - 0.5) * math.sqrt(12.0 / 108.0)
    return jnp.where(index < taps, values, 0.0).astype(BF16)


def features_kernel(seeds_ref, labels_ref, image_ref, out_ref, shifted, bank, pools):
    filters, (images, pixels) = seeds_ref.shape[1], image_ref.shape
    plane, window, half = SIDE * SIDE, 2 * BLOCK, BLOCK // 2
    taps = CHANNELS * KERNEL * KERNEL
    values = filter_values(seeds_ref[...], taps)
    tap = lax.broadcasted_iota(jnp.int32, (BLOCK, CHANNELS * window), 0)
    at = lax.broadcasted_iota(jnp.int32, (BLOCK, CHANNELS * window), 1)
    channel, row, column = at // window, (at % window) // SIDE, at % SIDE
    chosen = (tap == (channel * KERNEL + row) * KERNEL + column) & (row < KERNEL) & (column < KERNEL)
    spread = lax.dot_general(values, jnp.where(chosen, 1.0, 0.0).astype(BF16), ROWS, preferred_element_type=F32)
    for j in range(OUT):
        for t in range(0, CHANNELS * window, BLOCK):
            tile = spread[:, t : t + BLOCK]
            if j:
                tile = pltpu.roll(tile, 2 * j, 1)
            bank[j * filters : (j + 1) * filters, t : t + BLOCK] = tile.astype(BF16)
    shifted[:, : pixels - BLOCK] = image_ref[:, half : pixels - half]
    shifted[:, pixels - BLOCK :] = jnp.concatenate(
        [image_ref[:, pixels - half :], jnp.zeros((images, half), BF16)], axis=1
    )
    pools[...] = jnp.zeros_like(pools)

    def windows(ref, m):
        starts = [plane * c + BLOCK * m for c in range(CHANNELS)]
        return jnp.concatenate([ref[:, s : s + window] for s in starts], axis=1)

    for m in range(OUT // 2):
        both = jnp.concatenate([windows(image_ref, m), windows(shifted, m)], axis=0)
        active = jnp.maximum(lax.dot_general(bank[...], both, LANES, preferred_element_type=F32), 0.0)
        for q in range(2):
            total = active[POOL * q * filters : (POOL * q + 1) * filters]
            for j in range(POOL * q + 1, POOL * (q + 1)):
                total = total + active[j * filters : (j + 1) * filters]
            pools[2 * (2 * m // POOL) + q] += total[:, :images]
            pools[2 * ((2 * m + 1) // POOL) + q] += total[:, images:]
    for w in range(4):
        out_ref[pl.ds(w, filters, stride=4), :] = pools[w] * (1.0 / (POOL * POOL))
    if out_ref.shape[0] > 4 * filters:
        out_ref[4 * filters :, :] = jnp.broadcast_to(labels_ref[...].astype(F32), (8, images))


def panel_block(images, labels, seeds):
    count, pixels = images.shape
    filters = seeds.shape[0] // 2
    width = CHANNELS * 2 * BLOCK
    scratch = [((count, pixels), BF16), ((OUT * filters, width), BF16), ((4, filters, count), F32)]
    flops = 2 * OUT * OUT * filters * width * count
    halves, some = [], seeds[None, :filters]
    for n in range(2):
        outs = [(4 * filters + 8 * n, count)]
        halves += call(features_kernel, [some, labels[None], images], outs, scratch, flops=flops)
        if not n:
            halves[0], some = lax.optimization_barrier((halves[0], seeds[None, filters:]))
    return halves


def pieces(x):
    top = x.astype(BF16)
    rest = x - top.astype(F32)
    middle = rest.astype(BF16)
    return top, middle, (rest - middle.astype(F32)).astype(BF16)


def long_dot(one, two, dims):
    (left,), (right,) = dims
    a, b, c = one
    d, e, f = two
    return lax.dot_general(
        jnp.concatenate([a, a, b, a, b, c], axis=left),
        jnp.concatenate([d, e, d, f, e, d], axis=right),
        (dims, ((), ())),
        preferred_element_type=F32,
    )


def lane_copies(tile, lane):
    return jnp.broadcast_to(tile[:, lane : lane + 1], (8, BLOCK))


def row_copies(tile, row):
    return jnp.broadcast_to(tile[row : row + 1, :], (8, BLOCK))


def factor_block(tiles):
    lane = lax.broadcasted_iota(jnp.int32, (8, BLOCK), 1)
    row = lax.broadcasted_iota(jnp.int32, (8, BLOCK), 0)
    count = len(tiles)
    left = list(tiles)
    right = [jnp.where(lane == row + 8 * g, 1.0, 0.0) for g in range(count)]
    upper, inverse, raw = [], [], []
    own = [lane_copies(left[0], j) for j in range(8)]
    for p in range(count):
        top, bottom, scale = left[p], right[p], None
        stop = min(count, (p // STRIDE + 1) * STRIDE)
        cols = {g: [lane_copies(left[g], 8 * p + j) for j in range(8)] for g in range(p + 1, stop)}
        coming = [lane_copies(left[p + 1], 8 * p + 8 + j) for j in range(8)] if p + 1 < stop else []
        for j in range(8):
            pivot = row_copies(own[j], j)
            r = 1.0 / pivot
            for i in range(j + 1, 8):
                across = row_copies(own[i], j)
                t = across * r
                own[i] = own[i] - (own[j] * across) * r
                for g in cols:
                    cols[g][i] = cols[g][i] - cols[g][j] * t
            below = jnp.where(row > j, own[j], 0.0)
            top_row = row_copies(top, j) * r
            bottom_row = row_copies(bottom, j) * r
            top = top - below * top_row
            bottom = bottom - below * bottom_row
            for g in cols:
                left[g] = left[g] - cols[g][j] * top_row
                right[g] = right[g] - cols[g][j] * bottom_row
            if coming:
                edge = cols[p + 1][j]
                scaled = edge * r
                for c in range(8):
                    coming[c] = coming[c] - edge * row_copies(scaled, c)
            root = lax.rsqrt(pivot)
            scale = root if j == 0 else jnp.where(row == j, root, scale)
        raw.append(top * scale)
        upper.append(jnp.where(lane >= row + 8 * p, raw[p], 0.0))
        inverse.append(bottom * scale)
        if p + 1 == stop < count:
            done = slice(stop - STRIDE, stop)
            one = jnp.concatenate(raw[done], axis=0)
            both = jnp.concatenate([one, jnp.concatenate(inverse[done], axis=0)], axis=1)
            change = long_dot(pieces(one), pieces(both), ((0,), (0,)))
            for g in range(stop, count):
                left[g] = left[g] - change[8 * g : 8 * g + 8, :BLOCK]
                right[g] = right[g] - change[8 * g : 8 * g + 8, BLOCK:]
            coming = [lane_copies(left[stop], 8 * stop + j) for j in range(8)]
        own = coming
    return upper, inverse


def slots(feat):
    blocks = feat // BLOCK
    pairs = [(i, j) for i in range(blocks) for j in range(i, blocks)]
    return {pair: slice(n * BLOCK, (n + 1) * BLOCK) for n, pair in enumerate(pairs)}


def product(ones, twos):
    one, two = jnp.concatenate(ones, axis=1), jnp.concatenate(twos, axis=1)
    return lax.dot_general(one, two, LANES, preferred_element_type=F32)


def in_pairs(refs):
    return list(zip(refs[::2], refs[1::2]))


def split(block_refs, high, low):
    half, width = high.shape[0] // 2, block_refs[0][0].shape[1]
    for n, refs in enumerate(block_refs):
        at = slice(n * width, (n + 1) * width)
        for h, ref in enumerate(refs):
            rows = slice(h * half, (h + 1) * half)
            whole = ref[:half, :]
            top = whole.astype(BF16)
            high[rows, at] = top
            low[rows, at] = (whole - top.astype(F32)).astype(BF16)


def add_gram(so_far, gram_ref, high, low):
    feat = high.shape[0]
    place = slots(feat)
    for i in range(feat // BLOCK):
        at = slice(i * BLOCK, (i + 1) * BLOCK)
        one, two, rest = high[at, :], low[at, :], slice(i * BLOCK, feat)
        total = product([one, one, two, two], [high[rest, :], low[rest, :], high[rest, :], low[rest, :]])
        for j in range(i, feat // BLOCK):
            tile = total[:, (j - i) * BLOCK : (j - i + 1) * BLOCK]
            gram_ref[place[i, j], :] = tile if so_far is None else so_far[place[i, j], :] + tile


def add_label_sums(starts_ref, block_refs, so_far, sums_refs, high, low, marks):
    half, width = high.shape[0] // 2, block_refs[0][0].shape[1]
    class_row = lax.broadcasted_iota(jnp.int32, (marks.shape[0], width), 0)
    for d, sums_ref in enumerate(sums_refs):
        for n, (_, ref) in enumerate(block_refs):
            label = ref[half : half + 1, :].astype(jnp.int32) - starts_ref[d]
            marks[:, n * width : (n + 1) * width] = jnp.where(class_row == label, 1.0, 0.0).astype(BF16)
        total = product([marks[...], marks[...]], [high[...], low[...]])
        sums_ref[...] = total if so_far is None else so_far[d][...] + total


def sums_kernel(blocks, carried, starts_ref, *refs):
    so_far, block_refs, refs = refs[:carried], in_pairs(refs[carried : carried + 2 * blocks]), refs[carried + 2 * blocks :]
    gram_ref, sums_refs, (high, low, marks) = refs[0], refs[1:-3], refs[-3:]
    split(block_refs, high, low)
    add_gram(so_far[0] if carried else None, gram_ref, high, low)
    add_label_sums(starts_ref, block_refs, so_far[1:] or None, sums_refs, high, low, marks)


def panel_scratch(blocks, feat, classes):
    width = sum(block[0].shape[1] for block in blocks)
    return [((feat, width), BF16), ((feat, width), BF16), ((classes, width), BF16)]


def panel_sums(so_far, blocks, starts, feat, classes, parts):
    width = sum(block[0].shape[1] for block in blocks)
    packed = (len(slots(feat)) * BLOCK, BLOCK)
    carried = list(so_far or [])
    kernel = lambda *refs: sums_kernel(len(blocks), len(carried), *refs)
    aliases = {1 + d: d for d in range(len(carried))}
    flops = 8 * width * math.prod(packed) + 4 * parts * width * classes * feat
    outs = [packed] + [(classes, feat)] * parts
    operands = [starts] + carried + [half for block in blocks for half in block]
    return call(kernel, operands, outs, panel_scratch(blocks, feat, classes), 1, flops, aliases)


def solve_kernel(ridge, given, late, starts_ref, *refs):
    gram_refs, sums_refs, refs = refs[:given], refs[given : 2 * given], refs[2 * given :]
    block_refs, (factor_ref, turned_ref, gram, sums, inverse) = in_pairs(refs[: 2 * late]), refs[2 * late :][:5]
    sources = list(gram_refs)
    if late:
        packed, high, low, marks = refs[-4:]
        split(block_refs, high, low)
        add_gram(None, packed, high, low)
        add_label_sums(starts_ref, block_refs, None, [sums], high, low, marks)
        sources.append(packed)
    else:
        sums[...] = jnp.zeros_like(sums)
    for ref in sums_refs:
        sums[...] += ref[...]
    feat = gram.shape[0]
    for (i, j), at in slots(feat).items():
        gram[i * BLOCK : (i + 1) * BLOCK, j * BLOCK : (j + 1) * BLOCK] = sum(ref[at, :] for ref in sources)
    factor_ref[...] = jnp.zeros_like(factor_ref)
    lane = lax.broadcasted_iota(jnp.int32, (8, BLOCK), 1)
    row = lax.broadcasted_iota(jnp.int32, (8, BLOCK), 0)

    def turn(at):
        turned = lax.dot_general(sums[:, at], inverse[...], LANES, precision=HIGHEST, preferred_element_type=F32)
        turned_ref[:, at] = turned[: turned_ref.shape[0], :]
        return turned

    for start in range(0, feat, BLOCK):
        at, rest = slice(start, start + BLOCK), start + BLOCK
        if start:
            before = slice(start - BLOCK, start)
            taken = jnp.dot(turn(before), factor_ref[before, start:], precision=HIGHEST, preferred_element_type=F32)
            sums[:, start:] -= taken
        tiles = []
        for g in range(BLOCK // 8):
            tile = gram[start + 8 * g : start + 8 * g + 8, at]
            tiles.append(tile + jnp.where(lane == row + 8 * g, ridge, 0.0))
        upper, inverted = factor_block(tiles)
        for g in range(BLOCK // 8):
            factor_ref[start + 8 * g : start + 8 * g + 8, at] = upper[g]
            inverse[8 * g : 8 * g + 8, :] = inverted[g]
        parts, turner = [], pieces(inverse[...])
        for i in range(rest, feat, BLOCK):
            here = slice(i, i + BLOCK)
            across = long_dot(turner, pieces(gram[at, here]), ((1,), (0,)))
            factor_ref[at, here] = across
            parts.append(pieces(across))
            for n, part in enumerate(parts):
                there = slice(rest + n * BLOCK, rest + (n + 1) * BLOCK)
                gram[there, here] -= long_dot(part, parts[-1], ((0,), (0,)))
    turn(slice(feat - BLOCK, feat))


def factor_and_solve(grams, sums, late, starts, ridge, feat, classes):
    padded = sums[0].shape[0]
    kernel = lambda *refs: solve_kernel(ridge, len(grams), len(late), *refs)
    scratch = [((feat, feat), F32), ((padded, feat), F32), ((BLOCK, BLOCK), F32)]
    if late:
        scratch += [(grams[0].shape, F32)] + panel_scratch(late, feat, padded)
    outs = [(feat, feat), (classes, feat)]
    factor, turned = call(kernel, [starts] + grams + sums + [half for block in late for half in block], outs, scratch, 1, 6 * classes * feat**2)
    return factor, turned.T


def turns(size, step):
    return [(i, (i + step) % size) for i in range(size)]


def passed_on(blocks, axis):
    size = lax.axis_size(axis)
    return [lax.ppermute(block, axis, turns(size, d)) for block in blocks for d in range(1, size)]


def crossed(blocks):
    return list(zip(*[passed_on(halves, "cls") for halves in zip(*blocks)]))


def sums_passed_on(gram, sums):
    size = lax.axis_size("cls")
    return passed_on([gram], "cls"), [lax.ppermute(sums[d], "cls", turns(size, d)) for d in range(1, size)]


def gathered_sums(block, sums_of):
    size = lax.axis_size("img")
    far, next_ring, sums = [None, None], [None, None], None
    top, bottom = block
    for h in range(2):
        half = bottom if h else top
        far[h], next_ring[h] = passed_on([half], "sub"), lax.ppermute(half, "img", turns(size, 1))
        if not h:
            far[h], next_ring[h], bottom = lax.optimization_barrier((far[h], next_ring[h], bottom))
    came = [(top, bottom)]
    for step in range(1, size):
        last, swapped, passed = step == size - 1, [None, None], [None, None]
        for h in range(2):
            if step > 1 or h:
                tied = (next_ring[h], far[h], sums if h else None)
                next_ring[h], far[h], kept = lax.optimization_barrier(tied)
            if step == 1 and h:
                first = far[h]
            sums = kept if h else sums
            if not last:
                passed[h] = lax.ppermute(next_ring[h], "img", turns(size, 1))
            if last and h:
                swapped[h] = [lax.ppermute(half, "img", turns(size, -1)) for half in first]
            else:
                swapped[h] = passed_on([next_ring[h]], "sub")
        came += [tuple(next_ring)] + list(zip(*far))
        if step == 1 or last:
            sums, came = sums_of(sums, came), []
        next_ring, far = passed, swapped
    far, sums = lax.optimization_barrier((far, sums))
    late = list(zip(*far))
    gram, *sums = sums
    grams, others = sums_passed_on(gram, sums)
    return [gram] + grams, [sums[0]] + others, late + crossed(late)


def shards(images, labels, seeds):
    count = images.shape[0]
    feat = 4 * seeds.shape[0]
    parts = lax.axis_size("cls")
    members = math.prod(lax.axis_size(axis) for axis in ("img", "sub", "cls"))
    ridge = RIDGE * count * members
    classes = CLASSES // parts
    padded = -(-classes // BLOCK) * BLOCK
    starts = classes * ((lax.axis_index("cls") + jnp.arange(parts, dtype=jnp.int32)) % parts)
    block = panel_block(images, labels, seeds)

    def sums_of(so_far, blocks):
        return panel_sums(so_far, blocks, starts, feat, padded, parts)

    if members <= MOST_BLOCKS:
        grams, sums, late = gathered_sums(block, sums_of)
    else:
        gram, *sums = lax.psum(tuple(sums_of(None, [block])), ("img", "sub"))
        grams, others = sums_passed_on(gram, sums)
        grams, sums, late = [gram] + grams, [sums[0]] + others, []
    return factor_and_solve(grams, sums, late, starts, ridge, feat, classes)


def solution(mesh):
    placed = (P(("grp", "img", "sub", "cls"), None), P(("grp", "img", "sub", "cls")), P())
    return jax.shard_map(
        shards,
        mesh=mesh,
        in_specs=placed,
        out_specs=(P("grp", None), P("grp", "cls")),
        check_vma=False,
    )
```

```python
import math

import jax
import jax.numpy as jnp
from jax import lax
from jax.experimental import pallas as pl
from jax.experimental.pallas import tpu as pltpu
from jax.sharding import PartitionSpec as P

CLASSES = 1000
CHANNELS, SIDE, KERNEL, OUT, POOL = 3, 32, 6, 14, 7
MODULUS = 46337
RIDGE = 0.001
BLOCK = 128
HIGHEST = lax.Precision.HIGHEST
ROWS = (((0,), (0,)), ((), ()))
LANES = (((1,), (1,)), ((), ()))
VMEM_BYTES = 48 * 2**20
MOST_BLOCKS = 16
STRIDE = 8
F32, BF16 = jnp.float32, jnp.bfloat16


def call(kernel, operands, outs, scratch=(), scalars=0, flops=0, aliases=None):
    spaces = [pltpu.SMEM] * scalars + [pltpu.VMEM] * (len(operands) - scalars)
    moved = 4 * sum(math.prod(shape) for shape in outs) + sum(o.size * o.dtype.itemsize for o in operands)
    return pl.pallas_call(
        kernel,
        out_shape=[jax.ShapeDtypeStruct(shape, F32) for shape in outs],
        in_specs=[pl.BlockSpec(memory_space=space) for space in spaces],
        out_specs=[pl.BlockSpec(memory_space=pltpu.VMEM)] * len(outs),
        scratch_shapes=[pltpu.VMEM(shape, dtype) for shape, dtype in scratch],
        input_output_aliases=aliases or {},
        cost_estimate=pl.CostEstimate(flops=flops, bytes_accessed=moved, transcendentals=0),
        compiler_params=pltpu.CompilerParams(vmem_limit_bytes=VMEM_BYTES),
    )(*operands)


def residue(x):
    quotient = jnp.floor(x.astype(F32) * (1.0 / MODULUS)).astype(jnp.int32)
    rest = x - quotient * MODULUS
    rest = jnp.where(rest < 0, rest + MODULUS, rest)
    return jnp.where(rest >= MODULUS, rest - MODULUS, rest)


def filter_values(seeds, taps):
    index = lax.broadcasted_iota(jnp.int32, (BLOCK, seeds.shape[1]), 0)
    seed = jnp.broadcast_to(seeds, index.shape)
    first = residue(seed * 7919 + index * 104729)
    second = residue(first * first + seed)
    values = (second.astype(F32) / 46337.0 - 0.5) * math.sqrt(12.0 / 108.0)
    return jnp.where(index < taps, values, 0.0).astype(BF16)


def features_kernel(seeds_ref, labels_ref, image_ref, out_ref, shifted, bank, pools):
    filters, (images, pixels) = seeds_ref.shape[1], image_ref.shape
    plane, window, half = SIDE * SIDE, 2 * BLOCK, BLOCK // 2
    taps = CHANNELS * KERNEL * KERNEL
    values = filter_values(seeds_ref[...], taps)
    tap = lax.broadcasted_iota(jnp.int32, (BLOCK, CHANNELS * window), 0)
    at = lax.broadcasted_iota(jnp.int32, (BLOCK, CHANNELS * window), 1)
    channel, row, column = at // window, (at % window) // SIDE, at % SIDE
    chosen = (tap == (channel * KERNEL + row) * KERNEL + column) & (row < KERNEL) & (column < KERNEL)
    spread = lax.dot_general(values, jnp.where(chosen, 1.0, 0.0).astype(BF16), ROWS, preferred_element_type=F32)
    for j in range(OUT):
        for t in range(0, CHANNELS * window, BLOCK):
            tile = spread[:, t : t + BLOCK]
            if j:
                tile = pltpu.roll(tile, 2 * j, 1)
            bank[j * filters : (j + 1) * filters, t : t + BLOCK] = tile.astype(BF16)
    shifted[:, : pixels - BLOCK] = image_ref[:, half : pixels - half]
    shifted[:, pixels - BLOCK :] = jnp.concatenate(
        [image_ref[:, pixels - half :], jnp.zeros((images, half), BF16)], axis=1
    )
    pools[...] = jnp.zeros_like(pools)

    def windows(ref, m):
        starts = [plane * c + BLOCK * m for c in range(CHANNELS)]
        return jnp.concatenate([ref[:, s : s + window] for s in starts], axis=1)

    for m in range(OUT // 2):
        both = jnp.concatenate([windows(image_ref, m), windows(shifted, m)], axis=0)
        active = jnp.maximum(lax.dot_general(bank[...], both, LANES, preferred_element_type=F32), 0.0)
        for q in range(2):
            total = active[POOL * q * filters : (POOL * q + 1) * filters]
            for j in range(POOL * q + 1, POOL * (q + 1)):
                total = total + active[j * filters : (j + 1) * filters]
            pools[2 * (2 * m // POOL) + q] += total[:, :images]
            pools[2 * ((2 * m + 1) // POOL) + q] += total[:, images:]
    for w in range(4):
        out_ref[pl.ds(w, filters, stride=4), :] = pools[w] * (1.0 / (POOL * POOL))
    if out_ref.shape[0] > 4 * filters:
        out_ref[4 * filters :, :] = jnp.broadcast_to(labels_ref[...].astype(F32), (8, images))


def panel_block(images, labels, seeds):
    count, pixels = images.shape
    filters = seeds.shape[0] // 2
    width = CHANNELS * 2 * BLOCK
    scratch = [((count, pixels), BF16), ((OUT * filters, width), BF16), ((4, filters, count), F32)]
    flops = 2 * OUT * OUT * filters * width * count
    halves, some = [], seeds[None, :filters]
    for n in range(2):
        outs = [(4 * filters + 8 * n, count)]
        halves += call(features_kernel, [some, labels[None], images], outs, scratch, flops=flops)
        if not n:
            halves[0], some = lax.optimization_barrier((halves[0], seeds[None, filters:]))
    return halves


def pieces(x):
    top = x.astype(BF16)
    rest = x - top.astype(F32)
    middle = rest.astype(BF16)
    return top, middle, (rest - middle.astype(F32)).astype(BF16)


def long_dot(one, two, dims):
    (left,), (right,) = dims
    a, b, c = one
    d, e, f = two
    return lax.dot_general(
        jnp.concatenate([a, a, b, a, b, c], axis=left),
        jnp.concatenate([d, e, d, f, e, d], axis=right),
        (dims, ((), ())),
        preferred_element_type=F32,
    )


def lane_copies(tile, lane):
    return jnp.broadcast_to(tile[:, lane : lane + 1], (8, BLOCK))


def row_copies(tile, row):
    return jnp.broadcast_to(tile[row : row + 1, :], (8, BLOCK))


def factor_block(tiles):
    lane = lax.broadcasted_iota(jnp.int32, (8, BLOCK), 1)
    row = lax.broadcasted_iota(jnp.int32, (8, BLOCK), 0)
    count = len(tiles)
    left = list(tiles)
    right = [jnp.where(lane == row + 8 * g, 1.0, 0.0) for g in range(count)]
    upper, inverse, raw = [], [], []
    own = [lane_copies(left[0], j) for j in range(8)]
    for p in range(count):
        top, bottom, scale = left[p], right[p], None
        stop = min(count, (p // STRIDE + 1) * STRIDE)
        cols = {g: [lane_copies(left[g], 8 * p + j) for j in range(8)] for g in range(p + 1, stop)}
        coming = [lane_copies(left[p + 1], 8 * p + 8 + j) for j in range(8)] if p + 1 < stop else []
        for j in range(8):
            pivot = row_copies(own[j], j)
            r = 1.0 / pivot
            for i in range(j + 1, 8):
                across = row_copies(own[i], j)
                t = across * r
                own[i] = own[i] - (own[j] * across) * r
                for g in cols:
                    cols[g][i] = cols[g][i] - cols[g][j] * t
            below = jnp.where(row > j, own[j], 0.0)
            top_row = row_copies(top, j) * r
            bottom_row = row_copies(bottom, j) * r
            top = top - below * top_row
            bottom = bottom - below * bottom_row
            for g in cols:
                left[g] = left[g] - cols[g][j] * top_row
                right[g] = right[g] - cols[g][j] * bottom_row
            if coming:
                edge = cols[p + 1][j]
                scaled = edge * r
                for c in range(8):
                    coming[c] = coming[c] - edge * row_copies(scaled, c)
            root = lax.rsqrt(pivot)
            scale = root if j == 0 else jnp.where(row == j, root, scale)
        raw.append(top * scale)
        upper.append(jnp.where(lane >= row + 8 * p, raw[p], 0.0))
        inverse.append(bottom * scale)
        if p + 1 == stop < count:
            done = slice(stop - STRIDE, stop)
            one = jnp.concatenate(raw[done], axis=0)
            both = jnp.concatenate([one, jnp.concatenate(inverse[done], axis=0)], axis=1)
            change = long_dot(pieces(one), pieces(both), ((0,), (0,)))
            for g in range(stop, count):
                left[g] = left[g] - change[8 * g : 8 * g + 8, :BLOCK]
                right[g] = right[g] - change[8 * g : 8 * g + 8, BLOCK:]
            coming = [lane_copies(left[stop], 8 * stop + j) for j in range(8)]
        own = coming
    return upper, inverse


def slots(feat):
    blocks = feat // BLOCK
    pairs = [(i, j) for i in range(blocks) for j in range(i, blocks)]
    return {pair: slice(n * BLOCK, (n + 1) * BLOCK) for n, pair in enumerate(pairs)}


def product(ones, twos):
    one, two = jnp.concatenate(ones, axis=1), jnp.concatenate(twos, axis=1)
    return lax.dot_general(one, two, LANES, preferred_element_type=F32)


def in_pairs(refs):
    return list(zip(refs[::2], refs[1::2]))


def split(block_refs, high, low):
    half, width = high.shape[0] // 2, block_refs[0][0].shape[1]
    for n, refs in enumerate(block_refs):
        at = slice(n * width, (n + 1) * width)
        for h, ref in enumerate(refs):
            rows = slice(h * half, (h + 1) * half)
            whole = ref[:half, :]
            top = whole.astype(BF16)
            high[rows, at] = top
            low[rows, at] = (whole - top.astype(F32)).astype(BF16)


def add_gram(so_far, gram_ref, high, low):
    feat = high.shape[0]
    place = slots(feat)
    for i in range(feat // BLOCK):
        at = slice(i * BLOCK, (i + 1) * BLOCK)
        one, two, rest = high[at, :], low[at, :], slice(i * BLOCK, feat)
        total = product([one, one, two, two], [high[rest, :], low[rest, :], high[rest, :], low[rest, :]])
        for j in range(i, feat // BLOCK):
            tile = total[:, (j - i) * BLOCK : (j - i + 1) * BLOCK]
            gram_ref[place[i, j], :] = tile if so_far is None else so_far[place[i, j], :] + tile


def add_label_sums(starts_ref, block_refs, so_far, sums_refs, high, low, marks):
    half, width = high.shape[0] // 2, block_refs[0][0].shape[1]
    class_row = lax.broadcasted_iota(jnp.int32, (marks.shape[0], width), 0)
    for d, sums_ref in enumerate(sums_refs):
        for n, (_, ref) in enumerate(block_refs):
            label = ref[half : half + 1, :].astype(jnp.int32) - starts_ref[d]
            marks[:, n * width : (n + 1) * width] = jnp.where(class_row == label, 1.0, 0.0).astype(BF16)
        total = product([marks[...], marks[...]], [high[...], low[...]])
        sums_ref[...] = total if so_far is None else so_far[d][...] + total


def sums_kernel(blocks, carried, starts_ref, *refs):
    so_far, block_refs, refs = refs[:carried], in_pairs(refs[carried : carried + 2 * blocks]), refs[carried + 2 * blocks :]
    gram_ref, sums_refs, (high, low, marks) = refs[0], refs[1:-3], refs[-3:]
    split(block_refs, high, low)
    add_gram(so_far[0] if carried else None, gram_ref, high, low)
    add_label_sums(starts_ref, block_refs, so_far[1:] or None, sums_refs, high, low, marks)


def panel_scratch(blocks, feat, classes):
    width = sum(block[0].shape[1] for block in blocks)
    return [((feat, width), BF16), ((feat, width), BF16), ((classes, width), BF16)]


def panel_sums(so_far, blocks, starts, feat, classes, parts):
    width = sum(block[0].shape[1] for block in blocks)
    packed = (len(slots(feat)) * BLOCK, BLOCK)
    carried = list(so_far or [])
    kernel = lambda *refs: sums_kernel(len(blocks), len(carried), *refs)
    aliases = {1 + d: d for d in range(len(carried))}
    flops = 8 * width * math.prod(packed) + 4 * parts * width * classes * feat
    outs = [packed] + [(classes, feat)] * parts
    operands = [starts] + carried + [half for block in blocks for half in block]
    return call(kernel, operands, outs, panel_scratch(blocks, feat, classes), 1, flops, aliases)


def solve_kernel(ridge, given, late, starts_ref, *refs):
    gram_refs, sums_refs, refs = refs[:given], refs[given : 2 * given], refs[2 * given :]
    block_refs, (factor_ref, turned_ref, gram, sums, inverse) = in_pairs(refs[: 2 * late]), refs[2 * late :][:5]
    sources = list(gram_refs)
    if late:
        packed, high, low, marks = refs[-4:]
        split(block_refs, high, low)
        add_gram(None, packed, high, low)
        add_label_sums(starts_ref, block_refs, None, [sums], high, low, marks)
        sources.append(packed)
    else:
        sums[...] = jnp.zeros_like(sums)
    for ref in sums_refs:
        sums[...] += ref[...]
    feat = gram.shape[0]
    for (i, j), at in slots(feat).items():
        gram[i * BLOCK : (i + 1) * BLOCK, j * BLOCK : (j + 1) * BLOCK] = sum(ref[at, :] for ref in sources)
    factor_ref[...] = jnp.zeros_like(factor_ref)
    lane = lax.broadcasted_iota(jnp.int32, (8, BLOCK), 1)
    row = lax.broadcasted_iota(jnp.int32, (8, BLOCK), 0)

    def turn(at):
        turned = lax.dot_general(sums[:, at], inverse[...], LANES, precision=HIGHEST, preferred_element_type=F32)
        turned_ref[:, at] = turned[: turned_ref.shape[0], :]
        return turned

    for start in range(0, feat, BLOCK):
        at, rest = slice(start, start + BLOCK), start + BLOCK
        if start:
            before = slice(start - BLOCK, start)
            taken = jnp.dot(turn(before), factor_ref[before, start:], precision=HIGHEST, preferred_element_type=F32)
            sums[:, start:] -= taken
        tiles = []
        for g in range(BLOCK // 8):
            tile = gram[start + 8 * g : start + 8 * g + 8, at]
            tiles.append(tile + jnp.where(lane == row + 8 * g, ridge, 0.0))
        upper, inverted = factor_block(tiles)
        for g in range(BLOCK // 8):
            factor_ref[start + 8 * g : start + 8 * g + 8, at] = upper[g]
            inverse[8 * g : 8 * g + 8, :] = inverted[g]
        parts, turner = [], pieces(inverse[...])
        for i in range(rest, feat, BLOCK):
            here = slice(i, i + BLOCK)
            across = long_dot(turner, pieces(gram[at, here]), ((1,), (0,)))
            factor_ref[at, here] = across
            parts.append(pieces(across))
            for n, part in enumerate(parts):
                there = slice(rest + n * BLOCK, rest + (n + 1) * BLOCK)
                gram[there, here] -= long_dot(part, parts[-1], ((0,), (0,)))
    turn(slice(feat - BLOCK, feat))


def factor_and_solve(grams, sums, late, starts, ridge, feat, classes):
    padded = sums[0].shape[0]
    kernel = lambda *refs: solve_kernel(ridge, len(grams), len(late), *refs)
    scratch = [((feat, feat), F32), ((padded, feat), F32), ((BLOCK, BLOCK), F32)]
    if late:
        scratch += [(grams[0].shape, F32)] + panel_scratch(late, feat, padded)
    outs = [(feat, feat), (classes, feat)]
    factor, turned = call(kernel, [starts] + grams + sums + [half for block in late for half in block], outs, scratch, 1, 6 * classes * feat**2)
    return factor, turned.T


def turns(size, step):
    return [(i, (i + step) % size) for i in range(size)]


def passed_on(blocks, axis):
    size = lax.axis_size(axis)
    return [lax.ppermute(block, axis, turns(size, d)) for block in blocks for d in range(1, size)]


def sums_passed_on(gram, sums):
    size = lax.axis_size("cls")
    return passed_on([gram], "cls"), [lax.ppermute(sums[d], "cls", turns(size, d)) for d in range(1, size)]


def gathered_sums(block, sums_of):
    def moved(half):
        return lax.ppermute(half, "img", turns(size, 1)), passed_on([half], "sub")

    size = lax.axis_size("img")
    top, bottom = block
    ahead, bottom = lax.optimization_barrier((moved(top), bottom))
    behind, came, sums = moved(bottom), [(top, bottom)], None
    for phase in range(1, size):
        last = phase == size - 1
        coming = (None, passed_on([ahead[0]], "sub")) if last else moved(ahead[0])
        back = [lax.ppermute(half, "img", turns(size, -1)) for half in first] if last else None
        crossed = passed_on([ahead[0]] + ahead[1], "cls") if last else None
        if last or phase > 1:
            sums, came = sums_of(sums, came), []
        coming, behind, back, crossed, sums = lax.optimization_barrier((coming, behind, back, crossed, sums))
        if phase == 1:
            first = behind[1]
        came += [(ahead[0], behind[0])] + list(zip(ahead[1], behind[1]))
        if not last:
            ahead, behind = coming, moved(behind[0])
    gram, *sums = sums
    grams, others = sums_passed_on(gram, sums)
    crossed = list(zip(crossed, passed_on([behind[0]] + behind[1], "cls")))
    far = list(zip(coming[1], back))
    crossed += list(zip(passed_on(coming[1], "cls"), passed_on(back, "cls")))
    return [gram] + grams, [sums[0]] + others, came + far + crossed


def shards(images, labels, seeds):
    count = images.shape[0]
    feat = 4 * seeds.shape[0]
    parts = lax.axis_size("cls")
    members = math.prod(lax.axis_size(axis) for axis in ("img", "sub", "cls"))
    ridge = RIDGE * count * members
    classes = CLASSES // parts
    padded = -(-classes // BLOCK) * BLOCK
    starts = classes * ((lax.axis_index("cls") + jnp.arange(parts, dtype=jnp.int32)) % parts)
    block = panel_block(images, labels, seeds)

    def sums_of(so_far, blocks):
        return panel_sums(so_far, blocks, starts, feat, padded, parts)

    if members <= MOST_BLOCKS:
        grams, sums, late = gathered_sums(block, sums_of)
    else:
        gram, *sums = lax.psum(tuple(sums_of(None, [block])), ("img", "sub"))
        grams, others = sums_passed_on(gram, sums)
        grams, sums, late = [gram] + grams, [sums[0]] + others, []
    return factor_and_solve(grams, sums, late, starts, ridge, feat, classes)


def solution(mesh):
    placed = (P(("grp", "img", "sub", "cls"), None), P(("grp", "img", "sub", "cls")), P())
    return jax.shard_map(
        shards,
        mesh=mesh,
        in_specs=placed,
        out_specs=(P("grp", None), P("grp", "cls")),
        check_vma=False,
    )
```

```python
import functools
import math

import jax
import jax.numpy as jnp
from jax import lax
from jax.experimental import pallas as pl
from jax.experimental.pallas import tpu as pltpu
from jax.sharding import PartitionSpec as P

CLASSES = 1000
CHANNELS, SIDE, KERNEL, OUT, POOL = 3, 32, 6, 14, 7
MODULUS = 46337
RIDGE = 0.001
BLOCK = 128
HIGHEST = lax.Precision.HIGHEST
ROWS = (((0,), (0,)), ((), ()))
LANES = (((1,), (1,)), ((), ()))
VMEM_BYTES = 48 * 2**20
MOST_BLOCKS = 16
STRIDE = 8
F32, BF16 = jnp.float32, jnp.bfloat16


def call(kernel, operands, outs, scratch=(), scalars=0, flops=0, aliases=None):
    spaces = [pltpu.SMEM] * scalars + [pltpu.VMEM] * (len(operands) - scalars)
    moved = 4 * sum(math.prod(shape) for shape in outs) + sum(o.size * o.dtype.itemsize for o in operands)
    return pl.pallas_call(
        kernel,
        out_shape=[jax.ShapeDtypeStruct(shape, F32) for shape in outs],
        in_specs=[pl.BlockSpec(memory_space=space) for space in spaces],
        out_specs=[pl.BlockSpec(memory_space=pltpu.VMEM)] * len(outs),
        scratch_shapes=[pltpu.VMEM(shape, dtype) for shape, dtype in scratch],
        input_output_aliases=aliases or {},
        cost_estimate=pl.CostEstimate(flops=flops, bytes_accessed=moved, transcendentals=0),
        compiler_params=pltpu.CompilerParams(vmem_limit_bytes=VMEM_BYTES),
    )(*operands)


def residue(x):
    quotient = jnp.floor(x.astype(F32) * (1.0 / MODULUS)).astype(jnp.int32)
    rest = x - quotient * MODULUS
    rest = jnp.where(rest < 0, rest + MODULUS, rest)
    return jnp.where(rest >= MODULUS, rest - MODULUS, rest)


def filter_values(seeds, taps):
    index = lax.broadcasted_iota(jnp.int32, (BLOCK, seeds.shape[1]), 0)
    seed = jnp.broadcast_to(seeds, index.shape)
    first = residue(seed * 7919 + index * 104729)
    second = residue(first * first + seed)
    values = (second.astype(F32) / 46337.0 - 0.5) * math.sqrt(12.0 / 108.0)
    return jnp.where(index < taps, values, 0.0).astype(BF16)


def features_kernel(second, seeds_ref, image_ref, *refs):
    out_ref, shifted, bank, pools = refs[-4:]
    filters, (images, pixels) = pools.shape[1], image_ref.shape
    plane, window, half = SIDE * SIDE, 2 * BLOCK, BLOCK // 2
    taps = CHANNELS * KERNEL * KERNEL
    values = filter_values(seeds_ref[...], taps)
    tap = lax.broadcasted_iota(jnp.int32, (BLOCK, CHANNELS * window), 0)
    at = lax.broadcasted_iota(jnp.int32, (BLOCK, CHANNELS * window), 1)
    channel, row, column = at // window, (at % window) // SIDE, at % SIDE
    chosen = (tap == (channel * KERNEL + row) * KERNEL + column) & (row < KERNEL) & (column < KERNEL)
    spread = lax.dot_general(values, jnp.where(chosen, 1.0, 0.0).astype(BF16), ROWS, preferred_element_type=F32)
    for j in range(OUT):
        for t in range(0, CHANNELS * window, BLOCK):
            tile = spread[second * filters : (second + 1) * filters, t : t + BLOCK]
            if j:
                tile = pltpu.roll(tile, 2 * j, 1)
            bank[j * filters : (j + 1) * filters, t : t + BLOCK] = tile.astype(BF16)
    shifted[:, : pixels - BLOCK] = image_ref[:, half : pixels - half]
    shifted[:, pixels - BLOCK :] = jnp.concatenate(
        [image_ref[:, pixels - half :], jnp.zeros((images, half), BF16)], axis=1
    )
    pools[...] = jnp.zeros_like(pools)

    def windows(ref, m):
        starts = [plane * c + BLOCK * m for c in range(CHANNELS)]
        return jnp.concatenate([ref[:, s : s + window] for s in starts], axis=1)

    for m in range(OUT // 2):
        both = jnp.concatenate([windows(image_ref, m), windows(shifted, m)], axis=0)
        active = jnp.maximum(lax.dot_general(bank[...], both, LANES, preferred_element_type=F32), 0.0)
        for q in range(2):
            total = active[POOL * q * filters : (POOL * q + 1) * filters]
            for j in range(POOL * q + 1, POOL * (q + 1)):
                total = total + active[j * filters : (j + 1) * filters]
            pools[2 * (2 * m // POOL) + q] += total[:, :images]
            pools[2 * ((2 * m + 1) // POOL) + q] += total[:, images:]
    for w in range(4):
        out_ref[pl.ds(w, filters, stride=4), :] = pools[w] * (1.0 / (POOL * POOL))
    if second:
        out_ref[4 * filters :, :] = jnp.broadcast_to(refs[0][...].astype(F32), (8, images))


def panel_block(images, labels, seeds):
    count, pixels = images.shape
    filters = seeds.shape[0] // 2
    width = CHANNELS * 2 * BLOCK
    scratch = [((count, pixels), BF16), ((OUT * filters, width), BF16), ((4, filters, count), F32)]
    flops = 2 * OUT * OUT * filters * width * count
    halves, seeds = [], seeds[None]
    for n in range(2):
        kernel = functools.partial(features_kernel, n)
        operands = [seeds, images] + [labels[None]] * n
        halves += call(kernel, operands, [(4 * filters + 8 * n, count)], scratch, flops=flops)
        if not n:
            halves[0], seeds = lax.optimization_barrier((halves[0], seeds))
    return halves


def pieces(x):
    top = x.astype(BF16)
    rest = x - top.astype(F32)
    middle = rest.astype(BF16)
    return top, middle, (rest - middle.astype(F32)).astype(BF16)


def long_dot(one, two, dims):
    (left,), (right,) = dims
    a, b, c = one
    d, e, f = two
    return lax.dot_general(
        jnp.concatenate([a, a, b, a, b, c], axis=left),
        jnp.concatenate([d, e, d, f, e, d], axis=right),
        (dims, ((), ())),
        preferred_element_type=F32,
    )


def lane_copies(tile, lane):
    return jnp.broadcast_to(tile[:, lane : lane + 1], (8, BLOCK))


def row_copies(tile, row):
    return jnp.broadcast_to(tile[row : row + 1, :], (8, BLOCK))


def factor_block(tiles):
    lane = lax.broadcasted_iota(jnp.int32, (8, BLOCK), 1)
    row = lax.broadcasted_iota(jnp.int32, (8, BLOCK), 0)
    count = len(tiles)
    left = list(tiles)
    right = [jnp.where(lane == row + 8 * g, 1.0, 0.0) for g in range(count)]
    upper, inverse, raw = [], [], []
    own = [lane_copies(left[0], j) for j in range(8)]
    for p in range(count):
        top, bottom, scale = left[p], right[p], None
        stop = min(count, (p // STRIDE + 1) * STRIDE)
        cols = {g: [lane_copies(left[g], 8 * p + j) for j in range(8)] for g in range(p + 1, stop)}
        coming = [lane_copies(left[p + 1], 8 * p + 8 + j) for j in range(8)] if p + 1 < stop else []
        for j in range(8):
            pivot = row_copies(own[j], j)
            r = 1.0 / pivot
            for i in range(j + 1, 8):
                across = row_copies(own[i], j)
                t = across * r
                own[i] = own[i] - (own[j] * across) * r
                for g in cols:
                    cols[g][i] = cols[g][i] - cols[g][j] * t
            below = jnp.where(row > j, own[j], 0.0)
            top_row = row_copies(top, j) * r
            bottom_row = row_copies(bottom, j) * r
            top = top - below * top_row
            bottom = bottom - below * bottom_row
            for g in cols:
                left[g] = left[g] - cols[g][j] * top_row
                right[g] = right[g] - cols[g][j] * bottom_row
            if coming:
                edge = cols[p + 1][j]
                scaled = edge * r
                for c in range(8):
                    coming[c] = coming[c] - edge * row_copies(scaled, c)
            root = lax.rsqrt(pivot)
            scale = root if j == 0 else jnp.where(row == j, root, scale)
        raw.append(top * scale)
        upper.append(jnp.where(lane >= row + 8 * p, raw[p], 0.0))
        inverse.append(bottom * scale)
        if p + 1 == stop < count:
            done = slice(stop - STRIDE, stop)
            one = jnp.concatenate(raw[done], axis=0)
            both = jnp.concatenate([one, jnp.concatenate(inverse[done], axis=0)], axis=1)
            change = long_dot(pieces(one), pieces(both), ((0,), (0,)))
            for g in range(stop, count):
                left[g] = left[g] - change[8 * g : 8 * g + 8, :BLOCK]
                right[g] = right[g] - change[8 * g : 8 * g + 8, BLOCK:]
            coming = [lane_copies(left[stop], 8 * stop + j) for j in range(8)]
        own = coming
    return upper, inverse


def slots(feat):
    blocks = feat // BLOCK
    pairs = [(i, j) for i in range(blocks) for j in range(i, blocks)]
    return {pair: slice(n * BLOCK, (n + 1) * BLOCK) for n, pair in enumerate(pairs)}


def product(ones, twos):
    one, two = jnp.concatenate(ones, axis=1), jnp.concatenate(twos, axis=1)
    return lax.dot_general(one, two, LANES, preferred_element_type=F32)


def in_pairs(refs):
    return list(zip(refs[::2], refs[1::2]))


def split(block_refs, high, low):
    half, width = high.shape[0] // 2, block_refs[0][0].shape[1]
    for n, refs in enumerate(block_refs):
        at = slice(n * width, (n + 1) * width)
        for h, ref in enumerate(refs):
            rows = slice(h * half, (h + 1) * half)
            whole = ref[:half, :]
            top = whole.astype(BF16)
            high[rows, at] = top
            low[rows, at] = (whole - top.astype(F32)).astype(BF16)


def gram_row(i, high, low):
    feat = high.shape[0]
    at, rest = slice(i * BLOCK, (i + 1) * BLOCK), slice(i * BLOCK, feat)
    one, two = high[at, :], low[at, :]
    return product([one, one, two, two], [high[rest, :], low[rest, :], high[rest, :], low[rest, :]])


def add_gram(so_far, gram_ref, high, low):
    feat = high.shape[0]
    place = slots(feat)
    for i in range(feat // BLOCK):
        total = gram_row(i, high, low)
        for j in range(i, feat // BLOCK):
            tile = total[:, (j - i) * BLOCK : (j - i + 1) * BLOCK]
            gram_ref[place[i, j], :] = tile if so_far is None else so_far[place[i, j], :] + tile


def add_label_sums(starts_ref, block_refs, so_far, sums_refs, high, low, marks):
    half, width = high.shape[0] // 2, block_refs[0][0].shape[1]
    class_row = lax.broadcasted_iota(jnp.int32, (marks.shape[0], width), 0)
    for d, sums_ref in enumerate(sums_refs):
        for n, (_, ref) in enumerate(block_refs):
            label = ref[half : half + 1, :].astype(jnp.int32) - starts_ref[d]
            marks[:, n * width : (n + 1) * width] = jnp.where(class_row == label, 1.0, 0.0).astype(BF16)
        total = product([marks[...], marks[...]], [high[...], low[...]])
        sums_ref[...] = total if so_far is None else so_far[d][...] + total


def sums_kernel(blocks, carried, starts_ref, *refs):
    so_far, block_refs, refs = refs[:carried], in_pairs(refs[carried : carried + 2 * blocks]), refs[carried + 2 * blocks :]
    gram_ref, sums_refs, (high, low, marks) = refs[0], refs[1:-3], refs[-3:]
    split(block_refs, high, low)
    add_gram(so_far[0] if carried else None, gram_ref, high, low)
    add_label_sums(starts_ref, block_refs, so_far[1:] or None, sums_refs, high, low, marks)


def panel_scratch(blocks, feat, classes):
    width = sum(block[0].shape[1] for block in blocks)
    return [((feat, width), BF16), ((feat, width), BF16), ((classes, width), BF16)]


def panel_sums(so_far, blocks, starts, feat, classes, parts):
    width = sum(block[0].shape[1] for block in blocks)
    packed = (len(slots(feat)) * BLOCK, BLOCK)
    carried = list(so_far or [])
    kernel = lambda *refs: sums_kernel(len(blocks), len(carried), *refs)
    aliases = {1 + d: d for d in range(len(carried))}
    flops = 8 * width * math.prod(packed) + 4 * parts * width * classes * feat
    outs = [packed] + [(classes, feat)] * parts
    operands = [starts] + carried + [half for block in blocks for half in block]
    return call(kernel, operands, outs, panel_scratch(blocks, feat, classes), 1, flops, aliases)


def solve_kernel(ridge, given, late, starts_ref, *refs):
    gram_refs, sums_refs, refs = refs[:given], refs[given : 2 * given], refs[2 * given :]
    block_refs, (factor_ref, turned_ref, gram, sums, inverse) = in_pairs(refs[: 2 * late]), refs[2 * late :][:5]
    feat = gram.shape[0]
    place = slots(feat)
    if late:
        high, low, marks = refs[-3:]
        split(block_refs, high, low)

    def gather_row(i):
        row = gram_row(i, high, low) if late else None
        for j in range(i, feat // BLOCK):
            tile = sum(ref[place[i, j], :] for ref in gram_refs)
            if late:
                tile = tile + row[:, (j - i) * BLOCK : (j - i + 1) * BLOCK]
            gram[i * BLOCK : (i + 1) * BLOCK, j * BLOCK : (j + 1) * BLOCK] = tile

    def gather_sums():
        total = sum(ref[...] for ref in sums_refs)
        if late:
            add_label_sums(starts_ref, block_refs, [total], [sums], high, low, marks)
        else:
            sums[...] = total

    gather_row(0)
    factor_ref[...] = jnp.zeros_like(factor_ref)
    lane = lax.broadcasted_iota(jnp.int32, (8, BLOCK), 1)
    row = lax.broadcasted_iota(jnp.int32, (8, BLOCK), 0)

    def turn(at):
        turned = lax.dot_general(sums[:, at], inverse[...], LANES, precision=HIGHEST, preferred_element_type=F32)
        turned_ref[:, at] = turned[: turned_ref.shape[0], :]
        return turned

    for start in range(0, feat, BLOCK):
        at, rest = slice(start, start + BLOCK), start + BLOCK
        if start:
            before = slice(start - BLOCK, start)
            taken = jnp.dot(turn(before), factor_ref[before, start:], precision=HIGHEST, preferred_element_type=F32)
            sums[:, start:] -= taken
        tiles = []
        for g in range(BLOCK // 8):
            tile = gram[start + 8 * g : start + 8 * g + 8, at]
            tiles.append(tile + jnp.where(lane == row + 8 * g, ridge, 0.0))
        upper, inverted = factor_block(tiles)
        for g in range(BLOCK // 8):
            factor_ref[start + 8 * g : start + 8 * g + 8, at] = upper[g]
            inverse[8 * g : 8 * g + 8, :] = inverted[g]
        if not start:
            for n in range(1, feat // BLOCK):
                gather_row(n)
            gather_sums()
        parts, turner = [], pieces(inverse[...])
        for i in range(rest, feat, BLOCK):
            here = slice(i, i + BLOCK)
            across = long_dot(turner, pieces(gram[at, here]), ((1,), (0,)))
            factor_ref[at, here] = across
            parts.append(pieces(across))
            for n, part in enumerate(parts):
                there = slice(rest + n * BLOCK, rest + (n + 1) * BLOCK)
                gram[there, here] -= long_dot(part, parts[-1], ((0,), (0,)))
    turn(slice(feat - BLOCK, feat))


def factor_and_solve(grams, sums, late, starts, ridge, feat, classes):
    padded = sums[0].shape[0]
    kernel = lambda *refs: solve_kernel(ridge, len(grams), len(late), *refs)
    scratch = [((feat, feat), F32), ((padded, feat), F32), ((BLOCK, BLOCK), F32)]
    if late:
        scratch += panel_scratch(late, feat, padded)
    outs = [(feat, feat), (classes, feat)]
    factor, turned = call(kernel, [starts] + grams + sums + [half for block in late for half in block], outs, scratch, 1, 6 * classes * feat**2)
    return factor, turned.T


def turns(size, step):
    return [(i, (i + step) % size) for i in range(size)]


def passed_on(blocks, axis):
    size = lax.axis_size(axis)
    return [lax.ppermute(block, axis, turns(size, d)) for block in blocks for d in range(1, size)]


def crossed(blocks):
    return list(zip(*[passed_on(halves, "cls") for halves in zip(*blocks)]))


def sums_passed_on(gram, sums):
    size = lax.axis_size("cls")
    return passed_on([gram], "cls"), [lax.ppermute(sums[d], "cls", turns(size, d)) for d in range(1, size)]


def gathered_sums(block, sums_of):
    size = lax.axis_size("img")
    far, next_ring, sums = [None, None], [None, None], None
    top, bottom = block
    for h in range(2):
        half = bottom if h else top
        far[h], next_ring[h] = passed_on([half], "sub"), lax.ppermute(half, "img", turns(size, 1))
        if not h:
            far[h], next_ring[h], bottom = lax.optimization_barrier((far[h], next_ring[h], bottom))
    came = [(top, bottom)]
    for step in range(1, size):
        last, swapped, passed = step == size - 1, [None, None], [None, None]
        for h in range(2):
            if step > 1 or h:
                tied = (next_ring[h], far[h], sums if h else None)
                next_ring[h], far[h], kept = lax.optimization_barrier(tied)
            if step == 1 and h:
                first = far[h]
            sums = kept if h else sums
            if not last:
                passed[h] = lax.ppermute(next_ring[h], "img", turns(size, 1))
            if last and h:
                swapped[h] = [lax.ppermute(half, "img", turns(size, -1)) for half in first]
            else:
                swapped[h] = passed_on([next_ring[h]], "sub")
        came += [tuple(next_ring)] + list(zip(*far))
        if step == 1 or last:
            sums, came = sums_of(sums, came), []
        next_ring, far = passed, swapped
    far, sums = lax.optimization_barrier((far, sums))
    late = list(zip(*far))
    gram, *sums = sums
    grams, others = sums_passed_on(gram, sums)
    return [gram] + grams, [sums[0]] + others, late + crossed(late)


def shards(images, labels, seeds):
    count = images.shape[0]
    feat = 4 * seeds.shape[0]
    parts = lax.axis_size("cls")
    members = math.prod(lax.axis_size(axis) for axis in ("img", "sub", "cls"))
    ridge = RIDGE * count * members
    classes = CLASSES // parts
    padded = -(-classes // BLOCK) * BLOCK
    starts = classes * ((lax.axis_index("cls") + jnp.arange(parts, dtype=jnp.int32)) % parts)
    block = panel_block(images, labels, seeds)

    def sums_of(so_far, blocks):
        return panel_sums(so_far, blocks, starts, feat, padded, parts)

    if members <= MOST_BLOCKS:
        grams, sums, late = gathered_sums(block, sums_of)
    else:
        gram, *sums = lax.psum(tuple(sums_of(None, [block])), ("img", "sub"))
        grams, others = sums_passed_on(gram, sums)
        grams, sums, late = [gram] + grams, [sums[0]] + others, []
    return factor_and_solve(grams, sums, late, starts, ridge, feat, classes)


def solution(mesh):
    placed = (P(("grp", "img", "sub", "cls"), None), P(("grp", "img", "sub", "cls")), P())
    return jax.shard_map(
        shards,
        mesh=mesh,
        in_specs=placed,
        out_specs=(P("grp", None), P("grp", "cls")),
        check_vma=False,
    )
```

```python
import functools
import math

import jax
import jax.numpy as jnp
from jax import lax
from jax.experimental import pallas as pl
from jax.experimental.pallas import tpu as pltpu
from jax.sharding import PartitionSpec as P

CLASSES = 1000
CHANNELS, SIDE, KERNEL, OUT, POOL = 3, 32, 6, 14, 7
MODULUS = 46337
RIDGE = 0.001
BLOCK = 128
HIGHEST = lax.Precision.HIGHEST
ROWS = (((0,), (0,)), ((), ()))
LANES = (((1,), (1,)), ((), ()))
VMEM_BYTES = 48 * 2**20
MOST_BLOCKS = 16
STRIDE = 8
F32, BF16 = jnp.float32, jnp.bfloat16


def call(kernel, operands, outs, scratch=(), scalars=0, flops=0, aliases=None):
    spaces = [pltpu.SMEM] * scalars + [pltpu.VMEM] * (len(operands) - scalars)
    moved = 4 * sum(math.prod(shape) for shape in outs) + sum(o.size * o.dtype.itemsize for o in operands)
    return pl.pallas_call(
        kernel,
        out_shape=[jax.ShapeDtypeStruct(shape, F32) for shape in outs],
        in_specs=[pl.BlockSpec(memory_space=space) for space in spaces],
        out_specs=[pl.BlockSpec(memory_space=pltpu.VMEM)] * len(outs),
        scratch_shapes=[pltpu.VMEM(shape, dtype) for shape, dtype in scratch],
        input_output_aliases=aliases or {},
        cost_estimate=pl.CostEstimate(flops=flops, bytes_accessed=moved, transcendentals=0),
        compiler_params=pltpu.CompilerParams(vmem_limit_bytes=VMEM_BYTES),
    )(*operands)


def residue(x):
    quotient = jnp.floor(x.astype(F32) * (1.0 / MODULUS)).astype(jnp.int32)
    rest = x - quotient * MODULUS
    rest = jnp.where(rest < 0, rest + MODULUS, rest)
    return jnp.where(rest >= MODULUS, rest - MODULUS, rest)


def filter_values(seeds, taps):
    index = lax.broadcasted_iota(jnp.int32, (BLOCK, seeds.shape[1]), 0)
    seed = jnp.broadcast_to(seeds, index.shape)
    first = residue(seed * 7919 + index * 104729)
    second = residue(first * first + seed)
    values = (second.astype(F32) / 46337.0 - 0.5) * math.sqrt(12.0 / 108.0)
    return jnp.where(index < taps, values, 0.0).astype(BF16)


def features_kernel(second, seeds_ref, image_ref, *refs):
    out_ref, shifted, bank, pools = refs[-4:]
    filters, (images, pixels) = pools.shape[1], image_ref.shape
    plane, window, half = SIDE * SIDE, 2 * BLOCK, BLOCK // 2
    taps = CHANNELS * KERNEL * KERNEL
    values = filter_values(seeds_ref[...], taps)
    tap = lax.broadcasted_iota(jnp.int32, (BLOCK, CHANNELS * window), 0)
    at = lax.broadcasted_iota(jnp.int32, (BLOCK, CHANNELS * window), 1)
    channel, row, column = at // window, (at % window) // SIDE, at % SIDE
    chosen = (tap == (channel * KERNEL + row) * KERNEL + column) & (row < KERNEL) & (column < KERNEL)
    spread = lax.dot_general(values, jnp.where(chosen, 1.0, 0.0).astype(BF16), ROWS, preferred_element_type=F32)
    for j in range(OUT):
        for t in range(0, CHANNELS * window, BLOCK):
            tile = spread[second * filters : (second + 1) * filters, t : t + BLOCK]
            if j:
                tile = pltpu.roll(tile, 2 * j, 1)
            bank[j * filters : (j + 1) * filters, t : t + BLOCK] = tile.astype(BF16)
    shifted[:, : pixels - BLOCK] = image_ref[:, half : pixels - half]
    shifted[:, pixels - BLOCK :] = jnp.concatenate(
        [image_ref[:, pixels - half :], jnp.zeros((images, half), BF16)], axis=1
    )
    pools[...] = jnp.zeros_like(pools)

    def windows(ref, m):
        starts = [plane * c + BLOCK * m for c in range(CHANNELS)]
        return jnp.concatenate([ref[:, s : s + window] for s in starts], axis=1)

    for m in range(OUT // 2):
        both = jnp.concatenate([windows(image_ref, m), windows(shifted, m)], axis=0)
        active = jnp.maximum(lax.dot_general(bank[...], both, LANES, preferred_element_type=F32), 0.0)
        for q in range(2):
            total = active[POOL * q * filters : (POOL * q + 1) * filters]
            for j in range(POOL * q + 1, POOL * (q + 1)):
                total = total + active[j * filters : (j + 1) * filters]
            pools[2 * (2 * m // POOL) + q] += total[:, :images]
            pools[2 * ((2 * m + 1) // POOL) + q] += total[:, images:]
    for w in range(4):
        out_ref[pl.ds(w, filters, stride=4), :] = pools[w] * (1.0 / (POOL * POOL))
    if second:
        out_ref[4 * filters :, :] = jnp.broadcast_to(refs[0][...].astype(F32), (8, images))


def panel_block(images, labels, seeds):
    count, pixels = images.shape
    filters = seeds.shape[0] // 2
    width = CHANNELS * 2 * BLOCK
    scratch = [((count, pixels), BF16), ((OUT * filters, width), BF16), ((4, filters, count), F32)]
    flops = 2 * OUT * OUT * filters * width * count
    halves, seeds = [], seeds[None]
    for n in range(2):
        kernel = functools.partial(features_kernel, n)
        operands = [seeds, images] + [labels[None]] * n
        halves += call(kernel, operands, [(4 * filters + 8 * n, count)], scratch, flops=flops)
        if not n:
            halves[0], seeds = lax.optimization_barrier((halves[0], seeds))
    return halves


def pieces(x):
    top = x.astype(BF16)
    rest = x - top.astype(F32)
    middle = rest.astype(BF16)
    return top, middle, (rest - middle.astype(F32)).astype(BF16)


def long_dot(one, two, dims):
    (left,), (right,) = dims
    a, b, c = one
    d, e, f = two
    return lax.dot_general(
        jnp.concatenate([a, a, b, a, b, c], axis=left),
        jnp.concatenate([d, e, d, f, e, d], axis=right),
        (dims, ((), ())),
        preferred_element_type=F32,
    )


def lane_copies(tile, lane):
    return jnp.broadcast_to(tile[:, lane : lane + 1], (8, BLOCK))


def row_copies(tile, row):
    return jnp.broadcast_to(tile[row : row + 1, :], (8, BLOCK))


def factor_block(tiles):
    lane = lax.broadcasted_iota(jnp.int32, (8, BLOCK), 1)
    row = lax.broadcasted_iota(jnp.int32, (8, BLOCK), 0)
    count = len(tiles)
    left = list(tiles)
    right = [jnp.where(lane == row + 8 * g, 1.0, 0.0) for g in range(count)]
    upper, inverse, raw = [], [], []
    own = [lane_copies(left[0], j) for j in range(8)]
    for p in range(count):
        top, bottom, scale = left[p], right[p], None
        stop = min(count, (p // STRIDE + 1) * STRIDE)
        cols = {g: [lane_copies(left[g], 8 * p + j) for j in range(8)] for g in range(p + 1, stop)}
        coming = [lane_copies(left[p + 1], 8 * p + 8 + j) for j in range(8)] if p + 1 < stop else []
        for j in range(8):
            pivot = row_copies(own[j], j)
            r = 1.0 / pivot
            for i in range(j + 1, 8):
                across = row_copies(own[i], j)
                t = across * r
                own[i] = own[i] - (own[j] * across) * r
                for g in cols:
                    cols[g][i] = cols[g][i] - cols[g][j] * t
            below = jnp.where(row > j, own[j], 0.0)
            top_row = row_copies(top, j) * r
            bottom_row = row_copies(bottom, j) * r
            top = top - below * top_row
            bottom = bottom - below * bottom_row
            for g in cols:
                left[g] = left[g] - cols[g][j] * top_row
                right[g] = right[g] - cols[g][j] * bottom_row
            if coming:
                edge = cols[p + 1][j]
                scaled = edge * r
                for c in range(8):
                    coming[c] = coming[c] - edge * row_copies(scaled, c)
            root = lax.rsqrt(pivot)
            scale = root if j == 0 else jnp.where(row == j, root, scale)
        raw.append(top * scale)
        upper.append(jnp.where(lane >= row + 8 * p, raw[p], 0.0))
        inverse.append(bottom * scale)
        if p + 1 == stop < count:
            done = slice(stop - STRIDE, stop)
            one = jnp.concatenate(raw[done], axis=0)
            both = jnp.concatenate([one, jnp.concatenate(inverse[done], axis=0)], axis=1)
            change = long_dot(pieces(one), pieces(both), ((0,), (0,)))
            for g in range(stop, count):
                left[g] = left[g] - change[8 * g : 8 * g + 8, :BLOCK]
                right[g] = right[g] - change[8 * g : 8 * g + 8, BLOCK:]
            coming = [lane_copies(left[stop], 8 * stop + j) for j in range(8)]
        own = coming
    return upper, inverse


def slots(feat):
    blocks = feat // BLOCK
    pairs = [(i, j) for i in range(blocks) for j in range(i, blocks)]
    return {pair: slice(n * BLOCK, (n + 1) * BLOCK) for n, pair in enumerate(pairs)}


def product(ones, twos):
    one, two = jnp.concatenate(ones, axis=1), jnp.concatenate(twos, axis=1)
    return lax.dot_general(one, two, LANES, preferred_element_type=F32)


def in_pairs(refs):
    return list(zip(refs[::2], refs[1::2]))


def split(block_refs, high, low):
    half, width = high.shape[0] // 2, block_refs[0][0].shape[1]
    for n, refs in enumerate(block_refs):
        at = slice(n * width, (n + 1) * width)
        for h, ref in enumerate(refs):
            rows = slice(h * half, (h + 1) * half)
            whole = ref[:half, :]
            top = whole.astype(BF16)
            high[rows, at] = top
            low[rows, at] = (whole - top.astype(F32)).astype(BF16)


def gram_row(i, high, low):
    feat = high.shape[0]
    at, rest = slice(i * BLOCK, (i + 1) * BLOCK), slice(i * BLOCK, feat)
    one, two = high[at, :], low[at, :]
    return product([one, one, two, two], [high[rest, :], low[rest, :], high[rest, :], low[rest, :]])


def add_gram(so_far, gram_ref, high, low):
    feat = high.shape[0]
    place = slots(feat)
    for i in range(feat // BLOCK):
        total = gram_row(i, high, low)
        for j in range(i, feat // BLOCK):
            tile = total[:, (j - i) * BLOCK : (j - i + 1) * BLOCK]
            gram_ref[place[i, j], :] = tile if so_far is None else so_far[place[i, j], :] + tile


def add_label_sums(starts_ref, block_refs, so_far, sums_refs, high, low, marks):
    half, width = high.shape[0] // 2, block_refs[0][0].shape[1]
    class_row = lax.broadcasted_iota(jnp.int32, (marks.shape[0], width), 0)
    for d, sums_ref in enumerate(sums_refs):
        for n, (_, ref) in enumerate(block_refs):
            label = ref[half : half + 1, :].astype(jnp.int32) - starts_ref[d]
            marks[:, n * width : (n + 1) * width] = jnp.where(class_row == label, 1.0, 0.0).astype(BF16)
        total = product([marks[...], marks[...]], [high[...], low[...]])
        sums_ref[...] = total if so_far is None else so_far[d][...] + total


def sums_kernel(blocks, carried, starts_ref, *refs):
    so_far, block_refs, refs = refs[:carried], in_pairs(refs[carried : carried + 2 * blocks]), refs[carried + 2 * blocks :]
    gram_ref, sums_refs, (high, low, marks) = refs[0], refs[1:-3], refs[-3:]
    split(block_refs, high, low)
    add_gram(so_far[0] if carried else None, gram_ref, high, low)
    add_label_sums(starts_ref, block_refs, so_far[1:] or None, sums_refs, high, low, marks)


def panel_scratch(blocks, feat, classes):
    width = sum(block[0].shape[1] for block in blocks)
    return [((feat, width), BF16), ((feat, width), BF16), ((classes, width), BF16)]


def panel_sums(so_far, blocks, starts, feat, classes, parts):
    width = sum(block[0].shape[1] for block in blocks)
    packed = (len(slots(feat)) * BLOCK, BLOCK)
    carried = list(so_far or [])
    kernel = lambda *refs: sums_kernel(len(blocks), len(carried), *refs)
    aliases = {1 + d: d for d in range(len(carried))}
    flops = 8 * width * math.prod(packed) + 4 * parts * width * classes * feat
    outs = [packed] + [(classes, feat)] * parts
    operands = [starts] + carried + [half for block in blocks for half in block]
    return call(kernel, operands, outs, panel_scratch(blocks, feat, classes), 1, flops, aliases)


def factor_rows(ridge, start, gram, factor_ref, inverse, beside):
    feat = gram.shape[1]
    lane = lax.broadcasted_iota(jnp.int32, (8, BLOCK), 1)
    row = lax.broadcasted_iota(jnp.int32, (8, BLOCK), 0)
    at, rest = slice(start, start + BLOCK), start + BLOCK
    tiles = []
    for g in range(BLOCK // 8):
        tile = gram[start + 8 * g : start + 8 * g + 8, at]
        tiles.append(tile + jnp.where(lane == row + 8 * g, ridge, 0.0))
    upper, inverted = factor_block(tiles)
    for g in range(BLOCK // 8):
        factor_ref[start + 8 * g : start + 8 * g + 8, at] = upper[g]
        inverse[8 * g : 8 * g + 8, :] = inverted[g]
    beside()
    parts, turner = [], pieces(inverse[...])
    for i in range(rest, feat, BLOCK):
        here = slice(i, i + BLOCK)
        across = long_dot(turner, pieces(gram[at, here]), ((1,), (0,)))
        factor_ref[at, here] = across
        parts.append(pieces(across))
        for n, part in enumerate(parts):
            there = slice(rest + n * BLOCK, rest + (n + 1) * BLOCK)
            gram[there, here] -= long_dot(part, parts[-1], ((0,), (0,)))


def first_kernel(ridge, given, late, *refs):
    gram_refs, block_refs = refs[:given], in_pairs(refs[given : given + 2 * late])
    rows_ref, gram, inverse_ref, *scratch = refs[given + 2 * late :]
    feat = gram.shape[0]
    place = slots(feat)
    if late:
        split(block_refs, *scratch)

    def gather_row(i):
        row = gram_row(i, *scratch) if late else None
        for j in range(i, feat // BLOCK):
            tile = sum(ref[place[i, j], :] for ref in gram_refs)
            if late:
                tile = tile + row[:, (j - i) * BLOCK : (j - i + 1) * BLOCK]
            gram[i * BLOCK : (i + 1) * BLOCK, j * BLOCK : (j + 1) * BLOCK] = tile

    def beside():
        for i in range(1, feat // BLOCK):
            gather_row(i)

    gather_row(0)
    factor_rows(ridge, 0, gram, rows_ref, inverse_ref, beside)


def rest_kernel(ridge, given, late, starts_ref, rows_ref, gram_ref, inverse_ref, *refs):
    sums_refs, block_refs, refs = refs[:given], in_pairs(refs[given : given + 2 * late]), refs[given + 2 * late :]
    factor_ref, turned_ref, gram, sums, inverse = refs[:5]
    feat = gram.shape[0]
    factor_ref[...] = jnp.zeros_like(factor_ref)
    factor_ref[:BLOCK, :] = rows_ref[...]
    for i in range(BLOCK, feat, BLOCK):
        gram[i : i + BLOCK, i:] = gram_ref[i : i + BLOCK, i:]
    inverse[...] = inverse_ref[...]

    def gather_sums():
        total = sum(ref[...] for ref in sums_refs)
        if late:
            high, low, marks = refs[5:]
            split(block_refs, high, low)
            add_label_sums(starts_ref, block_refs, [total], [sums], high, low, marks)
        else:
            sums[...] = total

    def turn(at):
        turned = lax.dot_general(sums[:, at], inverse[...], LANES, precision=HIGHEST, preferred_element_type=F32)
        turned_ref[:, at] = turned[: turned_ref.shape[0], :]
        return turned

    gather_sums()
    for start in range(BLOCK, feat, BLOCK):
        before = slice(start - BLOCK, start)
        taken = jnp.dot(turn(before), factor_ref[before, start:], precision=HIGHEST, preferred_element_type=F32)
        sums[:, start:] -= taken
        factor_rows(ridge, start, gram, factor_ref, inverse, lambda: None)
    turn(slice(feat - BLOCK, feat))


def factor_and_solve(grams, sums, late, starts, ridge, feat, classes):
    padded, given = sums[0].shape[0], len(grams)
    halves = [half for block in late for half in block]
    scratch = panel_scratch(late, feat, padded) if late else []
    kernel = functools.partial(first_kernel, ridge, given, len(late))
    outs = [(BLOCK, feat), (feat, feat), (BLOCK, BLOCK)]
    first = call(kernel, grams + halves, outs, scratch[:2], flops=2 * feat**3)
    kernel = functools.partial(rest_kernel, ridge, given, len(late))
    operands = [starts] + list(first) + sums + halves
    scratch = [((feat, feat), F32), ((padded, feat), F32), ((BLOCK, BLOCK), F32)] + scratch
    factor, turned = call(kernel, operands, [(feat, feat), (classes, feat)], scratch, 1, 6 * classes * feat**2)
    return factor, turned.T


def turns(size, step):
    return [(i, (i + step) % size) for i in range(size)]


def passed_on(blocks, axis):
    size = lax.axis_size(axis)
    return [lax.ppermute(block, axis, turns(size, d)) for block in blocks for d in range(1, size)]


def crossed(blocks):
    return list(zip(*[passed_on(halves, "cls") for halves in zip(*blocks)]))


def sums_passed_on(gram, sums):
    size = lax.axis_size("cls")
    grams, sums = lax.optimization_barrier((passed_on([gram], "cls"), sums))
    return grams, [lax.ppermute(sums[d], "cls", turns(size, d)) for d in range(1, size)]


def gathered_sums(block, sums_of):
    size = lax.axis_size("img")
    far, next_ring, sums = [None, None], [None, None], None
    top, bottom = block
    for h in range(2):
        half = bottom if h else top
        far[h], next_ring[h] = passed_on([half], "sub"), lax.ppermute(half, "img", turns(size, 1))
        if not h:
            far[h], next_ring[h], bottom = lax.optimization_barrier((far[h], next_ring[h], bottom))
    came = [(top, bottom)]
    for step in range(1, size):
        last, swapped, passed = step == size - 1, [None, None], [None, None]
        for h in range(2):
            if step > 1 or h:
                tied = (next_ring[h], far[h], sums if h else None)
                next_ring[h], far[h], kept = lax.optimization_barrier(tied)
            if step == 1 and h:
                first = far[h]
            sums = kept if h else sums
            if not last:
                passed[h] = lax.ppermute(next_ring[h], "img", turns(size, 1))
            if last and h:
                swapped[h] = [lax.ppermute(half, "img", turns(size, -1)) for half in first]
            else:
                swapped[h] = passed_on([next_ring[h]], "sub")
        came += [tuple(next_ring)] + list(zip(*far))
        if step == 1 or last:
            sums, came = sums_of(sums, came), []
        next_ring, far = passed, swapped
    far, sums = lax.optimization_barrier((far, sums))
    late = list(zip(*far))
    gram, *sums = sums
    grams, others = sums_passed_on(gram, sums)
    return [gram] + grams, [sums[0]] + others, late + crossed(late)


def shards(images, labels, seeds):
    count = images.shape[0]
    feat = 4 * seeds.shape[0]
    parts = lax.axis_size("cls")
    members = math.prod(lax.axis_size(axis) for axis in ("img", "sub", "cls"))
    ridge = RIDGE * count * members
    classes = CLASSES // parts
    padded = -(-classes // BLOCK) * BLOCK
    starts = classes * ((lax.axis_index("cls") + jnp.arange(parts, dtype=jnp.int32)) % parts)
    block = panel_block(images, labels, seeds)

    def sums_of(so_far, blocks):
        return panel_sums(so_far, blocks, starts, feat, padded, parts)

    if members <= MOST_BLOCKS:
        grams, sums, late = gathered_sums(block, sums_of)
    else:
        gram, *sums = lax.psum(tuple(sums_of(None, [block])), ("img", "sub"))
        grams, others = sums_passed_on(gram, sums)
        grams, sums, late = [gram] + grams, [sums[0]] + others, []
    return factor_and_solve(grams, sums, late, starts, ridge, feat, classes)


def solution(mesh):
    placed = (P(("grp", "img", "sub", "cls"), None), P(("grp", "img", "sub", "cls")), P())
    return jax.shard_map(
        shards,
        mesh=mesh,
        in_specs=placed,
        out_specs=(P("grp", None), P("grp", "cls")),
        check_vma=False,
    )
```

```python
import functools
import math

import jax
import jax.numpy as jnp
from jax import lax
from jax.experimental import pallas as pl
from jax.experimental.pallas import tpu as pltpu
from jax.sharding import PartitionSpec as P

CLASSES = 1000
CHANNELS, SIDE, KERNEL, OUT, POOL = 3, 32, 6, 14, 7
MODULUS = 46337
RIDGE = 0.001
BLOCK = 128
HIGHEST = lax.Precision.HIGHEST
ROWS = (((0,), (0,)), ((), ()))
LANES = (((1,), (1,)), ((), ()))
VMEM_BYTES = 48 * 2**20
MOST_BLOCKS = 16
STRIDE = 8
F32, BF16 = jnp.float32, jnp.bfloat16


def call(kernel, operands, outs, scratch=(), scalars=0, flops=0, aliases=None):
    spaces = [pltpu.SMEM] * scalars + [pltpu.VMEM] * (len(operands) - scalars)
    moved = 4 * sum(math.prod(shape) for shape in outs) + sum(o.size * o.dtype.itemsize for o in operands)
    return pl.pallas_call(
        kernel,
        out_shape=[jax.ShapeDtypeStruct(shape, F32) for shape in outs],
        in_specs=[pl.BlockSpec(memory_space=space) for space in spaces],
        out_specs=[pl.BlockSpec(memory_space=pltpu.VMEM)] * len(outs),
        scratch_shapes=[pltpu.VMEM(shape, dtype) for shape, dtype in scratch],
        input_output_aliases=aliases or {},
        cost_estimate=pl.CostEstimate(flops=flops, bytes_accessed=moved, transcendentals=0),
        compiler_params=pltpu.CompilerParams(vmem_limit_bytes=VMEM_BYTES),
    )(*operands)


def residue(x):
    quotient = jnp.floor(x.astype(F32) * (1.0 / MODULUS)).astype(jnp.int32)
    rest = x - quotient * MODULUS
    rest = jnp.where(rest < 0, rest + MODULUS, rest)
    return jnp.where(rest >= MODULUS, rest - MODULUS, rest)


def filter_values(seeds, taps):
    index = lax.broadcasted_iota(jnp.int32, (BLOCK, seeds.shape[1]), 0)
    seed = jnp.broadcast_to(seeds, index.shape)
    first = residue(seed * 7919 + index * 104729)
    second = residue(first * first + seed)
    values = (second.astype(F32) / 46337.0 - 0.5) * math.sqrt(12.0 / 108.0)
    return jnp.where(index < taps, values, 0.0).astype(BF16)


def features_kernel(second, seeds_ref, image_ref, *refs):
    out_ref, shifted, bank, pools = refs[-4:]
    filters, (images, pixels) = pools.shape[1], image_ref.shape
    plane, window, half = SIDE * SIDE, 2 * BLOCK, BLOCK // 2
    taps = CHANNELS * KERNEL * KERNEL
    values = filter_values(seeds_ref[...], taps)
    tap = lax.broadcasted_iota(jnp.int32, (BLOCK, CHANNELS * window), 0)
    at = lax.broadcasted_iota(jnp.int32, (BLOCK, CHANNELS * window), 1)
    channel, row, column = at // window, (at % window) // SIDE, at % SIDE
    chosen = (tap == (channel * KERNEL + row) * KERNEL + column) & (row < KERNEL) & (column < KERNEL)
    spread = lax.dot_general(values, jnp.where(chosen, 1.0, 0.0).astype(BF16), ROWS, preferred_element_type=F32)
    for j in range(OUT):
        for t in range(0, CHANNELS * window, BLOCK):
            tile = spread[second * filters : (second + 1) * filters, t : t + BLOCK]
            if j:
                tile = pltpu.roll(tile, 2 * j, 1)
            bank[j * filters : (j + 1) * filters, t : t + BLOCK] = tile.astype(BF16)
    shifted[:, : pixels - BLOCK] = image_ref[:, half : pixels - half]
    shifted[:, pixels - BLOCK :] = jnp.concatenate(
        [image_ref[:, pixels - half :], jnp.zeros((images, half), BF16)], axis=1
    )
    pools[...] = jnp.zeros_like(pools)

    def windows(ref, m):
        starts = [plane * c + BLOCK * m for c in range(CHANNELS)]
        return jnp.concatenate([ref[:, s : s + window] for s in starts], axis=1)

    for m in range(OUT // 2):
        both = jnp.concatenate([windows(image_ref, m), windows(shifted, m)], axis=0)
        active = jnp.maximum(lax.dot_general(bank[...], both, LANES, preferred_element_type=F32), 0.0)
        for q in range(2):
            total = active[POOL * q * filters : (POOL * q + 1) * filters]
            for j in range(POOL * q + 1, POOL * (q + 1)):
                total = total + active[j * filters : (j + 1) * filters]
            pools[2 * (2 * m // POOL) + q] += total[:, :images]
            pools[2 * ((2 * m + 1) // POOL) + q] += total[:, images:]
    for w in range(4):
        out_ref[pl.ds(w, filters, stride=4), :] = pools[w] * (1.0 / (POOL * POOL))
    if second:
        out_ref[4 * filters :, :] = jnp.broadcast_to(refs[0][...].astype(F32), (8, images))


def panel_block(images, labels, seeds):
    count, pixels = images.shape
    filters = seeds.shape[0] // 2
    width = CHANNELS * 2 * BLOCK
    scratch = [((count, pixels), BF16), ((OUT * filters, width), BF16), ((4, filters, count), F32)]
    flops = 2 * OUT * OUT * filters * width * count
    halves, seeds = [], seeds[None]
    for n in range(2):
        kernel = functools.partial(features_kernel, n)
        operands = [seeds, images] + [labels[None]] * n
        halves += call(kernel, operands, [(4 * filters + 8 * n, count)], scratch, flops=flops)
        if not n:
            halves[0], seeds = lax.optimization_barrier((halves[0], seeds))
    return halves


def pieces(x):
    top = x.astype(BF16)
    rest = x - top.astype(F32)
    middle = rest.astype(BF16)
    return top, middle, (rest - middle.astype(F32)).astype(BF16)


def long_dot(one, two, dims):
    (left,), (right,) = dims
    a, b, c = one
    d, e, f = two
    return lax.dot_general(
        jnp.concatenate([a, a, b, a, b, c], axis=left),
        jnp.concatenate([d, e, d, f, e, d], axis=right),
        (dims, ((), ())),
        preferred_element_type=F32,
    )


def lane_copies(tile, lane):
    return jnp.broadcast_to(tile[:, lane : lane + 1], (8, BLOCK))


def row_copies(tile, row):
    return jnp.broadcast_to(tile[row : row + 1, :], (8, BLOCK))


def factor_block(tiles):
    lane = lax.broadcasted_iota(jnp.int32, (8, BLOCK), 1)
    row = lax.broadcasted_iota(jnp.int32, (8, BLOCK), 0)
    count = len(tiles)
    left = list(tiles)
    right = [jnp.where(lane == row + 8 * g, 1.0, 0.0) for g in range(count)]
    upper, inverse, raw = [], [], []
    own = [lane_copies(left[0], j) for j in range(8)]
    for p in range(count):
        top, bottom, scale = left[p], right[p], None
        stop = min(count, (p // STRIDE + 1) * STRIDE)
        cols = {g: [lane_copies(left[g], 8 * p + j) for j in range(8)] for g in range(p + 1, stop)}
        coming = [lane_copies(left[p + 1], 8 * p + 8 + j) for j in range(8)] if p + 1 < stop else []
        for j in range(8):
            pivot = row_copies(own[j], j)
            r = 1.0 / pivot
            for i in range(j + 1, 8):
                across = row_copies(own[i], j)
                t = across * r
                own[i] = own[i] - (own[j] * across) * r
                for g in cols:
                    cols[g][i] = cols[g][i] - cols[g][j] * t
            below = jnp.where(row > j, own[j], 0.0)
            top_row = row_copies(top, j) * r
            bottom_row = row_copies(bottom, j) * r
            top = top - below * top_row
            bottom = bottom - below * bottom_row
            for g in cols:
                left[g] = left[g] - cols[g][j] * top_row
                right[g] = right[g] - cols[g][j] * bottom_row
            if coming:
                edge = cols[p + 1][j]
                scaled = edge * r
                for c in range(8):
                    coming[c] = coming[c] - edge * row_copies(scaled, c)
            root = lax.rsqrt(pivot)
            scale = root if j == 0 else jnp.where(row == j, root, scale)
        raw.append(top * scale)
        upper.append(jnp.where(lane >= row + 8 * p, raw[p], 0.0))
        inverse.append(bottom * scale)
        if p + 1 == stop < count:
            done = slice(stop - STRIDE, stop)
            one = jnp.concatenate(raw[done], axis=0)
            both = jnp.concatenate([one, jnp.concatenate(inverse[done], axis=0)], axis=1)
            change = long_dot(pieces(one), pieces(both), ((0,), (0,)))
            for g in range(stop, count):
                left[g] = left[g] - change[8 * g : 8 * g + 8, :BLOCK]
                right[g] = right[g] - change[8 * g : 8 * g + 8, BLOCK:]
            coming = [lane_copies(left[stop], 8 * stop + j) for j in range(8)]
        own = coming
    return upper, inverse


def slots(feat):
    blocks = feat // BLOCK
    pairs = [(i, j) for i in range(blocks) for j in range(i, blocks)]
    return {pair: slice(n * BLOCK, (n + 1) * BLOCK) for n, pair in enumerate(pairs)}


def product(ones, twos):
    one, two = jnp.concatenate(ones, axis=1), jnp.concatenate(twos, axis=1)
    return lax.dot_general(one, two, LANES, preferred_element_type=F32)


def in_pairs(refs):
    return list(zip(refs[::2], refs[1::2]))


def split(block_refs, high, low):
    half, width = high.shape[0] // 2, block_refs[0][0].shape[1]
    for n, refs in enumerate(block_refs):
        at = slice(n * width, (n + 1) * width)
        for h, ref in enumerate(refs):
            rows = slice(h * half, (h + 1) * half)
            whole = ref[:half, :]
            top = whole.astype(BF16)
            high[rows, at] = top
            low[rows, at] = (whole - top.astype(F32)).astype(BF16)


def gram_row(i, high, low):
    feat = high.shape[0]
    at, rest = slice(i * BLOCK, (i + 1) * BLOCK), slice(i * BLOCK, feat)
    one, two = high[at, :], low[at, :]
    return product([one, one, two, two], [high[rest, :], low[rest, :], high[rest, :], low[rest, :]])


def add_gram(so_far, gram_ref, high, low):
    feat = high.shape[0]
    place = slots(feat)
    for i in range(feat // BLOCK):
        total = gram_row(i, high, low)
        for j in range(i, feat // BLOCK):
            tile = total[:, (j - i) * BLOCK : (j - i + 1) * BLOCK]
            gram_ref[place[i, j], :] = tile if so_far is None else so_far[place[i, j], :] + tile


def add_label_sums(starts_ref, block_refs, so_far, sums_refs, high, low, marks):
    half, width = high.shape[0] // 2, block_refs[0][0].shape[1]
    class_row = lax.broadcasted_iota(jnp.int32, (marks.shape[0], width), 0)
    for d, sums_ref in enumerate(sums_refs):
        for n, (_, ref) in enumerate(block_refs):
            label = ref[half : half + 1, :].astype(jnp.int32) - starts_ref[d]
            marks[:, n * width : (n + 1) * width] = jnp.where(class_row == label, 1.0, 0.0).astype(BF16)
        total = product([marks[...], marks[...]], [high[...], low[...]])
        sums_ref[...] = total if so_far is None else so_far[d][...] + total


def sums_kernel(blocks, carried, starts_ref, *refs):
    so_far, block_refs, refs = refs[:carried], in_pairs(refs[carried : carried + 2 * blocks]), refs[carried + 2 * blocks :]
    gram_ref, sums_refs, (high, low, marks) = refs[0], refs[1:-3], refs[-3:]
    split(block_refs, high, low)
    add_gram(so_far[0] if carried else None, gram_ref, high, low)
    add_label_sums(starts_ref, block_refs, so_far[1:] or None, sums_refs, high, low, marks)


def panel_scratch(blocks, feat, classes):
    width = sum(block[0].shape[1] for block in blocks)
    return [((feat, width), BF16), ((feat, width), BF16), ((classes, width), BF16)]


def panel_sums(so_far, blocks, starts, feat, classes, parts):
    width = sum(block[0].shape[1] for block in blocks)
    packed = (len(slots(feat)) * BLOCK, BLOCK)
    carried = list(so_far or [])
    kernel = lambda *refs: sums_kernel(len(blocks), len(carried), *refs)
    aliases = {1 + d: d for d in range(len(carried))}
    flops = 8 * width * math.prod(packed) + 4 * parts * width * classes * feat
    outs = [packed] + [(classes, feat)] * parts
    operands = [starts] + carried + [half for block in blocks for half in block]
    return call(kernel, operands, outs, panel_scratch(blocks, feat, classes), 1, flops, aliases)


def solve_kernel(ridge, given, late, starts_ref, *refs):
    gram_refs, sums_refs, refs = refs[:given], refs[given : 2 * given], refs[2 * given :]
    block_refs, (factor_ref, turned_ref, gram, sums, inverse) = in_pairs(refs[: 2 * late]), refs[2 * late :][:5]
    feat = gram.shape[0]
    place = slots(feat)
    if late:
        high, low, marks = refs[-3:]
        split(block_refs, high, low)

    def gather_row(i):
        row = gram_row(i, high, low) if late else None
        for j in range(i, feat // BLOCK):
            tile = sum(ref[place[i, j], :] for ref in gram_refs)
            if late:
                tile = tile + row[:, (j - i) * BLOCK : (j - i + 1) * BLOCK]
            gram[i * BLOCK : (i + 1) * BLOCK, j * BLOCK : (j + 1) * BLOCK] = tile

    def gather_sums():
        total = sum(ref[...] for ref in sums_refs)
        if late:
            add_label_sums(starts_ref, block_refs, [total], [sums], high, low, marks)
        else:
            sums[...] = total

    gather_row(0)
    factor_ref[...] = jnp.zeros_like(factor_ref)
    lane = lax.broadcasted_iota(jnp.int32, (8, BLOCK), 1)
    row = lax.broadcasted_iota(jnp.int32, (8, BLOCK), 0)

    def turn(at):
        turned = lax.dot_general(sums[:, at], inverse[...], LANES, precision=HIGHEST, preferred_element_type=F32)
        turned_ref[:, at] = turned[: turned_ref.shape[0], :]
        return turned

    for start in range(0, feat, BLOCK):
        at, rest = slice(start, start + BLOCK), start + BLOCK
        if start:
            before = slice(start - BLOCK, start)
            taken = jnp.dot(turn(before), factor_ref[before, start:], precision=HIGHEST, preferred_element_type=F32)
            sums[:, start:] -= taken
        tiles = []
        for g in range(BLOCK // 8):
            tile = gram[start + 8 * g : start + 8 * g + 8, at]
            tiles.append(tile + jnp.where(lane == row + 8 * g, ridge, 0.0))
        upper, inverted = factor_block(tiles)
        for g in range(BLOCK // 8):
            factor_ref[start + 8 * g : start + 8 * g + 8, at] = upper[g]
            inverse[8 * g : 8 * g + 8, :] = inverted[g]
        if not start:
            for n in range(1, feat // BLOCK):
                gather_row(n)
            gather_sums()
        parts, turner = [], pieces(inverse[...])
        for i in range(rest, feat, BLOCK):
            here = slice(i, i + BLOCK)
            across = long_dot(turner, pieces(gram[at, here]), ((1,), (0,)))
            factor_ref[at, here] = across
            parts.append(pieces(across))
            for n, part in enumerate(parts):
                there = slice(rest + n * BLOCK, rest + (n + 1) * BLOCK)
                gram[there, here] -= long_dot(part, parts[-1], ((0,), (0,)))
    turn(slice(feat - BLOCK, feat))


def factor_and_solve(grams, sums, late, starts, ridge, feat, classes):
    padded = sums[0].shape[0]
    kernel = lambda *refs: solve_kernel(ridge, len(grams), len(late), *refs)
    scratch = [((feat, feat), F32), ((padded, feat), F32), ((BLOCK, BLOCK), F32)]
    if late:
        scratch += panel_scratch(late, feat, padded)
    outs = [(feat, feat), (classes, feat)]
    factor, turned = call(kernel, [starts] + grams + sums + [half for block in late for half in block], outs, scratch, 1, 6 * classes * feat**2)
    return factor, turned.T


def turns(size, step):
    return [(i, (i + step) % size) for i in range(size)]


def passed_on(blocks, axis):
    size = lax.axis_size(axis)
    return [lax.ppermute(block, axis, turns(size, d)) for block in blocks for d in range(1, size)]


def crossed(blocks):
    return list(zip(*[passed_on(halves, "cls") for halves in zip(*blocks)]))


def sums_passed_on(gram, sums):
    size = lax.axis_size("cls")
    return passed_on([gram], "cls"), [lax.ppermute(sums[d], "cls", turns(size, d)) for d in range(1, size)]


def gathered_sums(block, sums_of):
    size = lax.axis_size("img")
    far, next_ring, sums = [None, None], [None, None], None
    top, bottom = block
    for h in range(2):
        half = bottom if h else top
        far[h], next_ring[h] = passed_on([half], "sub"), lax.ppermute(half, "img", turns(size, 1))
        if not h:
            far[h], next_ring[h], bottom = lax.optimization_barrier((far[h], next_ring[h], bottom))
    came = [(top, bottom)]
    early = lax.ppermute(top, "img", turns(size, -1)) if size > 2 else None
    for step in range(1, size):
        last, swapped, passed = step == size - 1, [None, None], [None, None]
        for h in range(2):
            if h:
                tied = (next_ring[1], far[1], sums, early)
                next_ring[1], far[1], sums, early = lax.optimization_barrier(tied)
            elif step > 1 and not last:
                next_ring[0], far[0] = lax.optimization_barrier((next_ring[0], far[0]))
            if step == 1 and h:
                first = far[h]
            if not last and (h or step < size - 2):
                passed[h] = lax.ppermute(next_ring[h], "img", turns(size, 1))
            if last and h:
                swapped[h] = [lax.ppermute(half, "img", turns(size, -1)) for half in first]
            else:
                swapped[h] = passed_on([next_ring[h]], "sub")
        came += [tuple(next_ring)] + list(zip(*far))
        if step == 1 or last:
            sums, came = sums_of(sums, came), []
        if step == size - 2:
            passed[0] = early
        next_ring, far = passed, swapped
    far, sums = lax.optimization_barrier((far, sums))
    late = list(zip(*far))
    gram, *sums = sums
    grams, others = sums_passed_on(gram, sums)
    return [gram] + grams, [sums[0]] + others, late + crossed(late)


def shards(images, labels, seeds):
    count = images.shape[0]
    feat = 4 * seeds.shape[0]
    parts = lax.axis_size("cls")
    members = math.prod(lax.axis_size(axis) for axis in ("img", "sub", "cls"))
    ridge = RIDGE * count * members
    classes = CLASSES // parts
    padded = -(-classes // BLOCK) * BLOCK
    starts = classes * ((lax.axis_index("cls") + jnp.arange(parts, dtype=jnp.int32)) % parts)
    block = panel_block(images, labels, seeds)

    def sums_of(so_far, blocks):
        return panel_sums(so_far, blocks, starts, feat, padded, parts)

    if members <= MOST_BLOCKS:
        grams, sums, late = gathered_sums(block, sums_of)
    else:
        gram, *sums = lax.psum(tuple(sums_of(None, [block])), ("img", "sub"))
        grams, others = sums_passed_on(gram, sums)
        grams, sums, late = [gram] + grams, [sums[0]] + others, []
    return factor_and_solve(grams, sums, late, starts, ridge, feat, classes)


def solution(mesh):
    placed = (P(("grp", "img", "sub", "cls"), None), P(("grp", "img", "sub", "cls")), P())
    return jax.shard_map(
        shards,
        mesh=mesh,
        in_specs=placed,
        out_specs=(P("grp", None), P("grp", "cls")),
        check_vma=False,
    )
```

```python
import functools
import math

import jax
import jax.numpy as jnp
from jax import lax
from jax.experimental import pallas as pl
from jax.experimental.pallas import tpu as pltpu
from jax.sharding import PartitionSpec as P

CLASSES = 1000
CHANNELS, SIDE, KERNEL, OUT, POOL = 3, 32, 6, 14, 7
MODULUS = 46337
RIDGE = 0.001
BLOCK = 128
HIGHEST = lax.Precision.HIGHEST
ROWS = (((0,), (0,)), ((), ()))
LANES = (((1,), (1,)), ((), ()))
VMEM_BYTES = 48 * 2**20
MOST_BLOCKS = 16
STRIDE = 8
F32, BF16 = jnp.float32, jnp.bfloat16


def call(kernel, operands, outs, scratch=(), scalars=0, flops=0, aliases=None, out_space=pltpu.VMEM):
    spaces = [pltpu.SMEM] * scalars + [pltpu.VMEM] * (len(operands) - scalars)
    moved = 4 * sum(math.prod(shape) for shape in outs) + sum(o.size * o.dtype.itemsize for o in operands)
    return pl.pallas_call(
        kernel,
        out_shape=[jax.ShapeDtypeStruct(shape, F32) for shape in outs],
        in_specs=[pl.BlockSpec(memory_space=space) for space in spaces],
        out_specs=[pl.BlockSpec(memory_space=out_space)] * len(outs),
        scratch_shapes=[pltpu.VMEM(*some) if isinstance(some, tuple) else some for some in scratch],
        input_output_aliases=aliases or {},
        cost_estimate=pl.CostEstimate(flops=flops, bytes_accessed=moved, transcendentals=0),
        compiler_params=pltpu.CompilerParams(vmem_limit_bytes=VMEM_BYTES),
    )(*operands)


def residue(x):
    quotient = jnp.floor(x.astype(F32) * (1.0 / MODULUS)).astype(jnp.int32)
    rest = x - quotient * MODULUS
    rest = jnp.where(rest < 0, rest + MODULUS, rest)
    return jnp.where(rest >= MODULUS, rest - MODULUS, rest)


def filter_values(seeds, taps):
    index = lax.broadcasted_iota(jnp.int32, (BLOCK, seeds.shape[1]), 0)
    seed = jnp.broadcast_to(seeds, index.shape)
    first = residue(seed * 7919 + index * 104729)
    second = residue(first * first + seed)
    values = (second.astype(F32) / 46337.0 - 0.5) * math.sqrt(12.0 / 108.0)
    return jnp.where(index < taps, values, 0.0).astype(BF16)


def features_kernel(second, seeds_ref, image_ref, *refs):
    out_ref, shifted, bank, pools = refs[-4:]
    filters, (images, pixels) = pools.shape[1], image_ref.shape
    plane, window, half = SIDE * SIDE, 2 * BLOCK, BLOCK // 2
    taps = CHANNELS * KERNEL * KERNEL
    values = filter_values(seeds_ref[...], taps)
    tap = lax.broadcasted_iota(jnp.int32, (BLOCK, CHANNELS * window), 0)
    at = lax.broadcasted_iota(jnp.int32, (BLOCK, CHANNELS * window), 1)
    channel, row, column = at // window, (at % window) // SIDE, at % SIDE
    chosen = (tap == (channel * KERNEL + row) * KERNEL + column) & (row < KERNEL) & (column < KERNEL)
    spread = lax.dot_general(values, jnp.where(chosen, 1.0, 0.0).astype(BF16), ROWS, preferred_element_type=F32)
    for j in range(OUT):
        for t in range(0, CHANNELS * window, BLOCK):
            tile = spread[second * filters : (second + 1) * filters, t : t + BLOCK]
            if j:
                tile = pltpu.roll(tile, 2 * j, 1)
            bank[j * filters : (j + 1) * filters, t : t + BLOCK] = tile.astype(BF16)
    shifted[:, : pixels - BLOCK] = image_ref[:, half : pixels - half]
    shifted[:, pixels - BLOCK :] = jnp.concatenate(
        [image_ref[:, pixels - half :], jnp.zeros((images, half), BF16)], axis=1
    )
    pools[...] = jnp.zeros_like(pools)

    def windows(ref, m):
        starts = [plane * c + BLOCK * m for c in range(CHANNELS)]
        return jnp.concatenate([ref[:, s : s + window] for s in starts], axis=1)

    for m in range(OUT // 2):
        both = jnp.concatenate([windows(image_ref, m), windows(shifted, m)], axis=0)
        active = jnp.maximum(lax.dot_general(bank[...], both, LANES, preferred_element_type=F32), 0.0)
        for q in range(2):
            total = active[POOL * q * filters : (POOL * q + 1) * filters]
            for j in range(POOL * q + 1, POOL * (q + 1)):
                total = total + active[j * filters : (j + 1) * filters]
            pools[2 * (2 * m // POOL) + q] += total[:, :images]
            pools[2 * ((2 * m + 1) // POOL) + q] += total[:, images:]
    for w in range(4):
        out_ref[pl.ds(w, filters, stride=4), :] = pools[w] * (1.0 / (POOL * POOL))
    if second:
        out_ref[4 * filters :, :] = jnp.broadcast_to(refs[0][...].astype(F32), (8, images))


def panel_block(images, labels, seeds):
    count, pixels = images.shape
    filters = seeds.shape[0] // 2
    width = CHANNELS * 2 * BLOCK
    scratch = [((count, pixels), BF16), ((OUT * filters, width), BF16), ((4, filters, count), F32)]
    flops = 2 * OUT * OUT * filters * width * count
    halves, seeds = [], seeds[None]
    for n in range(2):
        kernel = functools.partial(features_kernel, n)
        operands = [seeds, images] + [labels[None]] * n
        halves += call(kernel, operands, [(4 * filters + 8 * n, count)], scratch, flops=flops)
        if not n:
            halves[0], seeds = lax.optimization_barrier((halves[0], seeds))
    return halves


def pieces(x):
    top = x.astype(BF16)
    rest = x - top.astype(F32)
    middle = rest.astype(BF16)
    return top, middle, (rest - middle.astype(F32)).astype(BF16)


def long_dot(one, two, dims):
    (left,), (right,) = dims
    a, b, c = one
    d, e, f = two
    return lax.dot_general(
        jnp.concatenate([a, a, b, a, b, c], axis=left),
        jnp.concatenate([d, e, d, f, e, d], axis=right),
        (dims, ((), ())),
        preferred_element_type=F32,
    )


def lane_copies(tile, lane):
    return jnp.broadcast_to(tile[:, lane : lane + 1], (8, BLOCK))


def row_copies(tile, row):
    return jnp.broadcast_to(tile[row : row + 1, :], (8, BLOCK))


def factor_block(tiles):
    lane = lax.broadcasted_iota(jnp.int32, (8, BLOCK), 1)
    row = lax.broadcasted_iota(jnp.int32, (8, BLOCK), 0)
    count = len(tiles)
    left = list(tiles)
    right = [jnp.where(lane == row + 8 * g, 1.0, 0.0) for g in range(count)]
    upper, inverse, raw = [], [], []
    own = [lane_copies(left[0], j) for j in range(8)]
    for p in range(count):
        top, bottom, scale = left[p], right[p], None
        stop = min(count, (p // STRIDE + 1) * STRIDE)
        cols = {g: [lane_copies(left[g], 8 * p + j) for j in range(8)] for g in range(p + 1, stop)}
        coming = [lane_copies(left[p + 1], 8 * p + 8 + j) for j in range(8)] if p + 1 < stop else []
        for j in range(8):
            pivot = row_copies(own[j], j)
            r = 1.0 / pivot
            for i in range(j + 1, 8):
                across = row_copies(own[i], j)
                t = across * r
                own[i] = own[i] - (own[j] * across) * r
                for g in cols:
                    cols[g][i] = cols[g][i] - cols[g][j] * t
            below = jnp.where(row > j, own[j], 0.0)
            top_row = row_copies(top, j) * r
            bottom_row = row_copies(bottom, j) * r
            top = top - below * top_row
            bottom = bottom - below * bottom_row
            for g in cols:
                left[g] = left[g] - cols[g][j] * top_row
                right[g] = right[g] - cols[g][j] * bottom_row
            if coming:
                edge = cols[p + 1][j]
                scaled = edge * r
                for c in range(8):
                    coming[c] = coming[c] - edge * row_copies(scaled, c)
            root = lax.rsqrt(pivot)
            scale = root if j == 0 else jnp.where(row == j, root, scale)
        raw.append(top * scale)
        upper.append(jnp.where(lane >= row + 8 * p, raw[p], 0.0))
        inverse.append(bottom * scale)
        if p + 1 == stop < count:
            done = slice(stop - STRIDE, stop)
            one = jnp.concatenate(raw[done], axis=0)
            both = jnp.concatenate([one, jnp.concatenate(inverse[done], axis=0)], axis=1)
            change = long_dot(pieces(one), pieces(both), ((0,), (0,)))
            for g in range(stop, count):
                left[g] = left[g] - change[8 * g : 8 * g + 8, :BLOCK]
                right[g] = right[g] - change[8 * g : 8 * g + 8, BLOCK:]
            coming = [lane_copies(left[stop], 8 * stop + j) for j in range(8)]
        own = coming
    return upper, inverse


def slots(feat):
    blocks = feat // BLOCK
    pairs = [(i, j) for i in range(blocks) for j in range(i, blocks)]
    return {pair: slice(n * BLOCK, (n + 1) * BLOCK) for n, pair in enumerate(pairs)}


def product(ones, twos):
    one, two = jnp.concatenate(ones, axis=1), jnp.concatenate(twos, axis=1)
    return lax.dot_general(one, two, LANES, preferred_element_type=F32)


def in_pairs(refs):
    return list(zip(refs[::2], refs[1::2]))


def split(block_refs, high, low):
    half, width = high.shape[0] // 2, block_refs[0][0].shape[1]
    for n, refs in enumerate(block_refs):
        at = slice(n * width, (n + 1) * width)
        for h, ref in enumerate(refs):
            rows = slice(h * half, (h + 1) * half)
            whole = ref[:half, :]
            top = whole.astype(BF16)
            high[rows, at] = top
            low[rows, at] = (whole - top.astype(F32)).astype(BF16)


def gram_row(i, high, low):
    feat = high.shape[0]
    at, rest = slice(i * BLOCK, (i + 1) * BLOCK), slice(i * BLOCK, feat)
    one, two = high[at, :], low[at, :]
    return product([one, one, two, two], [high[rest, :], low[rest, :], high[rest, :], low[rest, :]])


def add_gram(so_far, gram_ref, high, low):
    feat = high.shape[0]
    place = slots(feat)
    for i in range(feat // BLOCK):
        total = gram_row(i, high, low)
        for j in range(i, feat // BLOCK):
            tile = total[:, (j - i) * BLOCK : (j - i + 1) * BLOCK]
            gram_ref[place[i, j], :] = tile if so_far is None else so_far[place[i, j], :] + tile


def add_label_sums(starts_ref, block_refs, so_far, sums_refs, high, low, marks):
    half, width = high.shape[0] // 2, block_refs[0][0].shape[1]
    class_row = lax.broadcasted_iota(jnp.int32, (marks.shape[0], width), 0)
    for d, sums_ref in enumerate(sums_refs):
        for n, (_, ref) in enumerate(block_refs):
            label = ref[half : half + 1, :].astype(jnp.int32) - starts_ref[d]
            marks[:, n * width : (n + 1) * width] = jnp.where(class_row == label, 1.0, 0.0).astype(BF16)
        total = product([marks[...], marks[...]], [high[...], low[...]])
        sums_ref[...] = total if so_far is None else so_far[d][...] + total


def sums_kernel(blocks, carried, starts_ref, *refs):
    so_far, block_refs, refs = refs[:carried], in_pairs(refs[carried : carried + 2 * blocks]), refs[carried + 2 * blocks :]
    gram_ref, sums_refs, (high, low, marks) = refs[0], refs[1:-3], refs[-3:]
    split(block_refs, high, low)
    add_gram(so_far[0] if carried else None, gram_ref, high, low)
    add_label_sums(starts_ref, block_refs, so_far[1:] or None, sums_refs, high, low, marks)


def panel_scratch(blocks, feat, classes):
    width = sum(block[0].shape[1] for block in blocks)
    return [((feat, width), BF16), ((feat, width), BF16), ((classes, width), BF16)]


def panel_sums(so_far, blocks, starts, feat, classes, parts):
    width = sum(block[0].shape[1] for block in blocks)
    packed = (len(slots(feat)) * BLOCK, BLOCK)
    carried = list(so_far or [])
    kernel = lambda *refs: sums_kernel(len(blocks), len(carried), *refs)
    aliases = {1 + d: d for d in range(len(carried))}
    flops = 8 * width * math.prod(packed) + 4 * parts * width * classes * feat
    outs = [packed] + [(classes, feat)] * parts
    operands = [starts] + carried + [half for block in blocks for half in block]
    return call(kernel, operands, outs, panel_scratch(blocks, feat, classes), 1, flops, aliases)


def solve_kernel(ridge, given, late, starts_ref, *refs):
    gram_refs, sums_refs, refs = refs[:given], refs[given : 2 * given], refs[2 * given :]
    block_refs, refs = in_pairs(refs[: 2 * late]), refs[2 * late :]
    factor_out, turned_out, factor_ref, turned_ref, gram, sums, inverse, sent = refs[:8]
    feat = gram.shape[0]
    place = slots(feat)
    if late:
        high, low, marks = refs[-3:]
        split(block_refs, high, low)

    def gather_row(i):
        row = gram_row(i, high, low) if late else None
        for j in range(i, feat // BLOCK):
            tile = sum(ref[place[i, j], :] for ref in gram_refs)
            if late:
                tile = tile + row[:, (j - i) * BLOCK : (j - i + 1) * BLOCK]
            gram[i * BLOCK : (i + 1) * BLOCK, j * BLOCK : (j + 1) * BLOCK] = tile

    def gather_sums():
        total = sum(ref[...] for ref in sums_refs)
        if late:
            add_label_sums(starts_ref, block_refs, [total], [sums], high, low, marks)
        else:
            sums[...] = total

    gather_row(0)
    factor_ref[...] = jnp.zeros_like(factor_ref)
    lane = lax.broadcasted_iota(jnp.int32, (8, BLOCK), 1)
    row = lax.broadcasted_iota(jnp.int32, (8, BLOCK), 0)

    copies = []

    def send(source, target):
        copies.append(pltpu.make_async_copy(source, target, sent.at[len(copies)]))
        copies[-1].start()

    def turn(at):
        turned = lax.dot_general(sums[:, at], inverse[...], LANES, precision=HIGHEST, preferred_element_type=F32)
        turned_ref[:, at] = turned[: turned_ref.shape[0], :]
        send(turned_ref.at[:, at], turned_out.at[:, at])
        return turned

    for start in range(0, feat, BLOCK):
        at, rest = slice(start, start + BLOCK), start + BLOCK
        if start:
            before = slice(start - BLOCK, start)
            taken = jnp.dot(turn(before), factor_ref[before, start:], precision=HIGHEST, preferred_element_type=F32)
            sums[:, start:] -= taken
        tiles = []
        for g in range(BLOCK // 8):
            tile = gram[start + 8 * g : start + 8 * g + 8, at]
            tiles.append(tile + jnp.where(lane == row + 8 * g, ridge, 0.0))
        upper, inverted = factor_block(tiles)
        for g in range(BLOCK // 8):
            factor_ref[start + 8 * g : start + 8 * g + 8, at] = upper[g]
            inverse[8 * g : 8 * g + 8, :] = inverted[g]
        if not start:
            for n in range(1, feat // BLOCK):
                gather_row(n)
            gather_sums()
        parts, turner = [], pieces(inverse[...])
        for i in range(rest, feat, BLOCK):
            here = slice(i, i + BLOCK)
            across = long_dot(turner, pieces(gram[at, here]), ((1,), (0,)))
            factor_ref[at, here] = across
            parts.append(pieces(across))
            for n, part in enumerate(parts):
                there = slice(rest + n * BLOCK, rest + (n + 1) * BLOCK)
                gram[there, here] -= long_dot(part, parts[-1], ((0,), (0,)))
        send(factor_ref.at[at, :], factor_out.at[at, :])
    turn(slice(feat - BLOCK, feat))
    for copy in copies:
        copy.wait()


def factor_and_solve(grams, sums, late, starts, ridge, feat, classes):
    padded = sums[0].shape[0]
    kernel = lambda *refs: solve_kernel(ridge, len(grams), len(late), *refs)
    scratch = [((feat, feat), F32), ((classes, feat), F32), ((feat, feat), F32), ((padded, feat), F32)]
    scratch += [((BLOCK, BLOCK), F32), pltpu.SemaphoreType.DMA((2 * feat // BLOCK,))]
    if late:
        scratch += panel_scratch(late, feat, padded)
    outs = [(feat, feat), (classes, feat)]
    factor, turned = call(kernel, [starts] + grams + sums + [half for block in late for half in block], outs, scratch, 1, 6 * classes * feat**2, None, pl.ANY)
    return factor, turned.T


def turns(size, step):
    return [(i, (i + step) % size) for i in range(size)]


def passed_on(blocks, axis):
    size = lax.axis_size(axis)
    return [lax.ppermute(block, axis, turns(size, d)) for block in blocks for d in range(1, size)]


def crossed(blocks):
    return list(zip(*[passed_on(halves, "cls") for halves in zip(*blocks)]))


def sums_passed_on(gram, sums):
    size = lax.axis_size("cls")
    return passed_on([gram], "cls"), [lax.ppermute(sums[d], "cls", turns(size, d)) for d in range(1, size)]


def gathered_sums(block, sums_of):
    size = lax.axis_size("img")
    far, next_ring, sums = [None, None], [None, None], None
    top, bottom = block
    for h in range(2):
        half = bottom if h else top
        far[h], next_ring[h] = passed_on([half], "sub"), lax.ppermute(half, "img", turns(size, 1))
        if not h:
            far[h], next_ring[h], bottom = lax.optimization_barrier((far[h], next_ring[h], bottom))
    came = [(top, bottom)]
    for step in range(1, size):
        last, swapped, passed = step == size - 1, [None, None], [None, None]
        for h in range(2):
            if step > 1 or h:
                tied = (next_ring[h], far[h], sums if h else None)
                next_ring[h], far[h], kept = lax.optimization_barrier(tied)
            if step == 1 and h:
                first = far[h]
            sums = kept if h else sums
            if not last:
                passed[h] = lax.ppermute(next_ring[h], "img", turns(size, 1))
            if last and h:
                swapped[h] = [lax.ppermute(half, "img", turns(size, -1)) for half in first]
            else:
                swapped[h] = passed_on([next_ring[h]], "sub")
        came += [tuple(next_ring)] + list(zip(*far))
        if step == 1 or last:
            sums, came = sums_of(sums, came), []
        next_ring, far = passed, swapped
    far, sums = lax.optimization_barrier((far, sums))
    late = list(zip(*far))
    gram, *sums = sums
    grams, others = sums_passed_on(gram, sums)
    return [gram] + grams, [sums[0]] + others, late + crossed(late)


def shards(images, labels, seeds):
    count = images.shape[0]
    feat = 4 * seeds.shape[0]
    parts = lax.axis_size("cls")
    members = math.prod(lax.axis_size(axis) for axis in ("img", "sub", "cls"))
    ridge = RIDGE * count * members
    classes = CLASSES // parts
    padded = -(-classes // BLOCK) * BLOCK
    starts = classes * ((lax.axis_index("cls") + jnp.arange(parts, dtype=jnp.int32)) % parts)
    block = panel_block(images, labels, seeds)

    def sums_of(so_far, blocks):
        return panel_sums(so_far, blocks, starts, feat, padded, parts)

    if members <= MOST_BLOCKS:
        grams, sums, late = gathered_sums(block, sums_of)
    else:
        gram, *sums = lax.psum(tuple(sums_of(None, [block])), ("img", "sub"))
        grams, others = sums_passed_on(gram, sums)
        grams, sums, late = [gram] + grams, [sums[0]] + others, []
    return factor_and_solve(grams, sums, late, starts, ridge, feat, classes)


def solution(mesh):
    placed = (P(("grp", "img", "sub", "cls"), None), P(("grp", "img", "sub", "cls")), P())
    return jax.shard_map(
        shards,
        mesh=mesh,
        in_specs=placed,
        out_specs=(P("grp", None), P("grp", "cls")),
        check_vma=False,
    )
```

```python
import functools
import math

import jax
import jax.numpy as jnp
from jax import lax
from jax.experimental import pallas as pl
from jax.experimental.pallas import tpu as pltpu
from jax.sharding import PartitionSpec as P

CLASSES = 1000
CHANNELS, SIDE, KERNEL, OUT, POOL = 3, 32, 6, 14, 7
MODULUS = 46337
RIDGE = 0.001
BLOCK = 128
HIGHEST = lax.Precision.HIGHEST
ROWS = (((0,), (0,)), ((), ()))
LANES = (((1,), (1,)), ((), ()))
VMEM_BYTES = 48 * 2**20
MOST_BLOCKS = 16
STRIDE = 8
F32, BF16 = jnp.float32, jnp.bfloat16


def call(kernel, operands, outs, scratch=(), scalars=0, flops=0, aliases=None):
    spaces = [pltpu.SMEM] * scalars + [pltpu.VMEM] * (len(operands) - scalars)
    moved = 4 * sum(math.prod(shape) for shape in outs) + sum(o.size * o.dtype.itemsize for o in operands)
    return pl.pallas_call(
        kernel,
        out_shape=[jax.ShapeDtypeStruct(shape, F32) for shape in outs],
        in_specs=[pl.BlockSpec(memory_space=space) for space in spaces],
        out_specs=[pl.BlockSpec(memory_space=pltpu.VMEM)] * len(outs),
        scratch_shapes=[pltpu.VMEM(shape, dtype) for shape, dtype in scratch],
        input_output_aliases=aliases or {},
        cost_estimate=pl.CostEstimate(flops=flops, bytes_accessed=moved, transcendentals=0),
        compiler_params=pltpu.CompilerParams(vmem_limit_bytes=VMEM_BYTES),
    )(*operands)


def residue(x):
    quotient = jnp.floor(x.astype(F32) * (1.0 / MODULUS)).astype(jnp.int32)
    rest = x - quotient * MODULUS
    rest = jnp.where(rest < 0, rest + MODULUS, rest)
    return jnp.where(rest >= MODULUS, rest - MODULUS, rest)


def filter_values(seeds, taps):
    index = lax.broadcasted_iota(jnp.int32, (BLOCK, seeds.shape[1]), 0)
    seed = jnp.broadcast_to(seeds, index.shape)
    first = residue(seed * 7919 + index * 104729)
    second = residue(first * first + seed)
    values = (second.astype(F32) / 46337.0 - 0.5) * math.sqrt(12.0 / 108.0)
    return jnp.where(index < taps, values, 0.0).astype(BF16)


def features_kernel(second, seeds_ref, image_ref, *refs):
    out_ref, shifted, bank, pools = refs[-4:]
    filters, (images, pixels) = pools.shape[1], image_ref.shape
    plane, window, half = SIDE * SIDE, 2 * BLOCK, BLOCK // 2
    taps = CHANNELS * KERNEL * KERNEL
    values = filter_values(seeds_ref[...], taps)
    tap = lax.broadcasted_iota(jnp.int32, (BLOCK, CHANNELS * window), 0)
    at = lax.broadcasted_iota(jnp.int32, (BLOCK, CHANNELS * window), 1)
    channel, row, column = at // window, (at % window) // SIDE, at % SIDE
    chosen = (tap == (channel * KERNEL + row) * KERNEL + column) & (row < KERNEL) & (column < KERNEL)
    spread = lax.dot_general(values, jnp.where(chosen, 1.0, 0.0).astype(BF16), ROWS, preferred_element_type=F32)
    for j in range(OUT):
        for t in range(0, CHANNELS * window, BLOCK):
            tile = spread[second * filters : (second + 1) * filters, t : t + BLOCK]
            if j:
                tile = pltpu.roll(tile, 2 * j, 1)
            bank[j * filters : (j + 1) * filters, t : t + BLOCK] = tile.astype(BF16)
    shifted[:, : pixels - BLOCK] = image_ref[:, half : pixels - half]
    shifted[:, pixels - BLOCK :] = jnp.concatenate(
        [image_ref[:, pixels - half :], jnp.zeros((images, half), BF16)], axis=1
    )
    pools[...] = jnp.zeros_like(pools)

    def windows(ref, m):
        starts = [plane * c + BLOCK * m for c in range(CHANNELS)]
        return jnp.concatenate([ref[:, s : s + window] for s in starts], axis=1)

    for m in range(OUT // 2):
        both = jnp.concatenate([windows(image_ref, m), windows(shifted, m)], axis=0)
        active = jnp.maximum(lax.dot_general(bank[...], both, LANES, preferred_element_type=F32), 0.0)
        for q in range(2):
            total = active[POOL * q * filters : (POOL * q + 1) * filters]
            for j in range(POOL * q + 1, POOL * (q + 1)):
                total = total + active[j * filters : (j + 1) * filters]
            pools[2 * (2 * m // POOL) + q] += total[:, :images]
            pools[2 * ((2 * m + 1) // POOL) + q] += total[:, images:]
    for w in range(4):
        out_ref[pl.ds(w, filters, stride=4), :] = pools[w] * (1.0 / (POOL * POOL))
    if second:
        out_ref[4 * filters :, :] = jnp.broadcast_to(refs[0][...].astype(F32), (8, images))


def panel_block(images, labels, seeds):
    count, pixels = images.shape
    filters = seeds.shape[0] // 2
    width = CHANNELS * 2 * BLOCK
    scratch = [((count, pixels), BF16), ((OUT * filters, width), BF16), ((4, filters, count), F32)]
    flops = 2 * OUT * OUT * filters * width * count
    halves, seeds = [], seeds[None]
    for n in range(2):
        kernel = functools.partial(features_kernel, n)
        operands = [seeds, images] + [labels[None]] * n
        halves += call(kernel, operands, [(4 * filters + 8 * n, count)], scratch, flops=flops)
        if not n:
            halves[0], seeds = lax.optimization_barrier((halves[0], seeds))
    return halves


def pieces(x):
    top = x.astype(BF16)
    rest = x - top.astype(F32)
    middle = rest.astype(BF16)
    return top, middle, (rest - middle.astype(F32)).astype(BF16)


def long_dot(one, two, dims):
    (left,), (right,) = dims
    a, b, c = one
    d, e, f = two
    return lax.dot_general(
        jnp.concatenate([a, a, b, a, b, c], axis=left),
        jnp.concatenate([d, e, d, f, e, d], axis=right),
        (dims, ((), ())),
        preferred_element_type=F32,
    )


def lane_copies(tile, lane):
    return jnp.broadcast_to(tile[:, lane : lane + 1], (8, BLOCK))


def row_copies(tile, row):
    return jnp.broadcast_to(tile[row : row + 1, :], (8, BLOCK))


def factor_block(tiles):
    lane = lax.broadcasted_iota(jnp.int32, (8, BLOCK), 1)
    row = lax.broadcasted_iota(jnp.int32, (8, BLOCK), 0)
    count = len(tiles)
    left = list(tiles)
    right = [jnp.where(lane == row + 8 * g, 1.0, 0.0) for g in range(count)]
    upper, inverse, raw = [], [], []
    own = [lane_copies(left[0], j) for j in range(8)]
    for p in range(count):
        top, bottom, scale = left[p], right[p], None
        stop = min(count, (p // STRIDE + 1) * STRIDE)
        cols = {g: [lane_copies(left[g], 8 * p + j) for j in range(8)] for g in range(p + 1, stop)}
        coming = [lane_copies(left[p + 1], 8 * p + 8 + j) for j in range(8)] if p + 1 < stop else []
        for j in range(8):
            pivot = row_copies(own[j], j)
            r = 1.0 / pivot
            for i in range(j + 1, 8):
                across = row_copies(own[i], j)
                t = across * r
                own[i] = own[i] - (own[j] * across) * r
                for g in cols:
                    cols[g][i] = cols[g][i] - cols[g][j] * t
            below = jnp.where(row > j, own[j], 0.0)
            top_row = row_copies(top, j) * r
            bottom_row = row_copies(bottom, j) * r
            top = top - below * top_row
            bottom = bottom - below * bottom_row
            for g in cols:
                left[g] = left[g] - cols[g][j] * top_row
                right[g] = right[g] - cols[g][j] * bottom_row
            if coming:
                edge = cols[p + 1][j]
                scaled = edge * r
                for c in range(8):
                    coming[c] = coming[c] - edge * row_copies(scaled, c)
            root = lax.rsqrt(pivot)
            scale = root if j == 0 else jnp.where(row == j, root, scale)
        raw.append(top * scale)
        upper.append(jnp.where(lane >= row + 8 * p, raw[p], 0.0))
        inverse.append(bottom * scale)
        if p + 1 == stop < count:
            done = slice(stop - STRIDE, stop)
            one = jnp.concatenate(raw[done], axis=0)
            both = jnp.concatenate([one, jnp.concatenate(inverse[done], axis=0)], axis=1)
            change = long_dot(pieces(one), pieces(both), ((0,), (0,)))
            for g in range(stop, count):
                left[g] = left[g] - change[8 * g : 8 * g + 8, :BLOCK]
                right[g] = right[g] - change[8 * g : 8 * g + 8, BLOCK:]
            coming = [lane_copies(left[stop], 8 * stop + j) for j in range(8)]
        own = coming
    return upper, inverse


def slots(feat):
    blocks = feat // BLOCK
    pairs = [(i, j) for i in range(blocks) for j in range(i, blocks)]
    return {pair: slice(n * BLOCK, (n + 1) * BLOCK) for n, pair in enumerate(pairs)}


def product(ones, twos):
    one, two = jnp.concatenate(ones, axis=1), jnp.concatenate(twos, axis=1)
    return lax.dot_general(one, two, LANES, preferred_element_type=F32)


def in_pairs(refs):
    return list(zip(refs[::2], refs[1::2]))


def split(block_refs, high, low):
    half, width = high.shape[0] // 2, block_refs[0][0].shape[1]
    for n, refs in enumerate(block_refs):
        at = slice(n * width, (n + 1) * width)
        for h, ref in enumerate(refs):
            rows = slice(h * half, (h + 1) * half)
            whole = ref[:half, :]
            top = whole.astype(BF16)
            high[rows, at] = top
            low[rows, at] = (whole - top.astype(F32)).astype(BF16)


def gram_row(i, high, low):
    feat = high.shape[0]
    at, rest = slice(i * BLOCK, (i + 1) * BLOCK), slice(i * BLOCK, feat)
    one, two = high[at, :], low[at, :]
    return product([one, one, two, two], [high[rest, :], low[rest, :], high[rest, :], low[rest, :]])


def add_gram(so_far, gram_ref, high, low):
    feat = high.shape[0]
    place = slots(feat)
    for i in range(feat // BLOCK):
        total = gram_row(i, high, low)
        for j in range(i, feat // BLOCK):
            tile = total[:, (j - i) * BLOCK : (j - i + 1) * BLOCK]
            gram_ref[place[i, j], :] = tile if so_far is None else so_far[place[i, j], :] + tile


def add_label_sums(starts_ref, block_refs, so_far, sums_refs, high, low, marks):
    half, width = high.shape[0] // 2, block_refs[0][0].shape[1]
    class_row = lax.broadcasted_iota(jnp.int32, (marks.shape[0], width), 0)
    for d, sums_ref in enumerate(sums_refs):
        for n, (_, ref) in enumerate(block_refs):
            label = ref[half : half + 1, :].astype(jnp.int32) - starts_ref[d]
            marks[:, n * width : (n + 1) * width] = jnp.where(class_row == label, 1.0, 0.0).astype(BF16)
        total = product([marks[...], marks[...]], [high[...], low[...]])
        sums_ref[...] = total if so_far is None else so_far[d][...] + total


def sums_kernel(blocks, carried, starts_ref, *refs):
    so_far, block_refs, refs = refs[:carried], in_pairs(refs[carried : carried + 2 * blocks]), refs[carried + 2 * blocks :]
    gram_ref, sums_refs, (high, low, marks) = refs[0], refs[1:-3], refs[-3:]
    split(block_refs, high, low)
    add_gram(so_far[0] if carried else None, gram_ref, high, low)
    add_label_sums(starts_ref, block_refs, so_far[1:] or None, sums_refs, high, low, marks)


def panel_scratch(blocks, feat, classes):
    width = sum(block[0].shape[1] for block in blocks)
    return [((feat, width), BF16), ((feat, width), BF16), ((classes, width), BF16)]


def panel_sums(so_far, blocks, starts, feat, classes, parts):
    width = sum(block[0].shape[1] for block in blocks)
    packed = (len(slots(feat)) * BLOCK, BLOCK)
    carried = list(so_far or [])
    kernel = lambda *refs: sums_kernel(len(blocks), len(carried), *refs)
    aliases = {1 + d: d for d in range(len(carried))}
    flops = 8 * width * math.prod(packed) + 4 * parts * width * classes * feat
    outs = [packed] + [(classes, feat)] * parts
    operands = [starts] + carried + [half for block in blocks for half in block]
    return call(kernel, operands, outs, panel_scratch(blocks, feat, classes), 1, flops, aliases)


def solve_kernel(ridge, given, late, starts_ref, *refs):
    gram_refs, sums_refs, refs = refs[:given], refs[given : 2 * given], refs[2 * given :]
    block_refs, (factor_ref, turned_ref, gram, sums, inverse) = in_pairs(refs[: 2 * late]), refs[2 * late :][:5]
    feat = gram.shape[0]
    place = slots(feat)
    if late:
        high, low, marks = refs[-3:]
        split(block_refs, high, low)

    def gather_row(i):
        row = gram_row(i, high, low) if late else None
        for j in range(i, feat // BLOCK):
            tile = sum(ref[place[i, j], :] for ref in gram_refs)
            if late:
                tile = tile + row[:, (j - i) * BLOCK : (j - i + 1) * BLOCK]
            gram[i * BLOCK : (i + 1) * BLOCK, j * BLOCK : (j + 1) * BLOCK] = tile

    def gather_sums():
        total = sum(ref[...] for ref in sums_refs)
        if late:
            add_label_sums(starts_ref, block_refs, [total], [sums], high, low, marks)
        else:
            sums[...] = total

    gather_row(0)
    factor_ref[...] = jnp.zeros_like(factor_ref)
    lane = lax.broadcasted_iota(jnp.int32, (8, BLOCK), 1)
    row = lax.broadcasted_iota(jnp.int32, (8, BLOCK), 0)

    def turn(at):
        turned = lax.dot_general(sums[:, at], inverse[...], LANES, precision=HIGHEST, preferred_element_type=F32)
        turned_ref[:, at] = turned[: turned_ref.shape[0], :]
        return turned

    for start in range(0, feat, BLOCK):
        at, rest = slice(start, start + BLOCK), start + BLOCK
        if start:
            before = slice(start - BLOCK, start)
            taken = jnp.dot(turn(before), factor_ref[before, start:], precision=HIGHEST, preferred_element_type=F32)
            sums[:, start:] -= taken
        tiles = []
        for g in range(BLOCK // 8):
            tile = gram[start + 8 * g : start + 8 * g + 8, at]
            tiles.append(tile + jnp.where(lane == row + 8 * g, ridge, 0.0))
        upper, inverted = factor_block(tiles)
        for g in range(BLOCK // 8):
            factor_ref[start + 8 * g : start + 8 * g + 8, at] = upper[g]
            inverse[8 * g : 8 * g + 8, :] = inverted[g]
        if not start:
            for n in range(1, feat // BLOCK):
                gather_row(n)
            gather_sums()
        parts, turner = [], pieces(inverse[...])
        for i in range(rest, feat, BLOCK):
            here = slice(i, i + BLOCK)
            across = long_dot(turner, pieces(gram[at, here]), ((1,), (0,)))
            factor_ref[at, here] = across
            parts.append(pieces(across))
            for n, part in enumerate(parts):
                there = slice(rest + n * BLOCK, rest + (n + 1) * BLOCK)
                gram[there, here] -= long_dot(part, parts[-1], ((0,), (0,)))
    turn(slice(feat - BLOCK, feat))


def factor_and_solve(grams, sums, late, starts, ridge, feat, classes):
    padded = sums[0].shape[0]
    kernel = lambda *refs: solve_kernel(ridge, len(grams), len(late), *refs)
    scratch = [((feat, feat), F32), ((padded, feat), F32), ((BLOCK, BLOCK), F32)]
    if late:
        scratch += panel_scratch(late, feat, padded)
    outs = [(feat, feat), (classes, feat)]
    factor, turned = call(kernel, [starts] + grams + sums + [half for block in late for half in block], outs, scratch, 1, 6 * classes * feat**2)
    return factor, turned.T


def turns(size, step):
    return [(i, (i + step) % size) for i in range(size)]


def passed_on(blocks, axis):
    size = lax.axis_size(axis)
    return [lax.ppermute(block, axis, turns(size, d)) for block in blocks for d in range(1, size)]


def crossed(blocks):
    return list(zip(*[passed_on(halves, "cls") for halves in zip(*blocks)]))


def sums_passed_on(gram, sums):
    size = lax.axis_size("cls")
    return passed_on([gram], "cls"), [lax.ppermute(sums[d], "cls", turns(size, d)) for d in range(1, size)]


def gathered_sums(block, sums_of):
    size = lax.axis_size("img")
    far, next_ring, sums = [None, None], [None, None], None
    top, bottom = block
    for h in range(2):
        half = bottom if h else top
        next_ring[h] = lax.ppermute(half, "img", turns(size, 1))
        far[h] = passed_on([half], "sub")
        if not h:
            next_ring[h], far[h], bottom = lax.optimization_barrier((next_ring[h], far[h], bottom))
    came = [(top, bottom)]
    for step in range(1, size):
        last, swapped, passed = step == size - 1, [None, None], [None, None]
        for h in range(2):
            if step > 1 or h:
                tied = (next_ring[h], far[h], sums if h else None)
                next_ring[h], far[h], kept = lax.optimization_barrier(tied)
            if step == 1 and h:
                first = far[h]
            sums = kept if h else sums
            if not last:
                passed[h] = lax.ppermute(next_ring[h], "img", turns(size, 1))
            if last and h:
                swapped[h] = [lax.ppermute(half, "img", turns(size, -1)) for half in first]
            else:
                swapped[h] = passed_on([next_ring[h]], "sub")
        came += [tuple(next_ring)] + list(zip(*far))
        if step == 1 or last:
            sums, came = sums_of(sums, came), []
        next_ring, far = passed, swapped
    far, sums = lax.optimization_barrier((far, sums))
    late = list(zip(*far))
    gram, *sums = sums
    grams, others = sums_passed_on(gram, sums)
    return [gram] + grams, [sums[0]] + others, late + crossed(late)


def shards(images, labels, seeds):
    count = images.shape[0]
    feat = 4 * seeds.shape[0]
    parts = lax.axis_size("cls")
    members = math.prod(lax.axis_size(axis) for axis in ("img", "sub", "cls"))
    ridge = RIDGE * count * members
    classes = CLASSES // parts
    padded = -(-classes // BLOCK) * BLOCK
    starts = classes * ((lax.axis_index("cls") + jnp.arange(parts, dtype=jnp.int32)) % parts)
    block = panel_block(images, labels, seeds)

    def sums_of(so_far, blocks):
        return panel_sums(so_far, blocks, starts, feat, padded, parts)

    if members <= MOST_BLOCKS:
        grams, sums, late = gathered_sums(block, sums_of)
    else:
        gram, *sums = lax.psum(tuple(sums_of(None, [block])), ("img", "sub"))
        grams, others = sums_passed_on(gram, sums)
        grams, sums, late = [gram] + grams, [sums[0]] + others, []
    return factor_and_solve(grams, sums, late, starts, ridge, feat, classes)


def solution(mesh):
    placed = (P(("grp", "img", "sub", "cls"), None), P(("grp", "img", "sub", "cls")), P())
    return jax.shard_map(
        shards,
        mesh=mesh,
        in_specs=placed,
        out_specs=(P("grp", None), P("grp", "cls")),
        check_vma=False,
    )
```
